32 devices in a mesh: section: 4 (over y, x), batch: 8 (over z, core).
Axes of the slice: x: 2, y: 2, z: 4, core: 2. Of those that a mesh axis runs over, the one named last changes fastest.
Arguments:
- tokens: bfloat16 [4096, 768], P('batch'), may hold values from -6 to 6
- key_tokens: bfloat16 [4096, 768], P('batch'), may hold values from -6 to 6
- cotangent: bfloat16 [4096, 768], P('batch'), may hold values from -6 to 6
- lengths: int32 [16, 4], P('batch'), may hold values from 0 to 256, as said below
- query_mats: float32 [2, 768, 9216], P(None, 'batch')
- query_small: float32 [2, 8448], replicated
- key_mats: float32 [2, 768, 9216], P(None, 'batch')
- key_small: float32 [2, 8448], replicated
Outputs:
- activations: bfloat16 [4096, 768], P('batch', 'section')
- pooled_query: float32 [16, 4, 768], P('batch', None, 'section')
- pooled_key: float32 [16, 4, 768], P('batch', None, 'section')
- input_grad: bfloat16 [4096, 768], P('batch', 'section')
- grad_mats: float32 [2, 768, 9216], P(None, 'batch')
- grad_small: float32 [2, 8448], P(None, 'batch')
- key_mats_step: float32 [2, 768, 9216], P(None, 'batch')
- key_small_step: float32 [2, 8448], replicated
The draws below stay inside these ranges and needn't reach their ends.
Inputs may be any that keep to these rules, and one draw needn't show every extreme that they name: `lengths`: each row lists its crops' token counts in order, each from 64 to 256, then zeros; a row's counts sum to 256 or less, and the tokens after them are padding.
All inputs are finite; a program needn't handle non-finite values.
Results may differ from the reference program's by a relative error of at most 0.018.
Values may be sent and summed in bfloat16 or wider, within the bound.
No kernel may reach another device: no remote copies, remote signals or barrier semaphores. Data moves between devices by JAX's collectives and lax.ppermute only.
A program may use at most 576 MiB of HBM per device.

```python
import jax
import jax.numpy as jnp
from jax import lax

HEADS = 12
HEAD_DIM = 64
D = 768
LAYERS = 2
ROW = 256
CROP_MIN = 64
CROP_MAX = 256
CROPS = 4
ROWS_TOTAL = 16
TOKENS = 4096


def column_scale(boost):
    column = jnp.arange(12 * D)
    factor = jnp.where(column < 3 * D, 1.0, jnp.where(column < 4 * D, boost, jnp.where(column < 8 * D, 1.0, 0.5)))
    return factor * D ** (-0.5)


def small_values(base):
    column = jnp.arange(11 * D)
    gains = (column >= 2 * D) & (column < 3 * D) | (column >= 9 * D) & (column < 10 * D)
    return jnp.where(gains, 1.0 + 0.15 * base, 0.3 * base)


def draw_query_mats(key, part):
    key = jax.random.fold_in(key, 11)
    base = jax.random.normal(key, (LAYERS, D, 12 * D), jnp.float32)
    return base * column_scale(6.0)


def draw_key_mats(key, part):
    key = jax.random.fold_in(key, 12)
    base = jax.random.normal(key, (LAYERS, D, 12 * D), jnp.float32)
    return base * column_scale(6.0)


def draw_query_small(key, part):
    key = jax.random.fold_in(key, 13)
    base = jax.random.normal(key, (LAYERS, 11 * D), jnp.float32)
    return small_values(base)


def draw_key_small(key, part):
    key = jax.random.fold_in(key, 14)
    base = jax.random.normal(key, (LAYERS, 11 * D), jnp.float32)
    return small_values(base)


def draw_lengths(key, part):
    key = jax.random.fold_in(key, 5)
    first_key, second_key = jax.random.split(key)
    sizes = jax.random.randint(first_key, (ROWS_TOTAL, CROPS), CROP_MIN, CROP_MAX + 1)
    widest = jax.random.randint(second_key, (), 0, ROWS_TOTAL)
    row_index = jnp.arange(ROWS_TOTAL)[:, None]
    slot_index = jnp.arange(CROPS)[None, :]
    sizes = jnp.where((row_index == widest) & (slot_index == 0), CROP_MAX, sizes)
    boundary = jnp.cumsum(sizes, axis=1)
    return jnp.where(boundary <= ROW, sizes, 0).astype(jnp.int32)


def block_scale(own_key, extent, shards, low, top_value):
    loudness = 1.0
    for dim, shards_of in shards:
        steps = jax.random.uniform(jax.random.fold_in(jax.random.fold_in(own_key, 6), dim), (shards_of,), jnp.float32, low / len(shards), top_value / len(shards))
        loudness = loudness * jnp.repeat(jnp.exp(steps), extent[dim] // shards_of).reshape((-1,) + (1,) * (len(extent) - 1 - dim))
    return loudness


def normal_values(stream_key, shape, scale, most, pieces=(), kind=jnp.bfloat16):
    result = jax.random.normal(stream_key, shape, jnp.float32) * scale
    if len(pieces) > 0:
        result = block_scale(stream_key, shape, pieces, -0.22, 0.18) * result
    return jnp.clip(result, min=-most, max=most).astype(kind)


def setup_inputs(seed: int = 0) -> dict:
    key_list = jax.random.split(jax.random.key(seed), 9)
    return {
        "tokens": normal_values(key_list[0], (TOKENS, D), 1.0, 6.0, ((0, 8),)),
        "key_tokens": normal_values(key_list[1], (TOKENS, D), 1.0, 6.0, ((0, 8),)),
        "cotangent": normal_values(key_list[2], (TOKENS, D), 1.0, 6.0, ((0, 8),)),
        "lengths": draw_lengths(jax.random.fold_in(key_list[8], 71), 0),
        "query_mats": draw_query_mats(jax.random.fold_in(key_list[8], 71), 0),
        "query_small": draw_query_small(jax.random.fold_in(key_list[8], 71), 0),
        "key_mats": draw_key_mats(jax.random.fold_in(key_list[8], 71), 0),
        "key_small": draw_key_small(jax.random.fold_in(key_list[8], 71), 0),
    }


@jax.custom_vjp
def low(v):
    return lax.optimization_barrier(v.astype(jnp.bfloat16)).astype(jnp.float32)

@jax.custom_vjp
def low_back(v):
    return v

def low_keep(v):
    return (low(v), None)

def low_pass(kept, grad):
    return (grad,)

def back_keep(v):
    return (v, None)

def back_low(kept, grad):
    return (low(grad),)
low.defvjp(low_keep, low_pass)
low_back.defvjp(back_keep, back_low)
precise = lax.Precision.HIGHEST
epsilon = 1e-05
keep_rate = 0.9995

def layout(lens_row):
    boundary = jnp.cumsum(lens_row).astype(jnp.int32)
    position = jnp.arange(ROW, dtype=jnp.int32)
    segment = lax.optimization_barrier(jnp.sum((position[:, None] >= boundary[None, :]).astype(jnp.int32), axis=1))
    filled = position < boundary[-1]
    allowed = (segment[:, None] == segment[None, :]) & filled[None, :] | (position[:, None] == position[None, :])
    member = ((segment[:, None] == jnp.arange(CROPS, dtype=jnp.int32)[None, :]) & filled[:, None]).astype(jnp.float32)
    return (allowed, member)

def normalize(summed, norm_gain, norm_shift):
    centre = summed - lax.optimization_barrier(jnp.mean(summed, axis=-1, keepdims=True))
    spread = lax.optimization_barrier(jnp.mean(centre * centre, axis=-1, keepdims=True))
    return centre * lax.rsqrt(spread + epsilon) * norm_gain + norm_shift

def attend_row(packed):
    query, key_rows, values, lens_row = packed
    allowed, member = layout(lens_row)
    shaped = (ROW, HEADS, HEAD_DIM)
    scores = jnp.einsum('qhd,khd->hqk', query.reshape(shaped), key_rows.reshape(shaped), precision=precise) * HEAD_DIM ** (-0.5)
    scores = low_back(scores)
    scores = jnp.where(allowed[None], scores, -1e+30)
    attn_prob = low(jax.nn.softmax(scores, axis=-1))
    mixed = jnp.einsum('hqk,khd->qhd', attn_prob, values.reshape(shaped), precision=precise)
    return mixed.reshape(ROW, D)

def attention_layer(inputs, weights, small, lengths):
    flat_rows = inputs.reshape(-1, D)
    project = jnp.dot(flat_rows, weights[:, :3 * D], precision=precise)
    query = low(low_back(project[:, :D]))
    key_rows = low(low_back(project[:, D:2 * D]))
    values = low(low_back(project[:, 2 * D:3 * D] + small[:D]))
    blocked = (-1, ROW, D)
    mixed = lax.map(jax.checkpoint(attend_row), (query.reshape(blocked), key_rows.reshape(blocked), values.reshape(blocked), lengths))
    mixed = low(low_back(mixed.reshape(-1, D)))
    branch = low_back(jnp.dot(mixed, weights[:, 3 * D:4 * D].T, precision=precise) + small[D:2 * D])
    output = normalize(flat_rows + branch, small[2 * D:3 * D], small[3 * D:4 * D])
    return low(low_back(output)).reshape(inputs.shape)

def feed_forward(inputs, weights, small):
    flat_rows = inputs.reshape(-1, D)
    hidden = low_back(jnp.dot(flat_rows, weights[:, 4 * D:8 * D], precision=precise) + small[4 * D:8 * D])
    active = low(jax.nn.gelu(hidden, approximate=False))
    branch = low_back(jnp.dot(active, weights[:, 8 * D:].T, precision=precise) + small[8 * D:9 * D])
    output = normalize(flat_rows + branch, small[9 * D:10 * D], small[10 * D:])
    return low(low_back(output)).reshape(inputs.shape)

def forward(inputs, mats, small, lengths):
    weights = low(mats)
    hidden_state = inputs
    for layer_idx in range(LAYERS):
        hidden_state = attention_layer(hidden_state, weights[layer_idx], small[layer_idx], lengths)
        hidden_state = feed_forward(hidden_state, weights[layer_idx], small[layer_idx])
    return hidden_state

def pool(final, lengths):
    member = jax.vmap(lambda row_lens: layout(row_lens)[1])(lengths)
    crop_sums = jnp.einsum('rpc,rpd->rcd', member, final, precision=precise)
    return crop_sums / jnp.maximum(lengths.astype(jnp.float32), 1.0)[:, :, None]

def reference(tokens, key_tokens, cotangent, lengths, query_mats, query_small, key_mats, key_small):
    blocked = (ROWS_TOTAL, ROW, D)
    start = tokens.astype(jnp.float32).reshape(blocked)
    key_start = key_tokens.astype(jnp.float32).reshape(blocked)

    def encode(inputs, mats, small):
        final = forward(inputs, mats, small, lengths)
        key_final = forward(key_start, key_mats, key_small, lengths)
        return (final, (pool(final, lengths), pool(key_final, lengths)))
    final, pullback, pooled = jax.vjp(encode, start, query_mats, query_small, has_aux=True)
    grad_in, grad_mats, grad_small = pullback(cotangent.astype(jnp.float32).reshape(blocked))
    pooled_query, pooled_key = pooled
    activations = final.reshape(TOKENS, D).astype(jnp.bfloat16)
    input_grad = grad_in.reshape(TOKENS, D).astype(jnp.bfloat16)
    key_mats_step = (query_mats - key_mats) * (1.0 - keep_rate)
    key_small_step = (query_small - key_small) * (1.0 - keep_rate)
    return (activations, pooled_query, pooled_key, input_grad, grad_mats, grad_small, key_mats_step, key_small_step)
```

```python
from functools import partial

import jax
import jax.numpy as jnp
from jax import lax
from jax.experimental import pallas as pl
from jax.experimental.pallas import tpu as pltpu
from jax.sharding import PartitionSpec as P

HEADS = 12
HEAD_DIM = 64
D = 768
LAYERS = 2
MICRO = 2
ROW = 256
CROPS = 4
TOK = MICRO * ROW
SMALL = 11 * D

epsilon = 1e-05
keep_rate = 0.9995
score_scale = HEAD_DIM ** (-0.5)
bf16 = jnp.bfloat16
f32 = jnp.float32

AT_BV, AT_BO, AT_G1, AT_S1, AT_B1, AT_B2, AT_G2, AT_S2 = (
    0,
    D,
    2 * D,
    3 * D,
    4 * D,
    8 * D,
    9 * D,
    10 * D,
)


def swap_x(block):
    return lax.ppermute(block, "section", [(0, 1), (1, 0), (2, 3), (3, 2)])


def swap_y(block):
    return lax.ppermute(block, "section", [(0, 2), (2, 0), (1, 3), (3, 1)])


def swap_core(block):
    count = lax.axis_size("batch")
    return lax.ppermute(block, "batch", [(i, i ^ 1) for i in range(count)])


def shift_z(block, distance):
    count = lax.axis_size("batch")
    return lax.ppermute(block, "batch", [(i, (i + 2 * distance) % count) for i in range(count)])


def add_low(left, right):
    return (left.astype(f32) + right.astype(f32)).astype(bf16)


def sum_parts(part_0, part_1):
    here_0, here_1 = swap_x(part_0), swap_y(part_1)
    half_0, half_1 = add_low(part_0, here_0), add_low(part_1, here_1)
    return (half_0, swap_y(half_0), half_1, swap_x(half_1))


def gather_rows(block):
    places = lax.axis_size("batch") // 2
    me = lax.axis_index("batch")
    z, core = me // 2, me % 2
    found = [block] + [shift_z(block, d) for d in range(1, places)]
    order = (z - jnp.arange(places)) % places
    stacked = jnp.stack(found)
    other = swap_core(stacked)
    both = jnp.where(core == 0, jnp.stack([stacked, other], 1), jnp.stack([other, stacked], 1))
    whole = jnp.take(both, (z - jnp.arange(places)) % places, axis=0)
    return whole.reshape(places * 2 * block.shape[0], block.shape[1])


def scatter_rows(block, rows):
    places = lax.axis_size("batch") // 2
    me = lax.axis_index("batch")
    z, core = me // 2, me % 2
    parted = block.reshape(places, 2, rows, block.shape[1])
    mine = lax.dynamic_index_in_dim(parted, core, 1, keepdims=False)
    other = lax.dynamic_index_in_dim(parted, 1 - core, 1, keepdims=False)
    chip = add_low(mine, swap_core(other))
    total = lax.dynamic_index_in_dim(chip, z, 0, keepdims=False).astype(f32)
    for d in range(1, places):
        leaving = lax.dynamic_index_in_dim(chip, (z + d) % places, 0, keepdims=False)
        total = total + shift_z(leaving, d).astype(f32)
    return total.astype(bf16)


def gather_section(block):
    count = lax.axis_size("section")
    me = lax.axis_index("section")
    found = [block] + [
        lax.ppermute(block, "section", [(i, i ^ k) for i in range(count)]) for k in range(1, count)
    ]
    stacked = jnp.stack(found)
    return jnp.take(stacked, me ^ jnp.arange(count), axis=0)


def dot_nn(left, right):
    return jnp.dot(left, right, preferred_element_type=f32)


def dot_nt(left, right):
    return lax.dot_general(left, right, (((1,), (1,)), ((), ())), preferred_element_type=f32)


def dot_tn(left, right):
    return lax.dot_general(left, right, (((0,), (0,)), ((), ())), preferred_element_type=f32)


def ends_of(lens_ref, row):
    ends, total = [], 0
    for c in range(CROPS):
        total = total + lens_ref[row, c]
        ends.append(total)
    return ends


def segments(ends, shape, dim):
    position = lax.broadcasted_iota(jnp.int32, shape, dim)
    segment = jnp.zeros(shape, jnp.int32)
    for end in ends:
        segment = segment + (position >= end).astype(jnp.int32)
    return position, segment


def allowed_of(lens_ref, row):
    ends = ends_of(lens_ref, row)
    pos_q, seg_q = segments(ends, (ROW, 1), 0)
    pos_k, seg_k = segments(ends, (1, ROW), 1)
    seg_k = jnp.where(pos_k < ends[-1], seg_k, -1)
    return (seg_q == seg_k) | (pos_q == pos_k)


def pooled_of(lens_ref, row, values):
    ends = ends_of(lens_ref, row)
    pos, seg = segments(ends, (1, ROW), 1)
    crop = lax.broadcasted_iota(jnp.int32, (8, 1), 0)
    seg = jnp.where(pos < ends[-1], seg, -1)
    member = (seg == crop).astype(f32).astype(bf16)
    counts = jnp.ones((8, 1), f32)
    for c in range(CROPS):
        counts = jnp.where(crop == c, jnp.maximum(lens_ref[row, c], 1).astype(f32), counts)
    return (dot_nn(member, values) / counts)[:CROPS]


def standard(summed):
    centre = summed - jnp.mean(summed, axis=-1, keepdims=True)
    spread = jnp.mean(centre * centre, axis=-1, keepdims=True)
    rate = lax.rsqrt(spread + epsilon)
    return centre * rate, rate


def small_at(small_ref, layer, offset, width=D):
    return small_ref[layer : layer + 1, offset : offset + width]


def rows_of(row):
    return slice(row * ROW, (row + 1) * ROW)


def norm_in(layer, gain_at, shift_at, bias_at, base_ref, sums, small_ref, row):
    half, other = sums[2 * row], sums[2 * row + 1]
    branch = half[...].astype(f32) + other[...].astype(f32) + small_at(small_ref, layer, bias_at)
    hat, rate = standard(base_ref[rows_of(row), :].astype(f32) + branch)
    out = hat * small_at(small_ref, layer, gain_at) + small_at(small_ref, layer, shift_at)
    return out.astype(bf16), hat, rate


def attention_kernel(layer, first, keep, *refs):
    refs = list(refs)
    if first:
        base_ref = refs.pop(0)
    else:
        base_ref, sums, small_ref = refs[0], refs[1:5], refs[5]
        refs = refs[6:]
    weights_ref, bv_ref, lens_ref = refs[:3]
    outs = refs[3:]
    part_refs, outs = outs[:2], outs[2:]
    if not first:
        y_ref, outs = outs[0], outs[1:]
        if keep:
            hat_ref, rate_ref = outs[:2]
            outs = outs[2:]
    if keep:
        q_ref, k_ref, v_ref, mixed_ref, prob_ref = outs
    part = HEADS // 4 * HEAD_DIM
    lane = lax.broadcasted_iota(jnp.int32, (1, part), 1)
    for row in range(MICRO):
        here = rows_of(row)
        if first:
            inputs = base_ref[here, :]
        else:
            inputs, hat, rate = norm_in(
                layer - 1, AT_G2, AT_S2, AT_B2, base_ref, sums, small_ref, row
            )
            y_ref[here, :] = inputs
            if keep:
                hat_ref[here, :] = hat
                rate_ref[here, :] = jnp.broadcast_to(rate, (ROW, 128))
        project = dot_nn(inputs, weights_ref[:, : 3 * part])
        query = project[:, :part]
        key_rows = project[:, part : 2 * part].astype(bf16)
        values = (project[:, 2 * part :] + bv_ref[layer : layer + 1, :]).astype(bf16)
        allowed = allowed_of(lens_ref, row)
        mixed = jnp.zeros((ROW, part), f32)
        for head in range(part // HEAD_DIM):
            inside = (lane >= head * HEAD_DIM) & (lane < (head + 1) * HEAD_DIM)
            head_q = jnp.where(inside, query, 0.0).astype(bf16)
            scores = jnp.where(allowed, dot_nt(head_q, key_rows) * score_scale, -1e30)
            terms = jnp.exp(scores - jnp.max(scores, axis=-1, keepdims=True))
            prob = terms / jnp.sum(terms, axis=-1, keepdims=True)
            if keep:
                prob_ref[row, head] = prob
            mixed = jnp.where(inside, dot_nn(prob.astype(bf16), values), mixed)
        mixed = mixed.astype(bf16)
        part_refs[row][...] = dot_nt(mixed, weights_ref[:, 3 * part :]).astype(bf16)
        if keep:
            q_ref[here, :] = query.astype(bf16)
            k_ref[here, :] = key_rows
            v_ref[here, :] = values
            mixed_ref[here, :] = mixed


def feed_kernel(layer, keep, *refs):
    base_ref, sums, small_ref = refs[0], refs[1:5], refs[5]
    weights_ref, b1_ref = refs[6:8]
    part_refs, y_ref = refs[8:10], refs[10]
    if keep:
        hat_ref, rate_ref, hidden_ref, active_ref = refs[11:]
    for row in range(MICRO):
        here = rows_of(row)
        inputs, hat, rate = norm_in(layer, AT_G1, AT_S1, AT_BO, base_ref, sums, small_ref, row)
        y_ref[here, :] = inputs
        hidden = dot_nn(inputs, weights_ref[:, :D]) + b1_ref[layer : layer + 1, :]
        active = (0.5 * hidden * (1.0 + lax.erf(hidden * (0.5**0.5)))).astype(bf16)
        part_refs[row][...] = dot_nt(active, weights_ref[:, D:]).astype(bf16)
        if keep:
            hat_ref[here, :] = hat
            rate_ref[here, :] = jnp.broadcast_to(rate, (ROW, 128))
            hidden_ref[here, :] = hidden
            active_ref[here, :] = active


def last_kernel(layer, base_ref, *refs):
    sums, small_ref, lens_ref, pooled_ref = refs[:4], refs[4], refs[5], refs[6]
    for row in range(MICRO):
        out, hat, rate = norm_in(layer, AT_G2, AT_S2, AT_B2, base_ref, sums, small_ref, row)
        pooled_ref[row] = pooled_of(lens_ref, row, out)


def norm_back(grad_out, hat, rate, gain):
    inner = grad_out * gain
    grad = rate * (
        inner
        - jnp.mean(inner, axis=-1, keepdims=True)
        - hat * jnp.mean(inner * hat, axis=-1, keepdims=True)
    )
    return grad


def row_sum(block):
    return jnp.sum(block, axis=0, keepdims=True)


def feed_back_kernel(layer, last, *refs):
    refs = list(refs)
    if last:
        base_ref, sums, cot_ref, lens_ref = refs[0], refs[1:5], refs[5], refs[6]
        refs = refs[7:]
    else:
        base_ref, sums, hat_ref, rate_ref = refs[0], refs[1:5], refs[5], refs[6]
        refs = refs[7:]
    small_ref, weights_ref, hidden_ref = refs[:3]
    part_refs = refs[3:5]
    carry_ref, branch_ref, grad_hidden_ref, sums_ref, bias_ref = refs[5:10]
    if last:
        y_ref, pooled_ref = refs[10:]
    gain = small_at(small_ref, layer, AT_G2)
    totals = [jnp.zeros((1, D), f32) for _ in range(4)]
    for row in range(MICRO):
        here = rows_of(row)
        if last:
            out, hat, rate = norm_in(layer, AT_G2, AT_S2, AT_B2, base_ref, sums, small_ref, row)
            y_ref[here, :] = out
            pooled_ref[row] = pooled_of(lens_ref, row, out)
            grad_out = cot_ref[here, :].astype(f32)
        else:
            hat, rate = hat_ref[here, :], rate_ref[here, :1]
            grad_out = base_ref[here, :] + (
                sums[2 * row][...].astype(f32) + sums[2 * row + 1][...].astype(f32)
            )
            grad_out = grad_out.astype(bf16).astype(f32)
        grad = norm_back(grad_out, hat, rate, gain)
        carry_ref[here, :] = grad
        branch = grad.astype(bf16)
        branch_ref[here, :] = branch
        grad_active = dot_nn(branch, weights_ref[:, D:])
        hidden = hidden_ref[here, :]
        slope = 0.5 * (1.0 + lax.erf(hidden * (0.5**0.5))) + hidden * (
            jnp.exp(-0.5 * hidden * hidden) * 0.3989422804014327
        )
        grad_hidden = (grad_active * slope).astype(bf16)
        grad_hidden_ref[here, :] = grad_hidden
        part_refs[row][...] = dot_nt(grad_hidden, weights_ref[:, :D]).astype(bf16)
        totals[0] += row_sum(branch.astype(f32))
        totals[1] += row_sum(grad_out * hat)
        totals[2] += row_sum(grad_out)
        totals[3] += row_sum(grad_hidden.astype(f32))
    for i in range(3):
        sums_ref[i : i + 1, :] = totals[i]
    bias_ref[...] = totals[3]


def attention_back_kernel(layer, *refs):
    base_ref, sums, hat_ref, rate_ref = refs[0], refs[1:5], refs[5], refs[6]
    small_ref, weights_ref, q_ref, k_ref, v_ref, prob_ref = refs[7:13]
    part_refs = refs[13:15]
    carry_ref, branch_ref, grad_proj_ref, sums_ref, bias_ref = refs[15:]
    part = HEADS // 4 * HEAD_DIM
    lane = lax.broadcasted_iota(jnp.int32, (1, part), 1)
    gain = small_at(small_ref, layer, AT_G1)
    totals = [jnp.zeros((1, D), f32) for _ in range(3)] + [jnp.zeros((1, part), f32)]
    for row in range(MICRO):
        here = rows_of(row)
        hat, rate = hat_ref[here, :], rate_ref[here, :1]
        grad_out = base_ref[here, :] + (
            sums[2 * row][...].astype(f32) + sums[2 * row + 1][...].astype(f32)
        )
        grad_out = grad_out.astype(bf16).astype(f32)
        grad = norm_back(grad_out, hat, rate, gain)
        carry_ref[here, :] = grad
        branch = grad.astype(bf16)
        branch_ref[here, :] = branch
        grad_mixed = dot_nn(branch, weights_ref[:, 3 * part :])
        low_mixed = grad_mixed.astype(bf16)
        query, key_rows, values = q_ref[here, :], k_ref[here, :], v_ref[here, :]
        grads = [jnp.zeros((ROW, part), f32) for _ in range(3)]
        for head in range(part // HEAD_DIM):
            inside = (lane >= head * HEAD_DIM) & (lane < (head + 1) * HEAD_DIM)
            prob = prob_ref[row, head]
            head_mixed = jnp.where(inside, grad_mixed, 0.0).astype(bf16)
            grad_prob = dot_nt(head_mixed, values)
            grad_scores = prob * (
                grad_prob - jnp.sum(grad_prob * prob, axis=-1, keepdims=True)
            )
            grad_scores = grad_scores.astype(bf16)
            grad_q = dot_nn(grad_scores, key_rows) * score_scale
            grad_k = dot_tn(grad_scores, query) * score_scale
            grad_v = dot_tn(prob.astype(bf16), low_mixed)
            grads = [
                jnp.where(inside, new, old) for new, old in zip((grad_q, grad_k, grad_v), grads)
            ]
        grad_proj = jnp.concatenate(grads, axis=1).astype(bf16)
        grad_proj_ref[here, :] = grad_proj
        part_refs[row][...] = dot_nt(grad_proj, weights_ref[:, : 3 * part]).astype(bf16)
        totals[0] += row_sum(branch.astype(f32))
        totals[1] += row_sum(grad_out * hat)
        totals[2] += row_sum(grad_out)
        totals[3] += row_sum(grads[2].astype(bf16).astype(f32))
    for i in range(3):
        sums_ref[i : i + 1, :] = totals[i]
    bias_ref[...] = totals[3]


VMEM = pl.BlockSpec(memory_space=pltpu.VMEM)
SMEM = pl.BlockSpec(memory_space=pltpu.SMEM)


def shaped(shape, kind):
    return jax.ShapeDtypeStruct(shape, kind)


def call(body, name, flops, operands, outs):
    specs = [SMEM if a.dtype == jnp.int32 else VMEM for a in operands]
    moved = sum(a.size * a.dtype.itemsize for a in (*operands, *outs))
    return pl.pallas_call(
        body,
        name=name,
        in_specs=specs,
        out_specs=[VMEM] * len(outs),
        out_shape=list(outs),
        cost_estimate=pl.CostEstimate(flops=flops, bytes_accessed=moved, transcendentals=0),
        compiler_params=pltpu.CompilerParams(vmem_limit_bytes=40 * 2**20),
    )(*operands)


part_out = [shaped((ROW, D), bf16)] * 2
rows_out = shaped((TOK, D), bf16)
wide_out = shaped((TOK, D), f32)
rate_out = shaped((TOK, 128), f32)


def heads_part():
    return D // lax.axis_size("section")


def attention(layer, inputs, sums, small, weights, bv, lengths, keep, tag):
    first, part = sums is None, heads_part()
    operands = [inputs] if first else [inputs, *sums, small]
    operands += [weights, bv, lengths]
    outs = list(part_out)
    if not first:
        outs += [rows_out] + ([wide_out, rate_out] if keep else [])
    if keep:
        outs += [shaped((TOK, part), bf16)] * 4
        outs += [shaped((MICRO, part // HEAD_DIM, ROW, ROW), f32)]
    return call(
        partial(attention_kernel, layer, first, keep),
        f"attention_{tag}{layer}",
        2 * TOK * part * (4 * D + 4 * ROW),
        operands,
        outs,
    )


def feed(layer, inputs, sums, small, weights, b1, keep, tag):
    outs = list(part_out) + [rows_out]
    if keep:
        outs += [wide_out, rate_out, wide_out, rows_out]
    return call(
        partial(feed_kernel, layer, keep),
        f"feed_{tag}{layer}",
        4 * TOK * D * D,
        [inputs, *sums, small, weights, b1],
        outs,
    )


def on_device(tokens, key_tokens, cotangent, lengths, query_mats, query_small, key_mats, key_small):
    sections = lax.axis_size("section")
    section = lax.axis_index("section")
    batches = lax.axis_size("batch")
    part = heads_part()
    rows = query_mats.shape[1]

    def own_cols(mats, layer):
        attn = jnp.concatenate(
            [
                lax.dynamic_slice(mats, (layer, 0, j * D + section * part), (1, rows, part))[0]
                for j in range(4)
            ],
            axis=1,
        ).astype(bf16)
        ffn = jnp.concatenate(
            [
                lax.dynamic_slice(
                    mats, (layer, 0, (4 + 4 * j) * D + section * D), (1, rows, D)
                )[0]
                for j in range(2)
            ],
            axis=1,
        ).astype(bf16)
        return attn, ffn

    def own_small(small):
        bv = lax.dynamic_slice(small, (0, section * part), (LAYERS, part))
        b1 = lax.dynamic_slice(small, (0, AT_B1 + section * D), (LAYERS, D))
        return bv, b1

    bv_q, b1_q = own_small(query_small)
    bv_k, b1_k = own_small(key_small)
    attn_q, feed_q = [], []
    for layer in range(LAYERS):
        attn, ffn = own_cols(query_mats, layer)
        attn_q.append(gather_rows(attn))
        feed_q.append(gather_rows(ffn))
    attn_k, feed_k = [], []
    for layer in range(LAYERS):
        attn, ffn = own_cols(key_mats, layer)
        both = gather_rows(jnp.concatenate([attn, ffn], axis=1))
        attn_k.append(both[:, : 4 * part])
        feed_k.append(both[:, 4 * part :])

    kept = []
    inputs, sums = tokens, None
    for layer in range(LAYERS):
        found = attention(
            layer, inputs, sums, query_small, attn_q[layer], bv_q, lengths, True, "q"
        )
        parts, found = found[:2], found[2:]
        if layer > 0:
            inputs, hat, rate = found[:3]
            kept[-1] += (hat, rate)
            found = found[3:]
        sums = sum_parts(*parts)
        attn_in, attn_kept = inputs, tuple(found)
        p0, p1, inputs, hat, rate, hidden, active = feed(
            layer, inputs, sums, query_small, feed_q[layer], b1_q, True, "q"
        )
        sums = sum_parts(p0, p1)
        kept.append((attn_in, attn_kept, hat, rate, inputs, hidden, active))

    inputs_k, sums_k = key_tokens, None
    for layer in range(LAYERS):
        found = attention(
            layer, inputs_k, sums_k, key_small, attn_k[layer], bv_k, lengths, False, "k"
        )
        if layer > 0:
            inputs_k = found[2]
        sums_k = sum_parts(*found[:2])
        p0, p1, inputs_k = feed(
            layer, inputs_k, sums_k, key_small, feed_k[layer], b1_k, False, "k"
        )
        sums_k = sum_parts(p0, p1)
    pooled_k = call(
        partial(last_kernel, LAYERS - 1),
        "last_k",
        2 * TOK * D * 8,
        [inputs_k, *sums_k, key_small, lengths],
        [shaped((MICRO, CROPS, D), f32)],
    )[0]

    grad_feed, grad_attn, small_parts = [None] * LAYERS, [None] * LAYERS, [None] * LAYERS
    sums_out, bias_out = shaped((3, D), f32), shaped((1, D), f32)
    for layer in reversed(range(LAYERS)):
        attn_in, attn_kept, hat1, rate1, feed_in, hidden, active, *rest = kept[layer]
        last = layer == LAYERS - 1
        if last:
            operands = [feed_in, *sums, cotangent, lengths]
        else:
            operands = [carry, *sums, *rest]
        outs = [*part_out, wide_out, rows_out, rows_out, sums_out, bias_out]
        if last:
            outs += [rows_out, shaped((MICRO, CROPS, D), f32)]
        p0, p1, carry, branch, grad_hidden, sums_2, db1, *tail = call(
            partial(feed_back_kernel, layer, last),
            f"feed_back{layer}",
            4 * TOK * D * D,
            [*operands, query_small, feed_q[layer], hidden],
            outs,
        )
        if last:
            out_q, pooled_q = tail
        sums = sum_parts(p0, p1)
        grad_feed[layer] = jnp.concatenate(
            [dot_tn(feed_in, grad_hidden), dot_tn(branch, active)], axis=1
        ).astype(bf16)
        q, k, v, mixed, prob = attn_kept
        p0, p1, carry, branch, grad_proj, sums_1, dbv = call(
            partial(attention_back_kernel, layer),
            f"attention_back{layer}",
            2 * TOK * part * (4 * D + 10 * ROW),
            [carry, *sums, hat1, rate1, query_small, attn_q[layer], q, k, v, prob],
            [
                *part_out,
                wide_out,
                rows_out,
                shaped((TOK, 3 * part), bf16),
                sums_out,
                shaped((1, part), f32),
            ],
        )
        grad_attn[layer] = jnp.concatenate(
            [dot_tn(attn_in, grad_proj), dot_tn(branch, mixed)], axis=1
        ).astype(bf16)
        sums = sum_parts(p0, p1)
        own = section == 0
        vector = jnp.concatenate(
            [
                jnp.zeros((D,), f32),
                jnp.where(own, sums_1.reshape(-1), 0.0),
                jnp.zeros((4 * D,), f32),
                jnp.where(own, sums_2.reshape(-1), 0.0),
            ]
        )
        vector = lax.dynamic_update_slice(vector, dbv[0], (section * part,))
        small_parts[layer] = lax.dynamic_update_slice(vector, db1[0], (AT_B1 + section * D,))

    small_cols = LAYERS * SMALL // D
    chunk = SMALL // batches
    small_rows = jnp.stack(small_parts).reshape(LAYERS, batches, chunk).transpose(1, 0, 2)
    small_rows = small_rows.reshape(D, small_cols)
    small_rows = jnp.pad(small_rows, ((0, 0), (0, 128 - small_cols))).astype(bf16)
    got_feed, got_attn = [None] * LAYERS, [None] * LAYERS
    for layer in reversed(range(LAYERS)):
        got_feed[layer] = gather_section(scatter_rows(grad_feed[layer], rows))
        block = grad_attn[layer]
        if layer == 0:
            block = jnp.concatenate([block, small_rows], axis=1)
        got_attn[layer] = gather_section(scatter_rows(block, rows))

    grad_layers = []
    for layer in range(LAYERS):
        attn = got_attn[layer][:, :, : 4 * part].reshape(sections, rows, 4, part)
        attn = attn.transpose(1, 2, 0, 3).reshape(rows, 4 * D)
        ffn = got_feed[layer].reshape(sections, rows, 2, D).transpose(1, 2, 0, 3)
        grad_layers.append(jnp.concatenate([attn, ffn.reshape(rows, 8 * D)], axis=1))
    grad_mats = jnp.stack(grad_layers).astype(f32)
    small_sum = jnp.sum(got_attn[0][:, :, 4 * part : 4 * part + small_cols].astype(f32), axis=0)
    grad_small = small_sum.reshape(LAYERS, chunk)

    def own_part(block):
        return lax.dynamic_slice_in_dim(block, section * part, part, block.ndim - 1)

    total = jnp.concatenate([add_f32(sums[0], sums[1]), add_f32(sums[2], sums[3])], axis=0)
    input_grad = own_part((carry + total).astype(bf16))
    return (
        own_part(out_q),
        own_part(pooled_q),
        own_part(pooled_k),
        input_grad,
        grad_mats,
        grad_small,
        (query_mats - key_mats) * (1.0 - keep_rate),
        (query_small - key_small) * (1.0 - keep_rate),
    )


def add_f32(left, right):
    return left.astype(f32) + right.astype(f32)


def solution(mesh):
    in_specs = (
        P("batch", None),
        P("batch", None),
        P("batch", None),
        P("batch", None),
        P(None, "batch", None),
        P(),
        P(None, "batch", None),
        P(),
    )
    out_specs = (
        P("batch", "section"),
        P("batch", None, "section"),
        P("batch", None, "section"),
        P("batch", "section"),
        P(None, "batch", None),
        P(None, "batch"),
        P(None, "batch", None),
        P(),
    )
    return jax.shard_map(
        on_device, mesh=mesh, in_specs=in_specs, out_specs=out_specs, check_vma=False
    )
```

```python
from functools import partial

import jax
import jax.numpy as jnp
from jax import lax
from jax.experimental import pallas as pl
from jax.experimental.pallas import tpu as pltpu
from jax.sharding import PartitionSpec as P

HEADS = 12
HEAD_DIM = 64
D = 768
LAYERS = 2
MICRO = 2
ROW = 256
CROPS = 4
TOK = MICRO * ROW
SMALL = 11 * D

epsilon = 1e-05
keep_rate = 0.9995
score_scale = HEAD_DIM ** (-0.5)
bf16 = jnp.bfloat16
f32 = jnp.float32

AT_BV, AT_BO, AT_G1, AT_S1, AT_B1, AT_B2, AT_G2, AT_S2 = (
    0,
    D,
    2 * D,
    3 * D,
    4 * D,
    8 * D,
    9 * D,
    10 * D,
)


def swap_x(block):
    return lax.ppermute(block, "section", [(0, 1), (1, 0), (2, 3), (3, 2)])


def swap_y(block):
    return lax.ppermute(block, "section", [(0, 2), (2, 0), (1, 3), (3, 1)])


def swap_core(block):
    count = lax.axis_size("batch")
    return lax.ppermute(block, "batch", [(i, i ^ 1) for i in range(count)])


def shift_z(block, distance):
    count = lax.axis_size("batch")
    return lax.ppermute(block, "batch", [(i, (i + 2 * distance) % count) for i in range(count)])


def put_after(value, *others):
    return lax.optimization_barrier((value, *others))[0] if others else value


def sum_parts(name, part_0, part_1, beside=None, begun=(), later=()):
    with jax.named_scope(f"sum_{name}_first"):
        here_0, here_1 = swap_x(part_0), swap_y(put_after(part_1, *begun))
    with jax.named_scope(f"sum_{name}_second"):
        half_0, half_1 = add_parts(part_0, here_0), add_parts(part_1, here_1, later)
        there_0, there_1 = swap_y(half_0), swap_x(half_1)
    done = beside((half_0, half_1)) if beside is not None else ()
    return (half_0, there_0, half_1, there_1), done


def sum_own_cols(name, place, sent, kept):
    wide = kept.shape[1] // 2
    with jax.named_scope(f"sum_{name}"):
        came = swap_y(sent)
        sent, kept = call(
            half_kernel, "own_half", [place, kept, came], [shaped((TOK, wide), bf16)] * 2
        )
        return kept, swap_x(sent)


def sum_in_steps(name, part_0, part_1):
    with jax.named_scope(f"sum_{name}_first"):
        here_0, here_1 = swap_x(part_0), swap_y(part_1)
    after = yield (part_0,)
    with jax.named_scope(f"sum_{name}_second"):
        half_0 = add_parts(part_0, here_0, after)
        half_1 = add_parts(part_1, here_1, after)
        sums = (half_0, swap_y(half_0), half_1, swap_x(half_1))
    after = yield (half_0, half_1)
    return sums, after


def pass_z(block, step, first=0):
    count = lax.axis_size("batch")
    last = count // 2 - 1
    sources = range(first, last) if step > 0 else range(1, last + 1 - first)
    pairs = [(2 * z + c, 2 * (z + step) + c) for z in sources for c in range(2)]
    return lax.ppermute(block, "batch", pairs)


def pass_ends(block):
    pairs = [(2 * z + c, 2 * t + c) for z, t in ((2, 3), (1, 0)) for c in range(2)]
    return lax.ppermute(block, "batch", pairs)


def gather_rows(place, block, at_once=False, then=(), onward=()):
    places = lax.axis_size("batch") // 2
    apart = block.shape[0] % 16 == 0
    if places == 4 and apart and not at_once:
        left, right = pass_z(block, 1), pass_z(block, -1)
        left_2 = pass_z(put_after(left, *onward), 1, 1)
        right_2 = pass_z(put_after(right, *onward), -1, 1)
        second = call(
            second_kernel, "second", [place, left_2, right_2], [shaped(block.shape, bf16)]
        )[0]
        own, kind = [block, left, right, second, pass_ends(second)], "line"
    else:
        own, kind = [block] + [shift_z(block, d) for d in range(1, places)], "circle"
    other = [swap_core(put_after(chunk, *then)) for chunk in own]
    if apart:
        return own + other, kind
    me = lax.axis_index("batch")
    z, core = me // 2, me % 2
    pair = jnp.stack([jnp.stack(own), jnp.stack(other)], 1)
    pair = jnp.where(core == 0, pair, pair[:, ::-1])
    whole = jnp.take(pair, (z - jnp.arange(places)) % places, axis=0)
    return [whole.reshape(places * 2 * block.shape[0], block.shape[1])], "whole"


def landed(found):
    chunks, kind = found
    if kind == "whole":
        return ()
    return tuple(chunks[1:] if kind == "circle" else chunks[4:5])


def steps_of(found):
    chunks, kind = found
    return [(chunks[i],) for i in (1, 3, 4)] if kind == "line" else [(), (), ()]


def gather_section(block, in_turn=False, after=()):
    count = lax.axis_size("section")
    found = [block]
    for k in range(1, count):
        if in_turn:
            after = (*after, *found[1:][-1:])
        pairs = [(i, i ^ k) for i in range(count)]
        found.append(lax.ppermute(put_after(block, *after), "section", pairs))
    return found


def dot_nn(left, right):
    return jnp.dot(left, right, preferred_element_type=f32)


def dot_nt(left, right):
    return lax.dot_general(left, right, (((1,), (1,)), ((), ())), preferred_element_type=f32)


def dot_tn(left, right):
    return lax.dot_general(left, right, (((0,), (0,)), ((), ())), preferred_element_type=f32)


def add_low(left, right):
    return (left.astype(f32) + right.astype(f32)).astype(bf16)


def ends_of(lens_ref, row):
    ends, total = [], 0
    for c in range(CROPS):
        total = total + lens_ref[row, c]
        ends.append(total)
    return ends


def segments(ends, shape, dim):
    position = lax.broadcasted_iota(jnp.int32, shape, dim)
    segment = jnp.zeros(shape, jnp.int32)
    for end in ends:
        segment = segment + (position >= end).astype(jnp.int32)
    return position, segment


def allowed_of(lens_ref, row):
    ends = ends_of(lens_ref, row)
    pos_q, seg_q = segments(ends, (ROW, 1), 0)
    pos_k, seg_k = segments(ends, (1, ROW), 1)
    seg_k = jnp.where(pos_k < ends[-1], seg_k, -1)
    return (seg_q == seg_k) | (pos_q == pos_k)


def pooled_of(lens_ref, row, values):
    ends = ends_of(lens_ref, row)
    pos, seg = segments(ends, (1, ROW), 1)
    crop = lax.broadcasted_iota(jnp.int32, (8, 1), 0)
    seg = jnp.where(pos < ends[-1], seg, -1)
    member = (seg == crop).astype(f32).astype(bf16)
    counts = jnp.ones((8, 1), f32)
    for c in range(CROPS):
        counts = jnp.where(crop == c, jnp.maximum(lens_ref[row, c], 1).astype(f32), counts)
    return (dot_nn(member, values) / counts)[:CROPS]


def standard(summed):
    centre = summed - jnp.mean(summed, axis=-1, keepdims=True)
    spread = jnp.mean(centre * centre, axis=-1, keepdims=True)
    rate = lax.rsqrt(spread + epsilon)
    return centre * rate, rate


def small_at(small_ref, layer, offset, width=D):
    return small_ref[layer : layer + 1, offset : offset + width]


def own_cols(block, section, part):
    value = block[:, :part]
    for k in range(1, block.shape[1] // part):
        value = jnp.where(section == k, block[:, k * part : (k + 1) * part], value)
    return value


def rows_of(row):
    return slice(row * ROW, (row + 1) * ROW)


def norm_in(layer, gain_at, shift_at, bias_at, base_ref, sums, small_ref, row):
    half, other = sums[2 * row], sums[2 * row + 1]
    branch = half[...].astype(f32) + other[...].astype(f32) + small_at(small_ref, layer, bias_at)
    hat, rate = standard(base_ref[rows_of(row), :].astype(f32) + branch)
    out = hat * small_at(small_ref, layer, gain_at) + small_at(small_ref, layer, shift_at)
    return out.astype(bf16), hat, rate


def add_kernel(left_ref, right_ref, out_ref):
    out_ref[...] = add_low(left_ref[...], right_ref[...])


def take_kernel(units, place_ref, query_ref, key_ref, *refs):
    outs, (held, sems) = refs[: len(units)], refs[len(units) :]
    section = place_ref[0]
    part = D // SECTIONS
    first = (section * part) // 128 * 128
    at, copies = 0, []
    for out_ref, pieces in zip(outs, units):
        to = 0
        for encoder, layer, kind in pieces:
            mats_ref = query_ref if encoder == "query" else key_ref
            for j in range(4 if kind == "attention" else 2):
                if kind == "attention":
                    source, wide, got = j * D + first, 256, part
                else:
                    source, wide, got = (4 + 4 * j + section) * D, D, D
                source = mats_ref.at[layer, :, pl.ds(pl.multiple_of(source, 128), wide)]
                copy = pltpu.make_async_copy(
                    source, held.at[:, at : at + wide], sems.at[len(copies)]
                )
                copy.start()
                copies.append((copy, at, wide, out_ref, to, got))
                at, to = at + wide, to + got
    for copy, at, wide, out_ref, to, got in copies:
        copy.wait()
        block = held[:, at : at + wide]
        if wide == 256:
            block = jnp.where(section % 2 == 1, pltpu.roll(block, 192, 1), block)
        out_ref[:, to : to + got] = block[:, :got].astype(bf16)


class Columns:
    def __init__(self, ref, at):
        self.ref, self.at = ref, at

    def __getitem__(self, index):
        start, stop = index[1].start or 0, index[1].stop
        return self.ref[:, self.at + start : self.at + stop]


def second_kernel(place_ref, left_ref, right_ref, out_ref):
    right_half = place_ref[1] >= 4
    out_ref[...] = jnp.where(right_half, left_ref[...], right_ref[...])


def place_rows(kind, refs, at, place_ref, whole_ref):
    wide = whole_ref.shape[1]
    rows, count = refs[0].shape[0], len(refs) // 2
    z, core = place_ref[1] // 2, place_ref[1] % 2

    def put(i, source):
        for chunk, its in ((refs[i], core), (refs[count + i], 1 - core)):
            start = pl.multiple_of((source * 2 + its) * rows, 16)
            whole_ref[pl.ds(start, rows), :] = chunk[:, at : at + wide]

    if kind == "circle":
        for i in range(count):
            put(i, lax.rem(z + count - i, count))
        return
    put(0, z)
    put(1, jnp.where(z == 0, 3, z - 1))
    put(2, jnp.where(z == 3, 0, z + 1))
    put(3, jnp.where(z >= 2, z - 2, z + 2))

    @pl.when((z == 0) | (z == 3))
    def _():
        put(4, 3 - z)


def weights_in(kind, refs, at, place_ref, whole_ref):
    if len(refs) == 1:
        return Columns(refs[0], at)
    place_rows(kind, refs, at, place_ref, whole_ref)
    return whole_ref


def attention_kernel(layer, first, keep, kind, count, at, *refs):
    refs = list(refs)
    place_ref, lens_ref, small_ref = refs[:3]
    chunk_refs, refs = refs[3 : 3 + count], refs[3 + count :]
    base_ref, refs = refs[0], refs[1:]
    if not first:
        sums, refs = refs[:4], refs[4:]
    part_refs, outs = refs[:2], refs[2:]
    whole_ref, outs = outs[-1], outs[:-1]
    weights_ref = weights_in(kind, chunk_refs, at, place_ref, whole_ref)
    if not first:
        y_ref, outs = outs[0], outs[1:]
        if keep:
            hat_ref, rate_ref = outs[:2]
            outs = outs[2:]
    if keep:
        q_ref, k_ref, v_ref, mixed_ref, prob_ref = outs
    part = D // SECTIONS
    bv = own_cols(small_at(small_ref, layer, AT_BV), place_ref[0], part)
    lane = lax.broadcasted_iota(jnp.int32, (1, part), 1)
    for row in range(MICRO):
        here = rows_of(row)
        if first:
            inputs = base_ref[here, :]
        else:
            inputs, hat, rate = norm_in(
                layer - 1, AT_G2, AT_S2, AT_B2, base_ref, sums, small_ref, row
            )
            y_ref[here, :] = inputs
            if keep:
                hat_ref[here, :] = hat
                rate_ref[here, :] = jnp.broadcast_to(rate, (ROW, 128))
        project = dot_nn(inputs, weights_ref[:, : 3 * part])
        query = project[:, :part]
        key_rows = project[:, part : 2 * part].astype(bf16)
        values = (project[:, 2 * part :] + bv).astype(bf16)
        allowed = allowed_of(lens_ref, row)
        mixed = jnp.zeros((ROW, part), f32)
        for head in range(part // HEAD_DIM):
            inside = (lane >= head * HEAD_DIM) & (lane < (head + 1) * HEAD_DIM)
            head_q = jnp.where(inside, query, 0.0).astype(bf16)
            scores = jnp.where(allowed, dot_nt(head_q, key_rows) * score_scale, -1e30)
            terms = jnp.exp(scores - jnp.max(scores, axis=-1, keepdims=True))
            prob = terms / jnp.sum(terms, axis=-1, keepdims=True)
            if keep:
                prob_ref[row, head] = prob
            mixed = jnp.where(inside, dot_nn(prob.astype(bf16), values), mixed)
        mixed = mixed.astype(bf16)
        part_refs[row][...] = dot_nt(mixed, weights_ref[:, 3 * part : 4 * part]).astype(bf16)
        if keep:
            q_ref[here, :] = query.astype(bf16)
            k_ref[here, :] = key_rows
            v_ref[here, :] = values
            mixed_ref[here, :] = mixed


def feed_kernel(layer, keep, kind, count, at, place_ref, small_ref, base_ref, *refs):
    sums, chunk_refs, refs = refs[:4], refs[4 : 4 + count], refs[4 + count :]
    part_refs, y_ref, whole_ref = refs[:2], refs[2], refs[-1]
    weights_ref = weights_in(kind, chunk_refs, at, place_ref, whole_ref)
    if keep:
        hat_ref, rate_ref, hidden_ref, active_ref = refs[3:7]
    b1 = own_cols(small_at(small_ref, layer, AT_B1, 4 * D), place_ref[0], D)
    for row in range(MICRO):
        here = rows_of(row)
        inputs, hat, rate = norm_in(layer, AT_G1, AT_S1, AT_BO, base_ref, sums, small_ref, row)
        y_ref[here, :] = inputs
        hidden = dot_nn(inputs, weights_ref[:, :D]) + b1
        active = (0.5 * hidden * (1.0 + lax.erf(hidden * (0.5**0.5)))).astype(bf16)
        part_refs[row][...] = dot_nt(active, weights_ref[:, D : 2 * D]).astype(bf16)
        if keep:
            hat_ref[here, :] = hat
            rate_ref[here, :] = jnp.broadcast_to(rate, (ROW, 128))
            hidden_ref[here, :] = hidden
            active_ref[here, :] = active


def last_kernel(layer, place_ref, lens_ref, small_ref, base_ref, *refs):
    sums, pooled_ref = refs[:4], refs[4]
    for row in range(MICRO):
        out, hat, rate = norm_in(layer, AT_G2, AT_S2, AT_B2, base_ref, sums, small_ref, row)
        part = pooled_ref.shape[-1]
        pooled_ref[row] = own_cols(pooled_of(lens_ref, row, out), place_ref[0], part)


def norm_back(grad_out, hat, rate, gain):
    inner = grad_out * gain
    return rate * (
        inner
        - jnp.mean(inner, axis=-1, keepdims=True)
        - hat * jnp.mean(inner * hat, axis=-1, keepdims=True)
    )


def row_sum(block):
    return jnp.sum(block, axis=0, keepdims=True)


def arrived_grad(base_ref, sums, row):
    grad = base_ref[rows_of(row), :] + (
        sums[2 * row][...].astype(f32) + sums[2 * row + 1][...].astype(f32)
    )
    return grad.astype(bf16)


def feed_back_kernel(layer, last, place_ref, small_ref, weights_ref, hidden_ref, base_ref, *refs):
    sums, refs = refs[:4], refs[4:]
    if last:
        cot_ref, lens_ref = refs[:2]
    else:
        hat_ref, rate_ref = refs[:2]
    part_refs = refs[2:4]
    carry_ref, branch_ref, grad_hidden_ref, sums_ref, bias_ref = refs[4:9]
    if last:
        y_ref, pooled_ref = refs[9:]
    gain = small_at(small_ref, layer, AT_G2)
    totals = [jnp.zeros((1, D), f32) for _ in range(4)]
    for row in range(MICRO):
        here = rows_of(row)
        if last:
            out, hat, rate = norm_in(layer, AT_G2, AT_S2, AT_B2, base_ref, sums, small_ref, row)
            part = y_ref.shape[1]
            y_ref[here, :] = own_cols(out, place_ref[0], part)
            pooled_ref[row] = own_cols(pooled_of(lens_ref, row, out), place_ref[0], part)
            grad_out = cot_ref[here, :].astype(f32)
        else:
            hat, rate = hat_ref[here, :], rate_ref[here, :1]
            grad_out = arrived_grad(base_ref, sums, row).astype(f32)
        grad = norm_back(grad_out, hat, rate, gain)
        carry_ref[here, :] = grad
        branch = grad.astype(bf16)
        branch_ref[here, :] = branch
        grad_active = dot_nn(branch, weights_ref[:, D : 2 * D])
        hidden = hidden_ref[here, :]
        slope = 0.5 * (1.0 + lax.erf(hidden * (0.5**0.5))) + hidden * (
            jnp.exp(-0.5 * hidden * hidden) * 0.3989422804014327
        )
        grad_hidden = (grad_active * slope).astype(bf16)
        grad_hidden_ref[here, :] = grad_hidden
        part_refs[row][...] = dot_nt(grad_hidden, weights_ref[:, :D]).astype(bf16)
        totals[0] += row_sum(branch.astype(f32))
        totals[1] += row_sum(grad_out * hat)
        totals[2] += row_sum(grad_out)
        totals[3] += row_sum(grad_hidden.astype(f32))
    for i in range(3):
        sums_ref[i : i + 1, :] = totals[i]
    bias_ref[...] = totals[3]


def attention_back_kernel(layer, small_ref, place_ref, weights_ref, base_ref, *refs):
    sums, hat_ref, rate_ref = refs[:4], refs[4], refs[5]
    q_ref, k_ref, v_ref, prob_ref = refs[6:10]
    part_refs = refs[10:12]
    carry_ref, branch_ref, grad_proj_ref, sums_ref, bias_ref = refs[12:]
    part = q_ref.shape[1]
    lane = lax.broadcasted_iota(jnp.int32, (1, part), 1)
    gain = small_at(small_ref, layer, AT_G1)
    totals = [jnp.zeros((1, D), f32) for _ in range(3)] + [jnp.zeros((1, part), f32)]
    for row in range(MICRO):
        here = rows_of(row)
        hat, rate = hat_ref[here, :], rate_ref[here, :1]
        grad_out = arrived_grad(base_ref, sums, row).astype(f32)
        grad = norm_back(grad_out, hat, rate, gain)
        carry_ref[here, :] = grad
        branch = grad.astype(bf16)
        branch_ref[here, :] = branch
        grad_mixed = dot_nn(branch, weights_ref[:, 3 * part : 4 * part])
        low_mixed = grad_mixed.astype(bf16)
        query, key_rows, values = q_ref[here, :], k_ref[here, :], v_ref[here, :]
        grads = [jnp.zeros((ROW, part), f32) for _ in range(3)]
        for head in range(part // HEAD_DIM):
            inside = (lane >= head * HEAD_DIM) & (lane < (head + 1) * HEAD_DIM)
            prob = prob_ref[row, head]
            head_mixed = jnp.where(inside, grad_mixed, 0.0).astype(bf16)
            grad_prob = dot_nt(head_mixed, values)
            grad_scores = prob * (
                grad_prob - jnp.sum(grad_prob * prob, axis=-1, keepdims=True)
            )
            grad_scores = grad_scores.astype(bf16)
            grad_q = dot_nn(grad_scores, key_rows) * score_scale
            grad_k = dot_tn(grad_scores, query) * score_scale
            grad_v = dot_tn(prob.astype(bf16), low_mixed)
            grads = [
                jnp.where(inside, new, old) for new, old in zip((grad_q, grad_k, grad_v), grads)
            ]
        grad_proj = jnp.concatenate(grads, axis=1).astype(bf16)
        grad_proj_ref[here, :] = grad_proj
        parted = dot_nt(grad_proj, weights_ref[:, : 3 * part]).astype(bf16)
        if layer > 0:
            part_refs[row][...] = parted
        else:
            half, upper = D // 2, place_ref[0] >= 2
            part_refs[0][here, :] = jnp.where(upper, parted[:, :half], parted[:, half:])
            part_refs[1][here, :] = jnp.where(upper, parted[:, half:], parted[:, :half])
        totals[0] += row_sum(branch.astype(f32))
        totals[1] += row_sum(grad_out * hat)
        totals[2] += row_sum(grad_out)
        totals[3] += row_sum(grads[2].astype(bf16).astype(f32))
    for i in range(3):
        sums_ref[i : i + 1, :] = totals[i]
    bias_ref[...] = totals[3]


def half_kernel(place_ref, kept_ref, came_ref, sent_out, kept_out):
    total = add_low(kept_ref[...], came_ref[...])
    wide = kept_out.shape[1]
    odd = place_ref[0] % 2 == 1
    kept_out[...] = jnp.where(odd, total[:, wide:], total[:, :wide])
    sent_out[...] = jnp.where(odd, total[:, :wide], total[:, wide:])


def input_kernel(place_ref, base_ref, kept_ref, came_ref, out_ref):
    base = own_cols(base_ref[...], place_ref[0], out_ref.shape[1])
    total = kept_ref[...].astype(f32) + came_ref[...].astype(f32)
    out_ref[...] = (base + total).astype(bf16)


def pack_kernel(rows, place_ref, *refs):
    ins, (out_ref, vector_ref, piece_ref) = refs[: 4 * LAYERS], refs[4 * LAYERS :]
    section = place_ref[0]
    own = section == 0
    slot = rows // LAYERS
    share = SMALL // (D // rows)
    out_ref[...] = jnp.zeros(out_ref.shape, bf16)
    piece_ref[...] = jnp.zeros(piece_ref.shape, f32)
    for layer in range(LAYERS):
        norm_1, value_bias, norm_2, hidden_bias = ins[4 * layer : 4 * layer + 4]
        part = value_bias.shape[1]
        for k in range(SECTIONS):
            mine = section == k
            vector_ref[:, k * part : (k + 1) * part] = jnp.where(mine, value_bias[...], 0.0)
            at = AT_B1 + k * D
            vector_ref[:, at : at + D] = jnp.where(mine, hidden_bias[...], 0.0)
        for i in range(3):
            vector_ref[:, AT_BO + i * D : AT_BO + (i + 1) * D] = jnp.where(
                own, norm_1[i : i + 1, :], 0.0
            )
            vector_ref[:, AT_B2 + i * D : AT_B2 + (i + 1) * D] = jnp.where(
                own, norm_2[i : i + 1, :], 0.0
            )
        for i in range(SMALL // 128):
            piece_ref[i : i + 1, :] = vector_ref[:, i * 128 : (i + 1) * 128]
        for b in range(D // rows):
            first = b * share // 128
            last = (b * share + share - 1) // 128 + 1
            start = b * rows + layer * slot
            out_ref[start : start + last - first, :] = piece_ref[first:last, :].astype(bf16)


def grad_kernel(rows, count, place_ref, *refs):
    mine_ref, other_ref, whole_ref = refs[-3:]
    at = 0
    for left_ref, right_ref in zip(refs[: 2 * count : 2], refs[1 : 2 * count : 2]):
        wide = right_ref.shape[1]
        whole_ref[:, at : at + wide] = dot_tn(left_ref[...], right_ref[...]).astype(bf16)
        at += wide
    if at < whole_ref.shape[1]:
        whole_ref[:, at:] = refs[2 * count][...]
    core = place_ref[1] % 2
    for out, owner in ((other_ref, 1 - core), (mine_ref, core)):
        for z in range(mine_ref.shape[0]):
            start = pl.multiple_of((2 * z + owner) * rows, 16)
            out[z] = whole_ref[pl.ds(start, rows), :]


def chip_kernel(place_ref, mine_ref, came_ref, *refs):
    places = mine_ref.shape[0]
    z = place_ref[1] // 2
    for d, out in enumerate(refs):
        owner = lax.rem(z + d, places)
        out[...] = add_low(mine_ref[owner], came_ref[owner])


def total_kernel(*refs):
    total = refs[0][...].astype(f32)
    for ref in refs[1:-1]:
        total = total + ref[...].astype(f32)
    refs[-1][...] = total.astype(bf16)


def place_kernel(copies, place_ref, *refs):
    out_ref, small_ref, vector_ref = refs[-3:]
    section = place_ref[0]
    part = D // SECTIONS
    rows = out_ref.buffer.shape[1]
    share = small_ref.shape[1]

    def owned(group, start, stop):
        found = []
        for slot in range(SECTIONS):
            value = group[0][:, start:stop]
            for k in range(1, SECTIONS):
                value = jnp.where(section ^ slot == k, group[k][:, start:stop], value)
            found.append(value.astype(f32))
        return found

    groups = [refs[i * SECTIONS : (i + 1) * SECTIONS] for i in range(3)]
    for copy in copies:
        copy.wait()
    for layer in reversed(range(LAYERS)):
        if layer > 0:
            attn, ffn = owned(groups[2], 0, D), owned(groups[2], D, 3 * D)
        else:
            attn, ffn = owned(groups[0], 0, D), owned(groups[1], 0, 2 * D)
        for j in range(4):
            columns = [a[:, j * part : (j + 1) * part] for a in attn]
            out_ref[layer, :, j * D : (j + 1) * D] = jnp.concatenate(columns, axis=1)
        for slot, block in enumerate(ffn):
            for j in range(2):
                start = (4 + 4 * j + slot) * D
                out_ref[layer, :, start : start + D] = block[:, j * D : (j + 1) * D]
        out_ref.push(layer)
    for layer in range(LAYERS):
        slot = rows // LAYERS
        at, count = layer * slot, min(16, slot)
        total = jnp.zeros((count, 128), f32)
        for k in range(SECTIONS):
            total = total + refs[k][at : at + count, 4 * part :].astype(f32)
        for i in range(vector_ref.shape[1] // 128):
            vector_ref[:, i * 128 : (i + 1) * 128] = total[i : i + 1, :]
        wide = vector_ref.shape[1]
        inside = lax.rem(place_ref[1] * share, 128)
        moved = pltpu.roll(jnp.broadcast_to(vector_ref[...], (8, wide)), wide - inside, 1)
        small_ref[layer : layer + 1, :] = moved[:1, :share]


def momentum_kernel(layer, query_ref, key_ref, query_small, key_small, *refs):
    out_ref, small_out, q_buf, k_buf, out_buf, in_sems, out_sems = refs[-7:]
    rows = query_ref.shape[1]
    depth, step = q_buf.shape[0], q_buf.shape[1]
    blocks = [(layer, pl.ds(j, step)) for j in range(0, rows, step)]

    def fetch(n):
        i, j = blocks[n]
        pair = [
            pltpu.make_async_copy(ref.at[i, j], buf.at[n % depth], in_sems.at[m, n % depth])
            for m, (ref, buf) in enumerate(((query_ref, q_buf), (key_ref, k_buf)))
        ]
        for copy in pair:
            copy.start()
        return pair

    small_out[...] = (query_small[...] - key_small[...]) * (1.0 - keep_rate)
    coming = [fetch(n) for n in range(min(depth, len(blocks)))]
    leaving = []
    for n, (i, j) in enumerate(blocks):
        for copy in coming[n]:
            copy.wait()
        if n >= depth:
            leaving[n - depth].wait()
        at = n % depth
        out_buf[at] = (q_buf[at] - k_buf[at]) * (1.0 - keep_rate)
        leaving.append(pltpu.make_async_copy(out_buf.at[at], out_ref.at[i, j], out_sems.at[at]))
        leaving[-1].start()
        if n + depth < len(blocks):
            coming.append(fetch(n + depth))
    for copy in leaving[-depth:]:
        copy.wait()


VMEM = pl.BlockSpec(memory_space=pltpu.VMEM)
SMEM = pl.BlockSpec(memory_space=pltpu.SMEM)
ANY = pl.BlockSpec(memory_space=pl.ANY)
SECTIONS = 4


def shaped(shape, kind):
    return jax.ShapeDtypeStruct(shape, kind)


class Raw:
    def __init__(self, value):
        self.value = value


class Leaving:
    def __init__(self, target, buffer, sems):
        self.buffer, self.target, self.sems, self.copies = buffer, target, sems, []

    def __setitem__(self, index, value):
        self.buffer[index] = value

    def push(self, part):
        sem = self.sems.at[len(self.copies)]
        copy = pltpu.make_async_copy(self.buffer.at[part], self.target.at[part], sem)
        copy.start()
        self.copies.append(copy)


def call(body, name, operands, outs, after=(), scratch=(), limit=12, aliases=None):
    arrays = [a.value if isinstance(a, Raw) else a for a in operands]
    results = [a.value if isinstance(a, Raw) else a for a in outs]
    specs = []
    for given, array in zip(operands, arrays):
        specs.append(ANY if isinstance(given, Raw) else SMEM if array.dtype == jnp.int32 else VMEM)
    count, skipped = len(operands), len(after)

    def kernel(*refs):
        body(*refs[:count], *refs[count + skipped :])

    return pl.pallas_call(
        kernel,
        name=name,
        in_specs=specs + [ANY] * len(after),
        out_specs=[ANY if isinstance(a, Raw) else VMEM for a in outs],
        out_shape=results,
        scratch_shapes=list(scratch),
        input_output_aliases=aliases or {},
        cost_estimate=pl.CostEstimate(flops=1, bytes_accessed=1, transcendentals=0),
        compiler_params=pltpu.CompilerParams(vmem_limit_bytes=limit * 2**20),
    )(*arrays, *after)


part_out = [shaped((ROW, D), bf16)] * 2
rows_out = shaped((TOK, D), bf16)
wide_out = shaped((TOK, D), f32)
rate_out = shaped((TOK, 128), f32)


def add_parts(left, right, after=()):
    return call(add_kernel, "add_parts", [left, right], [shaped(left.shape, bf16)], after)[0]


def momentum(layer, query, key, query_small, key_small, into, after):
    depth, step = 3, 24
    block = (depth, step, query.shape[2])
    return call(
        partial(momentum_kernel, layer),
        f"momentum{layer}",
        [Raw(query), Raw(key), query_small, key_small] + [Raw(a) for a in into],
        [Raw(shaped(query.shape, f32)), shaped(query_small.shape, f32)],
        after,
        [pltpu.VMEM(block, f32)] * 3
        + [pltpu.SemaphoreType.DMA((2, depth)), pltpu.SemaphoreType.DMA((depth,))],
        58,
        {4: 0} if into else {},
    )


def take(place, query_mats, key_mats, units, after=()):
    rows = query_mats.shape[1]
    kinds = [[kind for _, _, kind in pieces] for pieces in units]
    cols = [sum(D if kind == "attention" else 2 * D for kind in found) for found in kinds]
    held = sum(4 * 256 if kind == "attention" else 2 * D for found in kinds for kind in found)
    count = sum(4 if kind == "attention" else 2 for found in kinds for kind in found)
    return call(
        partial(take_kernel, units),
        "take",
        [place, Raw(query_mats), Raw(key_mats)],
        [shaped((rows, c), bf16) for c in cols],
        after,
        [pltpu.VMEM((rows, held), f32), pltpu.SemaphoreType.DMA((count,))],
        limit=58,
    )


def attention(layer, inputs, sums, shared, weights, keep, tag, after=()):
    (chunks, kind), at = weights
    part = D // SECTIONS
    operands = [*shared, *chunks, inputs] + ([] if sums is None else list(sums))
    outs = list(part_out)
    if sums is not None:
        outs += [rows_out] + ([wide_out, rate_out] if keep else [])
    if keep:
        outs += [shaped((TOK, part), bf16)] * 4
        outs += [shaped((MICRO, part // HEAD_DIM, ROW, ROW), f32)]
    shape = (D, 4 * part)
    return call(
        partial(attention_kernel, layer, sums is None, keep, kind, len(chunks), at),
        f"attention_{tag}{layer}",
        operands,
        outs + ([shaped(shape, bf16)] if keep else []),
        after,
        [] if keep else [pltpu.VMEM(shape, bf16)],
    )


def feed(layer, inputs, sums, shared, weights, keep, tag, after=()):
    (chunks, kind), at = weights
    place, lengths, small = shared
    shape = (D, 2 * D)
    outs = [*part_out, rows_out]
    outs += [wide_out, rate_out, wide_out, rows_out, shaped(shape, bf16)] if keep else []
    return call(
        partial(feed_kernel, layer, keep, kind, len(chunks), at),
        f"feed_{tag}{layer}",
        [place, small, inputs, *sums, *chunks],
        outs,
        after,
        [] if keep else [pltpu.VMEM(shape, bf16)],
    )


def grad_over_batch(place, rows, pairs, extra=None, after=(), begin=(), in_turn=False):
    places = lax.axis_size("batch") // 2
    wide = sum(right.shape[1] for _, right in pairs)
    cols = wide + (0 if extra is None else extra.shape[1])
    chunk = shaped((rows, cols), bf16)
    if rows % 16 == 0:
        mine, other = call(
            partial(grad_kernel, rows, len(pairs)),
            "grad",
            [place, *(x for pair in pairs for x in pair)] + ([] if extra is None else [extra]),
            [shaped((places, rows, cols), bf16)] * 2,
            begin,
            [pltpu.VMEM((D, cols), bf16)],
        )
        chunks = call(
            chip_kernel, "chip_sum", [place, mine, swap_core(other)], [chunk] * places, after
        )
    else:
        me = lax.axis_index("batch")
        z, core = me // 2, me % 2
        block = jnp.concatenate([dot_tn(l, r).astype(bf16) for l, r in pairs], axis=1)
        if extra is not None:
            block = jnp.concatenate([block, extra], axis=1)
        parted = block.reshape(places, 2, rows, cols)
        mine = lax.dynamic_index_in_dim(parted, core, 1, keepdims=False)
        other = lax.dynamic_index_in_dim(parted, 1 - core, 1, keepdims=False)
        chip = add_low(mine, swap_core(other))
        chunks = [
            lax.dynamic_index_in_dim(chip, (z + d) % places, 0, keepdims=False)
            for d in range(places)
        ]
    came = {}
    for d in sorted(range(1, places), key=lambda d: min(d, places - d)):
        came[d] = shift_z(put_after(chunks[d], *(list(came.values())[-1:] if in_turn else ())), d)
    total = call(total_kernel, "total", [chunks[0], *came.values()], [chunk])[0]
    return total, (*came.values(), chunks[0])


def on_device(tokens, key_tokens, cotangent, lengths, query_mats, query_small, key_mats, key_small):
    section, batch = lax.axis_index("section"), lax.axis_index("batch")
    part = D // SECTIONS
    rows = query_mats.shape[1]
    place = jnp.stack([section, batch]).astype(jnp.int32)
    shared_q, shared_k = (place, lengths, query_small), (place, lengths, key_small)
    own_out = shaped((TOK, part), bf16)
    pooled_out = shaped((MICRO, CROPS, part), f32)

    units = [
        [("query", 0, "attention")],
        [("query", 0, "feed"), ("query", 1, "attention")],
        [("query", 1, "feed"), ("key", 0, "attention")],
        [("key", 0, "feed"), ("key", 1, "attention")],
        [("key", 1, "feed")],
    ]
    blocks = take(place, query_mats, key_mats, units[:1])
    blocks += take(place, query_mats, key_mats, units[1:], (blocks[0],))
    both = (query_mats, key_mats, query_small, key_small)
    mats_step, early_step = momentum(0, *both, (), (blocks[1],))
    with jax.named_scope("weights_unit_0"):
        chunks = [gather_rows(place, blocks[0], True, (early_step,))]
    attn_q = [(chunks[0], 0)]
    found_0 = attention(0, tokens, None, shared_q, attn_q[0], True, "q")
    for n in range(1, len(units)):
        with jax.named_scope(f"weights_unit_{n}"):
            before = landed(chunks[-1])
            if n == 1:
                before = (*chunks[0][0][1 : len(chunks[0][0]) // 2], early_step)
            block = put_after(blocks[n], *before)
            chunks.append(gather_rows(place, block, onward=found_0[:1] if n == 1 else ()))
    attn_q.append((chunks[1], 2 * D))
    feed_q = [(chunks[1], 0), (chunks[2], 0)]
    attn_k = [(chunks[2], 2 * D), (chunks[3], 2 * D)]
    feed_k = [(chunks[3], 0), (chunks[4], 0)]

    def key_encoder():
        after = yield
        inputs, sums = key_tokens, None
        for layer in range(LAYERS):
            found = attention(layer, inputs, sums, shared_k, attn_k[layer], False, "k", after)
            inputs = found[2] if layer > 0 else inputs
            sums, after = yield from sum_in_steps(f"k{2 * layer}", *found[:2])
            p0, p1, inputs = feed(layer, inputs, sums, shared_k, feed_k[layer], False, "k", after)
            sums, after = yield from sum_in_steps(f"k{2 * layer + 1}", p0, p1)
        key_end.append((inputs, sums))
        yield ()

    key_end = []
    steps = key_encoder()
    next(steps)

    def beside(arrays):
        return () if key_end else steps.send(arrays)

    lines = [steps_of(found) for found in chunks[1:]]

    kept, weights = [], []
    inputs, sums = tokens, None
    done = ()
    gates = [((), ()), ((), lines[1][0]), (lines[1][1], lines[1][2]), (lines[2][0], lines[2][1])]
    for layer in range(LAYERS):
        found = found_0
        if layer > 0:
            found = attention(layer, inputs, sums, shared_q, attn_q[layer], True, "q", done)
        parts, found, attn_w = found[:2], found[2:-1], found[-1]
        if layer > 0:
            inputs, hat, rate = found[:3]
            kept[-1] += (hat, rate)
            found = found[3:]
        along = beside if layer > 0 else None
        sums, done = sum_parts(f"q{2 * layer}", *parts, along, *gates[2 * layer])
        attn_in, attn_kept = inputs, tuple(found)
        p0, p1, inputs, hat, rate, hidden, active, feed_w = feed(
            layer, inputs, sums, shared_q, feed_q[layer], True, "q", done
        )
        sums, done = sum_parts(f"q{2 * layer + 1}", p0, p1, along, *gates[2 * layer + 1])
        if chunks[0][1] == "whole":
            attn_w, feed_w = (
                found[0][:, at : at + wide]
                for ((found, _), at), wide in ((attn_q[layer], D), (feed_q[layer], 2 * D))
            )
        weights.append((attn_w, feed_w))
        kept.append((attn_in, attn_kept, hat, rate, inputs, hidden, active))

    small_parts = [None] * LAYERS
    sums_out, turn = shaped((3, D), f32), lines[3][2]
    for layer in reversed(range(LAYERS)):
        attn_in, attn_kept, hat1, rate1, feed_in, hidden, active, *rest = kept[layer]
        attn_w, feed_w = weights[layer]
        last = layer == LAYERS - 1
        operands = [feed_in, *sums, cotangent, lengths] if last else [carry, *sums, *rest]
        outs = [*part_out, wide_out, rows_out, rows_out, sums_out, shaped((1, D), f32)]
        if last:
            outs += [own_out, pooled_out]
        p0, p1, carry, branch, grad_hidden, sums_2, db1, *tail = call(
            partial(feed_back_kernel, layer, last),
            f"feed_back{layer}",
            [place, query_small, feed_w, hidden, *operands],
            outs,
            done,
        )
        if last:
            out_q, pooled_q = tail
        gate = (lines[2][2], lines[3][0]) if last else (turn[:1], turn[1:2])
        sums, done = sum_parts(f"back{2 * layer + 1}", p0, p1, beside, *gate)
        feed_pairs = [(feed_in, grad_hidden), (branch, active)]
        if layer == 0:
            with jax.named_scope("grad_feed0"):
                total_feed, turn_feed = grad_over_batch(
                    place, rows, feed_pairs, None, turn[1:2], sums[::2]
                )
            done = (*done, turn_feed[-1])
        q, k, v, mixed, prob = attn_kept
        p0, p1, carry, branch, grad_proj, sums_1, dbv = call(
            partial(attention_back_kernel, layer),
            f"attention_back{layer}",
            [query_small, place, attn_w, carry, *sums, hat1, rate1, q, k, v, prob],
            [
                *(part_out if layer > 0 else [shaped((TOK, D // 2), bf16)] * 2),
                wide_out,
                rows_out,
                shaped((TOK, 3 * part), bf16),
                sums_out,
                shaped((1, part), f32),
            ],
            done,
        )
        if layer > 0:
            sums, done = sum_parts(f"back{2 * layer}", p0, p1, beside, *lines[3][1:])
        else:
            sums = sum_own_cols("back0", place, p0, p1)
        small_parts[layer] = [sums_1, dbv, sums_2, db1]
        attn_pairs = [(attn_in, grad_proj), (branch, mixed)]
        if layer > 0:
            with jax.named_scope("grad_layer1"):
                total_layer, turn = grad_over_batch(
                    place, rows, attn_pairs + feed_pairs, None, turn, sums[::2], True
                )
    (extra,) = call(
        partial(pack_kernel, rows),
        "pack_small",
        [place, *small_parts[0], *small_parts[1]],
        [shaped((D, 128), bf16)],
        scratch=[pltpu.VMEM((1, SMALL), f32), pltpu.VMEM((72, 128), f32)],
    )
    with jax.named_scope("grad_attention0"):
        total_attn, turn_attn = grad_over_batch(place, rows, attn_pairs, extra)
    with jax.named_scope("place_layer1"):
        got_layer = gather_section(total_layer, True, turn_attn[-1:])
    mats_step, small_step = momentum(1, *both, (mats_step,), turn_attn[-1:])
    with jax.named_scope("place_layer0"):
        got_feed = gather_section(total_feed)
        got_attn = gather_section(total_attn)
    while not key_end:
        beside(())
    inputs_k, sums_k = key_end[0]
    (pooled_k,) = call(
        partial(last_kernel, LAYERS - 1),
        "last_k",
        [place, lengths, key_small, inputs_k, *sums_k],
        [pooled_out],
    )
    (input_grad,) = call(input_kernel, "input_grad", [place, carry, *sums], [own_out])

    share = SMALL // lax.axis_size("batch")
    mats_shape = (LAYERS, rows, 12 * D)
    touched = -(-(share + 127) // 128) * 128

    gathered = [*got_attn, *got_feed, *got_layer]

    def place_body(place_ref, *refs):
        sources, refs = refs[: len(gathered)], refs[len(gathered) :]
        out_ref, small_ref, buffer, vector_ref, sems, in_sems, *held = refs
        copies = [
            pltpu.make_async_copy(source, there, in_sems.at[i])
            for i, (source, there) in enumerate(zip(sources, held))
        ]
        for copy in copies:
            copy.start()
        out = Leaving(out_ref, buffer, sems)
        place_kernel(copies, place_ref, *held, out, small_ref, vector_ref)
        for copy in out.copies:
            copy.wait()

    grad_mats, grad_small = call(
        place_body,
        "place_grads",
        [place, *map(Raw, gathered)],
        [Raw(shaped(mats_shape, f32)), shaped((LAYERS, share), f32)],
        scratch=[
            pltpu.VMEM(mats_shape, f32),
            pltpu.VMEM((1, touched), f32),
            pltpu.SemaphoreType.DMA((LAYERS,)),
            pltpu.SemaphoreType.DMA((len(gathered),)),
            *(pltpu.VMEM(block.shape, bf16) for block in gathered),
        ],
        limit=58,
    )
    return (
        out_q,
        pooled_q,
        pooled_k,
        input_grad,
        grad_mats,
        grad_small,
        mats_step,
        small_step,
    )


def solution(mesh):
    in_specs = (
        P("batch", None),
        P("batch", None),
        P("batch", None),
        P("batch", None),
        P(None, "batch", None),
        P(),
        P(None, "batch", None),
        P(),
    )
    out_specs = (
        P("batch", "section"),
        P("batch", None, "section"),
        P("batch", None, "section"),
        P("batch", "section"),
        P(None, "batch", None),
        P(None, "batch"),
        P(None, "batch", None),
        P(),
    )
    return jax.shard_map(
        on_device, mesh=mesh, in_specs=in_specs, out_specs=out_specs, check_vma=False
    )
```

```python
from functools import partial

import jax
import jax.numpy as jnp
from jax import lax
from jax.experimental import pallas as pl
from jax.experimental.pallas import tpu as pltpu
from jax.sharding import PartitionSpec as P

HEADS = 12
HEAD_DIM = 64
D = 768
LAYERS = 2
MICRO = 2
ROW = 256
CROPS = 4
TOK = MICRO * ROW
SMALL = 11 * D

epsilon = 1e-05
keep_rate = 0.9995
score_scale = HEAD_DIM ** (-0.5)
bf16 = jnp.bfloat16
f32 = jnp.float32

AT_BV, AT_BO, AT_G1, AT_S1, AT_B1, AT_B2, AT_G2, AT_S2 = (
    0,
    D,
    2 * D,
    3 * D,
    4 * D,
    8 * D,
    9 * D,
    10 * D,
)


def swap_x(block):
    return lax.ppermute(block, "section", [(0, 1), (1, 0), (2, 3), (3, 2)])


def swap_y(block):
    return lax.ppermute(block, "section", [(0, 2), (2, 0), (1, 3), (3, 1)])


def swap_core(block):
    count = lax.axis_size("batch")
    return lax.ppermute(block, "batch", [(i, i ^ 1) for i in range(count)])


def shift_z(block, distance):
    count = lax.axis_size("batch")
    return lax.ppermute(block, "batch", [(i, (i + 2 * distance) % count) for i in range(count)])


def put_after(value, *others):
    return lax.optimization_barrier((value, *others))[0] if others else value


def sum_parts(name, part_0, part_1, begun=(), later=(), beside=None):
    with jax.named_scope(f"sum_{name}_first"):
        here_0, here_1 = swap_x(part_0), swap_y(put_after(part_1, *begun))
    with jax.named_scope(f"sum_{name}_second"):
        half_0, half_1 = add_parts(part_0, here_0), add_parts(part_1, here_1, later)
        sums = (half_0, swap_y(half_0), half_1, swap_x(half_1))
    return sums, () if beside is None else beside((half_0, half_1))


def sum_in_steps(name, part_0, part_1):
    with jax.named_scope(f"sum_{name}_first"):
        here_0, here_1 = swap_x(part_0), swap_y(part_1)
    after = yield (part_0,)
    with jax.named_scope(f"sum_{name}_second"):
        half_0 = add_parts(part_0, here_0, after)
        half_1 = add_parts(part_1, here_1, after)
        sums = (half_0, swap_y(half_0), half_1, swap_x(half_1))
    after = yield (half_0, half_1)
    return sums, after


def sum_own_cols(name, place, sent, kept):
    wide = kept.shape[1] // 2
    with jax.named_scope(f"sum_{name}"):
        came = swap_y(sent)
        sent, kept = call(
            half_kernel, "own_half", [place, kept, came], [shaped((TOK, wide), bf16)] * 2
        )
        return kept, swap_x(sent)


def pass_z(block, step, first=0):
    count = lax.axis_size("batch")
    last = count // 2 - 1
    sources = range(first, last) if step > 0 else range(1, last + 1 - first)
    pairs = [(2 * z + c, 2 * (z + step) + c) for z in sources for c in range(2)]
    return lax.ppermute(block, "batch", pairs)


def pass_sums(block, step, turn):
    count = lax.axis_size("batch")
    last = count // 2 - 1
    sources = range(turn) if step > 0 else range(last + 1 - turn, last + 1)
    pairs = [(2 * z + c, 2 * (z + step) + c) for z in sources for c in range(2)]
    return lax.ppermute(block, "batch", pairs)


def pass_ends(block):
    pairs = [(2 * z + c, 2 * t + c) for z, t in ((2, 3), (1, 0)) for c in range(2)]
    return lax.ppermute(block, "batch", pairs)


def gather_rows(place, block, way, then=()):
    places = lax.axis_size("batch") // 2
    apart = block.shape[0] % 16 == 0
    if places == 4 and apart and way == "line":
        left, right = pass_z(block, 1), pass_z(block, -1)
        left_2, right_2 = pass_z(left, 1, 1), pass_z(right, -1, 1)
        second = call(
            second_kernel, "second", [place, left_2, right_2], [shaped(block.shape, bf16)]
        )[0]
        own, kind = [block, left, right, second, pass_ends(second)], "line"
    else:
        found = {0: block, 1: shift_z(block, 1), places - 1: shift_z(block, places - 1)}
        for d in range(2, places - 1):
            before = (found[d - 1],) if way == "twice" else ()
            found[d] = shift_z(put_after(block, *before), d)
        own, kind = [found[d] for d in range(places)], "circle"
    other = [swap_core(put_after(chunk, *then)) for chunk in own]
    if apart:
        return own + other, kind
    me = lax.axis_index("batch")
    z, core = me // 2, me % 2
    pair = jnp.stack([jnp.stack(own), jnp.stack(other)], 1)
    pair = jnp.where(core == 0, pair, pair[:, ::-1])
    whole = jnp.take(pair, (z - jnp.arange(places)) % places, axis=0)
    return [whole.reshape(places * 2 * block.shape[0], block.shape[1])], "whole"


def near(found):
    chunks, kind = found
    return () if kind == "whole" else (chunks[1], chunks[len(chunks) // 2 - 1])


def landed(found):
    chunks, kind = found
    return () if kind == "whole" else tuple(chunks[1 : len(chunks) // 2])


def steps_of(found):
    chunks, kind = found
    return [(chunks[i],) for i in (1, 3, 4)] if kind == "line" else [(), (), ()]


def gather_section(block):
    over_x = swap_x(block)
    over_y = swap_y(put_after(block, over_x))
    return [block, over_x, over_y, swap_y(put_after(over_x, over_y))]


def dot_nn(left, right):
    return jnp.dot(left, right, preferred_element_type=f32)


def dot_nt(left, right):
    return lax.dot_general(left, right, (((1,), (1,)), ((), ())), preferred_element_type=f32)


def dot_tn(left, right):
    return lax.dot_general(left, right, (((0,), (0,)), ((), ())), preferred_element_type=f32)


def add_low(left, right):
    return (left.astype(f32) + right.astype(f32)).astype(bf16)


def ends_of(lens_ref, row):
    ends, total = [], 0
    for c in range(CROPS):
        total = total + lens_ref[row, c]
        ends.append(total)
    return ends


def segments(ends, shape, dim):
    position = lax.broadcasted_iota(jnp.int32, shape, dim)
    segment = jnp.zeros(shape, jnp.int32)
    for end in ends:
        segment = segment + (position >= end).astype(jnp.int32)
    return position, segment


def allowed_of(lens_ref, row):
    ends = ends_of(lens_ref, row)
    pos_q, seg_q = segments(ends, (ROW, 1), 0)
    pos_k, seg_k = segments(ends, (1, ROW), 1)
    seg_k = jnp.where(pos_k < ends[-1], seg_k, -1)
    return (seg_q == seg_k) | (pos_q == pos_k)


def pooled_of(lens_ref, row, values):
    ends = ends_of(lens_ref, row)
    pos, seg = segments(ends, (1, ROW), 1)
    crop = lax.broadcasted_iota(jnp.int32, (8, 1), 0)
    seg = jnp.where(pos < ends[-1], seg, -1)
    member = (seg == crop).astype(f32).astype(bf16)
    counts = jnp.ones((8, 1), f32)
    for c in range(CROPS):
        counts = jnp.where(crop == c, jnp.maximum(lens_ref[row, c], 1).astype(f32), counts)
    return (dot_nn(member, values) / counts)[:CROPS]


def standard(summed):
    centre = summed - jnp.mean(summed, axis=-1, keepdims=True)
    spread = jnp.mean(centre * centre, axis=-1, keepdims=True)
    rate = lax.rsqrt(spread + epsilon)
    return centre * rate, rate


def small_at(small_ref, layer, offset, width=D):
    return small_ref[layer : layer + 1, offset : offset + width]


def own_cols(block, section, part):
    value = block[:, :part]
    for k in range(1, block.shape[1] // part):
        value = jnp.where(section == k, block[:, k * part : (k + 1) * part], value)
    return value


def rows_of(row):
    return slice(row * ROW, (row + 1) * ROW)


def summed_row(sums, row):
    return sums[2 * row][...].astype(f32) + sums[2 * row + 1][...].astype(f32)


def norm_in(layer, gain_at, shift_at, bias_at, base_ref, sums, small_ref, row):
    branch = summed_row(sums, row) + small_at(small_ref, layer, bias_at)
    hat, rate = standard(base_ref[rows_of(row), :].astype(f32) + branch)
    out = hat * small_at(small_ref, layer, gain_at) + small_at(small_ref, layer, shift_at)
    return out.astype(bf16), hat, rate


def add_kernel(left_ref, right_ref, out_ref):
    out_ref[...] = add_low(left_ref[...], right_ref[...])


def take_kernel(units, place_ref, query_ref, key_ref, *refs):
    outs, (held, sems) = refs[: len(units)], refs[len(units) :]
    section = place_ref[0]
    part = D // SECTIONS
    first = (section * part) // 128 * 128
    at, copies = 0, []
    for out_ref, pieces in zip(outs, units):
        to = 0
        for encoder, layer, kind in pieces:
            mats_ref = query_ref if encoder == "query" else key_ref
            for j in range(4 if kind == "attention" else 2):
                if kind == "attention":
                    source, wide, got = j * D + first, 256, part
                else:
                    source, wide, got = (4 + 4 * j + section) * D, D, D
                source = mats_ref.at[layer, :, pl.ds(pl.multiple_of(source, 128), wide)]
                copy = pltpu.make_async_copy(
                    source, held.at[:, at : at + wide], sems.at[len(copies)]
                )
                copy.start()
                copies.append((copy, at, wide, out_ref, to, got))
                at, to = at + wide, to + got
    for copy, at, wide, out_ref, to, got in copies:
        copy.wait()
        block = held[:, at : at + wide]
        if wide == 256:
            block = jnp.where(section % 2 == 1, pltpu.roll(block, 192, 1), block)
        out_ref[:, to : to + got] = block[:, :got].astype(bf16)


class Columns:
    def __init__(self, ref, at):
        self.ref, self.at = ref, at

    def __getitem__(self, index):
        start, stop = index[1].start or 0, index[1].stop
        return self.ref[:, self.at + start : self.at + stop]


def second_kernel(place_ref, left_ref, right_ref, out_ref):
    right_half = place_ref[1] >= 4
    out_ref[...] = jnp.where(right_half, left_ref[...], right_ref[...])


def place_rows(kind, refs, at, place_ref, whole_ref):
    wide = whole_ref.shape[1]
    rows, count = refs[0].shape[0], len(refs) // 2
    z, core = place_ref[1] // 2, place_ref[1] % 2

    def put(i, source):
        for chunk, its in ((refs[i], core), (refs[count + i], 1 - core)):
            start = pl.multiple_of((source * 2 + its) * rows, 16)
            whole_ref[pl.ds(start, rows), :] = chunk[:, at : at + wide]

    if kind == "circle":
        for i in range(count):
            put(i, lax.rem(z + count - i, count))
        return
    put(0, z)
    put(1, jnp.where(z == 0, 3, z - 1))
    put(2, jnp.where(z == 3, 0, z + 1))
    put(3, jnp.where(z >= 2, z - 2, z + 2))

    @pl.when((z == 0) | (z == 3))
    def _():
        put(4, 3 - z)


def weights_in(kind, refs, at, place_ref, whole_ref):
    if len(refs) == 1:
        return Columns(refs[0], at)
    place_rows(kind, refs, at, place_ref, whole_ref)
    return whole_ref


def attention_kernel(layer, first, keep, kind, count, at, *refs):
    refs = list(refs)
    place_ref, lens_ref, small_ref = refs[:3]
    chunk_refs, refs = refs[3 : 3 + count], refs[3 + count :]
    base_ref, refs = refs[0], refs[1:]
    if not first:
        sums, refs = refs[:4], refs[4:]
    part_refs, outs = refs[:2], refs[2:]
    whole_ref, outs = outs[-1], outs[:-1]
    weights_ref = weights_in(kind, chunk_refs, at, place_ref, whole_ref)
    if not first:
        y_ref, outs = outs[0], outs[1:]
        if keep:
            hat_ref, rate_ref = outs[:2]
            outs = outs[2:]
    if keep:
        q_ref, k_ref, v_ref, mixed_ref, prob_ref = outs
    part = D // SECTIONS
    bv = own_cols(small_at(small_ref, layer, AT_BV), place_ref[0], part)
    lane = lax.broadcasted_iota(jnp.int32, (1, part), 1)
    for row in range(MICRO):
        here = rows_of(row)
        if first:
            inputs = base_ref[here, :]
        else:
            inputs, hat, rate = norm_in(
                layer - 1, AT_G2, AT_S2, AT_B2, base_ref, sums, small_ref, row
            )
            y_ref[here, :] = inputs
            if keep:
                hat_ref[here, :] = hat
                rate_ref[here, :] = jnp.broadcast_to(rate, (ROW, 128))
        project = dot_nn(inputs, weights_ref[:, : 3 * part])
        query = project[:, :part]
        key_rows = project[:, part : 2 * part].astype(bf16)
        values = (project[:, 2 * part :] + bv).astype(bf16)
        allowed = allowed_of(lens_ref, row)
        mixed = jnp.zeros((ROW, part), f32)
        for head in range(part // HEAD_DIM):
            inside = (lane >= head * HEAD_DIM) & (lane < (head + 1) * HEAD_DIM)
            head_q = jnp.where(inside, query, 0.0).astype(bf16)
            scores = jnp.where(allowed, dot_nt(head_q, key_rows) * score_scale, -1e30)
            terms = jnp.exp(scores - jnp.max(scores, axis=-1, keepdims=True))
            prob = terms / jnp.sum(terms, axis=-1, keepdims=True)
            if keep:
                prob_ref[row, head] = prob
            mixed = jnp.where(inside, dot_nn(prob.astype(bf16), values), mixed)
        mixed = mixed.astype(bf16)
        part_refs[row][...] = dot_nt(mixed, weights_ref[:, 3 * part : 4 * part]).astype(bf16)
        if keep:
            q_ref[here, :] = query.astype(bf16)
            k_ref[here, :] = key_rows
            v_ref[here, :] = values
            mixed_ref[here, :] = mixed


def feed_kernel(layer, keep, kind, count, at, place_ref, small_ref, base_ref, *refs):
    sums, chunk_refs, refs = refs[:4], refs[4 : 4 + count], refs[4 + count :]
    part_refs, y_ref, whole_ref = refs[:2], refs[2], refs[-1]
    weights_ref = weights_in(kind, chunk_refs, at, place_ref, whole_ref)
    if keep:
        hat_ref, rate_ref, hidden_ref, active_ref = refs[3:7]
    b1 = own_cols(small_at(small_ref, layer, AT_B1, 4 * D), place_ref[0], D)
    for row in range(MICRO):
        here = rows_of(row)
        inputs, hat, rate = norm_in(layer, AT_G1, AT_S1, AT_BO, base_ref, sums, small_ref, row)
        y_ref[here, :] = inputs
        hidden = dot_nn(inputs, weights_ref[:, :D]) + b1
        active = (0.5 * hidden * (1.0 + lax.erf(hidden * (0.5**0.5)))).astype(bf16)
        part_refs[row][...] = dot_nt(active, weights_ref[:, D : 2 * D]).astype(bf16)
        if keep:
            hat_ref[here, :] = hat
            rate_ref[here, :] = jnp.broadcast_to(rate, (ROW, 128))
            hidden_ref[here, :] = hidden
            active_ref[here, :] = active


def last_kernel(layer, place_ref, lens_ref, small_ref, base_ref, *refs):
    sums, pooled_ref = refs[:4], refs[4]
    for row in range(MICRO):
        out, hat, rate = norm_in(layer, AT_G2, AT_S2, AT_B2, base_ref, sums, small_ref, row)
        part = pooled_ref.shape[-1]
        pooled_ref[row] = own_cols(pooled_of(lens_ref, row, out), place_ref[0], part)


def norm_back(grad_out, hat, rate, gain):
    inner = grad_out * gain
    return rate * (
        inner
        - jnp.mean(inner, axis=-1, keepdims=True)
        - hat * jnp.mean(inner * hat, axis=-1, keepdims=True)
    )


def row_sum(block):
    return jnp.sum(block, axis=0, keepdims=True)


def arrived_grad(base_ref, sums, row):
    return (base_ref[rows_of(row), :] + summed_row(sums, row)).astype(bf16)


def feed_back_kernel(layer, last, place_ref, small_ref, weights_ref, hidden_ref, base_ref, *refs):
    sums, refs = refs[:4], refs[4:]
    if last:
        cot_ref, lens_ref = refs[:2]
    else:
        hat_ref, rate_ref = refs[:2]
    part_refs = refs[2:4]
    carry_ref, branch_ref, grad_hidden_ref, sums_ref, bias_ref = refs[4:9]
    if last:
        y_ref, pooled_ref = refs[9:]
    gain = small_at(small_ref, layer, AT_G2)
    totals = [jnp.zeros((1, D), f32) for _ in range(4)]
    for row in range(MICRO):
        here = rows_of(row)
        if last:
            out, hat, rate = norm_in(layer, AT_G2, AT_S2, AT_B2, base_ref, sums, small_ref, row)
            part = y_ref.shape[0]
            y_ref[:, here] = own_cols(out.astype(f32), place_ref[0], part).T.astype(bf16)
            pooled_ref[row] = own_cols(pooled_of(lens_ref, row, out), place_ref[0], part)
            grad_out = cot_ref[here, :].astype(f32)
        else:
            hat, rate = hat_ref[here, :], rate_ref[here, :1]
            grad_out = arrived_grad(base_ref, sums, row).astype(f32)
        grad = norm_back(grad_out, hat, rate, gain)
        carry_ref[here, :] = grad
        branch = grad.astype(bf16)
        branch_ref[here, :] = branch
        grad_active = dot_nn(branch, weights_ref[:, D : 2 * D])
        hidden = hidden_ref[here, :]
        slope = 0.5 * (1.0 + lax.erf(hidden * (0.5**0.5))) + hidden * (
            jnp.exp(-0.5 * hidden * hidden) * 0.3989422804014327
        )
        grad_hidden = (grad_active * slope).astype(bf16)
        grad_hidden_ref[here, :] = grad_hidden
        part_refs[row][...] = dot_nt(grad_hidden, weights_ref[:, :D]).astype(bf16)
        totals[0] += row_sum(branch.astype(f32))
        totals[1] += row_sum(grad_out * hat)
        totals[2] += row_sum(grad_out)
        totals[3] += row_sum(grad_hidden.astype(f32))
    for i in range(3):
        sums_ref[i : i + 1, :] = totals[i]
    bias_ref[...] = totals[3]


def attention_back_kernel(layer, small_ref, place_ref, weights_ref, base_ref, *refs):
    sums, hat_ref, rate_ref = refs[:4], refs[4], refs[5]
    q_ref, k_ref, v_ref, prob_ref = refs[6:10]
    refs = refs[10:]
    part_refs = refs[:2]
    carry_ref, branch_ref, grad_proj_ref, sums_ref, bias_ref = refs[2:]
    part = q_ref.shape[1]
    lane = lax.broadcasted_iota(jnp.int32, (1, part), 1)
    gain = small_at(small_ref, layer, AT_G1)
    totals = [jnp.zeros((1, D), f32) for _ in range(3)] + [jnp.zeros((1, part), f32)]
    for row in range(MICRO):
        here = rows_of(row)
        hat, rate = hat_ref[here, :], rate_ref[here, :1]
        grad_out = arrived_grad(base_ref, sums, row).astype(f32)
        grad = norm_back(grad_out, hat, rate, gain)
        carry_ref[here, :] = grad
        branch = grad.astype(bf16)
        branch_ref[here, :] = branch
        grad_mixed = dot_nn(branch, weights_ref[:, 3 * part : 4 * part])
        low_mixed = grad_mixed.astype(bf16)
        query, key_rows, values = q_ref[here, :], k_ref[here, :], v_ref[here, :]
        grads = [jnp.zeros((ROW, part), f32) for _ in range(3)]
        for head in range(part // HEAD_DIM):
            inside = (lane >= head * HEAD_DIM) & (lane < (head + 1) * HEAD_DIM)
            prob = prob_ref[row, head]
            head_mixed = jnp.where(inside, grad_mixed, 0.0).astype(bf16)
            grad_prob = dot_nt(head_mixed, values)
            grad_scores = prob * (
                grad_prob - jnp.sum(grad_prob * prob, axis=-1, keepdims=True)
            )
            grad_scores = grad_scores.astype(bf16)
            grad_q = dot_nn(grad_scores, key_rows) * score_scale
            grad_k = dot_tn(grad_scores, query) * score_scale
            grad_v = dot_tn(prob.astype(bf16), low_mixed)
            grads = [
                jnp.where(inside, new, old) for new, old in zip((grad_q, grad_k, grad_v), grads)
            ]
        grad_proj = jnp.concatenate(grads, axis=1).astype(bf16)
        grad_proj_ref[here, :] = grad_proj
        parted = dot_nt(grad_proj, weights_ref[:, : 3 * part]).astype(bf16)
        if layer > 0:
            part_refs[row][...] = parted
        else:
            half, upper = D // 2, place_ref[0] >= 2
            part_refs[0][here, :] = jnp.where(upper, parted[:, :half], parted[:, half:])
            part_refs[1][here, :] = jnp.where(upper, parted[:, half:], parted[:, :half])
        totals[0] += row_sum(branch.astype(f32))
        totals[1] += row_sum(grad_out * hat)
        totals[2] += row_sum(grad_out)
        totals[3] += row_sum(grads[2].astype(bf16).astype(f32))
    for i in range(3):
        sums_ref[i : i + 1, :] = totals[i]
    bias_ref[...] = totals[3]


def half_kernel(place_ref, kept_ref, came_ref, sent_out, kept_out):
    total = add_low(kept_ref[...], came_ref[...])
    wide = kept_out.shape[1]
    odd = place_ref[0] % 2 == 1
    kept_out[...] = jnp.where(odd, total[:, wide:], total[:, :wide])
    sent_out[...] = jnp.where(odd, total[:, :wide], total[:, wide:])


def input_kernel(place_ref, base_ref, kept_ref, came_ref, out_ref):
    base = own_cols(base_ref[...], place_ref[0], out_ref.shape[0])
    total = kept_ref[...].astype(f32) + came_ref[...].astype(f32)
    out_ref[...] = (base + total).T.astype(bf16)


def pack_kernel(rows, place_ref, *refs):
    ins, (out_ref, vector_ref, piece_ref) = refs[: 4 * LAYERS], refs[4 * LAYERS :]
    section = place_ref[0]
    own = section == 0
    slot = rows // LAYERS
    share = SMALL // (D // rows)
    out_ref[...] = jnp.zeros(out_ref.shape, bf16)
    piece_ref[...] = jnp.zeros(piece_ref.shape, f32)
    for layer in range(LAYERS):
        norm_1, value_bias, norm_2, hidden_bias = ins[4 * layer : 4 * layer + 4]
        part = value_bias.shape[1]
        for k in range(SECTIONS):
            mine = section == k
            vector_ref[:, k * part : (k + 1) * part] = jnp.where(mine, value_bias[...], 0.0)
            at = AT_B1 + k * D
            vector_ref[:, at : at + D] = jnp.where(mine, hidden_bias[...], 0.0)
        for i in range(3):
            vector_ref[:, AT_BO + i * D : AT_BO + (i + 1) * D] = jnp.where(
                own, norm_1[i : i + 1, :], 0.0
            )
            vector_ref[:, AT_B2 + i * D : AT_B2 + (i + 1) * D] = jnp.where(
                own, norm_2[i : i + 1, :], 0.0
            )
        for i in range(SMALL // 128):
            piece_ref[i : i + 1, :] = vector_ref[:, i * 128 : (i + 1) * 128]
        for b in range(D // rows):
            first = b * share // 128
            last = (b * share + share - 1) // 128 + 1
            start = b * rows + layer * slot
            out_ref[start : start + last - first, :] = piece_ref[first:last, :].astype(bf16)


def grad_kernel(rows, count, place_ref, *refs):
    mine_ref, other_ref, whole_ref = refs[-3:]
    at = 0
    for left_ref, right_ref in zip(refs[: 2 * count : 2], refs[1 : 2 * count : 2]):
        wide = right_ref.shape[1]
        whole_ref[:, at : at + wide] = dot_tn(left_ref[...], right_ref[...]).astype(bf16)
        at += wide
    if at < whole_ref.shape[1]:
        whole_ref[:, at:] = refs[2 * count][...]
    core = place_ref[1] % 2
    for out, owner in ((other_ref, 1 - core), (mine_ref, core)):
        for z in range(mine_ref.shape[0]):
            start = pl.multiple_of((2 * z + owner) * rows, 16)
            out[z] = whole_ref[pl.ds(start, rows), :]


def line_kernel(turn, place_ref, mine_ref, came_ref, *refs):
    places = mine_ref.shape[0]
    z = place_ref[1] // 2

    def rows_for(chip):
        return mine_ref[chip].astype(f32) + came_ref[chip].astype(f32)

    outs = refs if turn == 1 else refs[2:]
    right = rows_for(jnp.minimum(z + places - turn, places - 1))
    left = rows_for(jnp.maximum(z - places + turn, 0))
    if turn > 1:
        right, left = right + refs[0][...].astype(f32), left + refs[1][...].astype(f32)
    outs[0][...], outs[1][...] = right.astype(bf16), left.astype(bf16)
    if turn == places - 1:
        outs[2][...] = rows_for(z).astype(bf16)


def total_kernel(counts, *refs):
    out_ref, at = refs[-1], 0
    for count in counts:
        total = refs[0][...].astype(f32)
        for ref in refs[1:count]:
            total = total + ref[...].astype(f32)
        refs = refs[count:]
        out_ref[:, at : at + total.shape[1]] = total.astype(bf16)
        at += total.shape[1]


def place_kernel(layer, count, attn_at, feed_at, place_ref, *refs):
    blocks, refs = refs[:SECTIONS], refs[SECTIONS:]
    out_ref, buffer, sems = refs[count:]
    section = place_ref[0]
    part = D // SECTIONS

    def owned(group, start, stop):
        found = []
        for slot in range(SECTIONS):
            value = group[0][:, start:stop]
            for k in range(1, SECTIONS):
                value = jnp.where(section ^ slot == k, group[k][:, start:stop], value)
            found.append(value.astype(f32))
        return found

    copies = []

    def push(start, stop):
        there = out_ref.at[layer, :, start:stop]
        copies.append(pltpu.make_async_copy(buffer.at[:, start:stop], there, sems.at[len(copies)]))
        copies[-1].start()

    ffn = owned(blocks, feed_at, feed_at + 2 * D)
    for j in range(2):
        for slot, block in enumerate(ffn):
            start = (4 + 4 * j + slot) * D
            buffer[:, start : start + D] = block[:, j * D : (j + 1) * D]
        push((4 + 4 * j) * D, (8 + 4 * j) * D)
    attn = owned(blocks, attn_at, attn_at + D)
    for j in range(4):
        columns = [a[:, j * part : (j + 1) * part] for a in attn]
        buffer[:, j * D : (j + 1) * D] = jnp.concatenate(columns, axis=1)
    push(0, 4 * D)
    for copy in copies:
        copy.wait()


def small_kernel(place_ref, *refs):
    blocks, (small_ref, vector_ref) = refs[:SECTIONS], refs[SECTIONS:]
    rows, share = blocks[0].shape[0], small_ref.shape[1]
    for layer in range(LAYERS):
        slot = rows // LAYERS
        at, count = layer * slot, min(16, slot)
        total = jnp.zeros((count, 128), f32)
        for block in blocks:
            total = total + block[at : at + count, 3 * D :].astype(f32)
        wide = vector_ref.shape[1]
        for i in range(wide // 128):
            vector_ref[:, i * 128 : (i + 1) * 128] = total[i : i + 1, :]
        inside = lax.rem(place_ref[1] * share, 128)
        moved = pltpu.roll(jnp.broadcast_to(vector_ref[...], (8, wide)), wide - inside, 1)
        small_ref[layer : layer + 1, :] = moved[:1, :share]


def momentum_kernel(layer, query_ref, key_ref, query_small, key_small, *refs):
    out_ref, small_out, q_buf, k_buf, out_buf, in_sems, out_sems = refs[-7:]
    rows = query_ref.shape[1]
    depth, step = q_buf.shape[0], q_buf.shape[1]
    blocks = [(layer, pl.ds(j, step)) for j in range(0, rows, step)]

    def fetch(n):
        i, j = blocks[n]
        pair = [
            pltpu.make_async_copy(ref.at[i, j], buf.at[n % depth], in_sems.at[m, n % depth])
            for m, (ref, buf) in enumerate(((query_ref, q_buf), (key_ref, k_buf)))
        ]
        for copy in pair:
            copy.start()
        return pair

    small_out[...] = (query_small[...] - key_small[...]) * (1.0 - keep_rate)
    coming = [fetch(n) for n in range(min(depth, len(blocks)))]
    leaving = []
    for n, (i, j) in enumerate(blocks):
        for copy in coming[n]:
            copy.wait()
        if n >= depth:
            leaving[n - depth].wait()
        at = n % depth
        out_buf[at] = (q_buf[at] - k_buf[at]) * (1.0 - keep_rate)
        leaving.append(pltpu.make_async_copy(out_buf.at[at], out_ref.at[i, j], out_sems.at[at]))
        leaving[-1].start()
        if n + depth < len(blocks):
            coming.append(fetch(n + depth))
    for copy in leaving[-depth:]:
        copy.wait()


VMEM = pl.BlockSpec(memory_space=pltpu.VMEM)
SMEM = pl.BlockSpec(memory_space=pltpu.SMEM)
ANY = pl.BlockSpec(memory_space=pl.ANY)
SECTIONS = 4


def shaped(shape, kind):
    return jax.ShapeDtypeStruct(shape, kind)


class Raw:
    def __init__(self, value):
        self.value = value


def call(body, name, operands, outs, after=(), scratch=(), limit=12, aliases=None):
    arrays = [a.value if isinstance(a, Raw) else a for a in operands]
    results = [a.value if isinstance(a, Raw) else a for a in outs]
    specs = []
    for given, array in zip(operands, arrays):
        specs.append(ANY if isinstance(given, Raw) else SMEM if array.dtype == jnp.int32 else VMEM)
    count, skipped = len(operands), len(after)

    def kernel(*refs):
        body(*refs[:count], *refs[count + skipped :])

    return pl.pallas_call(
        kernel,
        name=name,
        in_specs=specs + [ANY] * len(after),
        out_specs=[ANY if isinstance(a, Raw) else VMEM for a in outs],
        out_shape=results,
        scratch_shapes=list(scratch),
        input_output_aliases=aliases or {},
        cost_estimate=pl.CostEstimate(flops=1, bytes_accessed=1, transcendentals=0),
        compiler_params=pltpu.CompilerParams(vmem_limit_bytes=limit * 2**20),
    )(*arrays, *after)


part_out = [shaped((ROW, D), bf16)] * 2
rows_out = shaped((TOK, D), bf16)
wide_out = shaped((TOK, D), f32)
rate_out = shaped((TOK, 128), f32)


def add_parts(left, right, after=()):
    return call(add_kernel, "add_parts", [left, right], [shaped(left.shape, bf16)], after)[0]


def momentum(layer, query, key, query_small, key_small, into, after):
    depth, step = 3, 24
    block = (depth, step, query.shape[2])
    return call(
        partial(momentum_kernel, layer),
        f"momentum{layer}",
        [Raw(query), Raw(key), query_small, key_small] + [Raw(a) for a in into],
        [Raw(shaped(query.shape, f32)), shaped(query_small.shape, f32)],
        after,
        [pltpu.VMEM(block, f32)] * 3
        + [pltpu.SemaphoreType.DMA((2, depth)), pltpu.SemaphoreType.DMA((depth,))],
        58,
        {4: 0} if into else {},
    )


def take(place, query_mats, key_mats, units, after=()):
    rows = query_mats.shape[1]
    kinds = [[kind for _, _, kind in pieces] for pieces in units]
    cols = [sum(D if kind == "attention" else 2 * D for kind in found) for found in kinds]
    held = sum(4 * 256 if kind == "attention" else 2 * D for found in kinds for kind in found)
    count = sum(4 if kind == "attention" else 2 for found in kinds for kind in found)
    return call(
        partial(take_kernel, units),
        "take",
        [place, Raw(query_mats), Raw(key_mats)],
        [shaped((rows, c), bf16) for c in cols],
        after,
        [pltpu.VMEM((rows, held), f32), pltpu.SemaphoreType.DMA((count,))],
        limit=58,
    )


def attention(layer, inputs, sums, shared, weights, keep, tag, after=()):
    (chunks, kind), at = weights
    part = D // SECTIONS
    operands = [*shared, *chunks, inputs] + ([] if sums is None else list(sums))
    outs = list(part_out)
    if sums is not None:
        outs += [rows_out] + ([wide_out, rate_out] if keep else [])
    if keep:
        outs += [shaped((TOK, part), bf16)] * 4
        outs += [shaped((MICRO, part // HEAD_DIM, ROW, ROW), f32)]
    shape = (D, 4 * part)
    return call(
        partial(attention_kernel, layer, sums is None, keep, kind, len(chunks), at),
        f"attention_{tag}{layer}",
        operands,
        outs + ([shaped(shape, bf16)] if keep else []),
        after,
        [] if keep else [pltpu.VMEM(shape, bf16)],
    )


def feed(layer, inputs, sums, shared, weights, keep, tag, after=()):
    (chunks, kind), at = weights
    place, lengths, small = shared
    shape = (D, 2 * D)
    outs = [*part_out, rows_out]
    outs += [wide_out, rate_out, wide_out, rows_out, shaped(shape, bf16)] if keep else []
    return call(
        partial(feed_kernel, layer, keep, kind, len(chunks), at),
        f"feed_{tag}{layer}",
        [place, small, inputs, *sums, *chunks],
        outs,
        after,
        [] if keep else [pltpu.VMEM(shape, bf16)],
    )


def grad_over_batch(place, rows, pairs, extra=None, begin=()):
    places = lax.axis_size("batch") // 2
    wide = sum(right.shape[1] for _, right in pairs)
    cols = wide + (0 if extra is None else extra.shape[1])
    chunk = shaped((rows, cols), bf16)
    if places == 4 and rows % 16 == 0:
        mine, other = call(
            partial(grad_kernel, rows, len(pairs)),
            "grad",
            [place, *(x for pair in pairs for x in pair)] + ([] if extra is None else [extra]),
            [shaped((places, rows, cols), bf16)] * 2,
            begin,
            [pltpu.VMEM((D, cols), bf16)],
        )
        came, arrived, shown = swap_core(other), (), []
        for turn in range(1, places):
            sent = call(
                partial(line_kernel, turn),
                "line_sums",
                [place, mine, came, *arrived],
                [chunk] * (3 if turn == places - 1 else 2),
            )
            arrived = (pass_sums(sent[0], 1, turn), pass_sums(sent[1], -1, turn))
            shown.append(arrived)
        return [sent[2], *arrived], (*shown, (sent[0],))
    me = lax.axis_index("batch")
    z, core = me // 2, me % 2
    block = jnp.concatenate([dot_tn(l, r).astype(bf16) for l, r in pairs], axis=1)
    if extra is not None:
        block = jnp.concatenate([block, extra], axis=1)
    parted = block.reshape(places, 2, rows, cols)
    mine = lax.dynamic_index_in_dim(parted, core, 1, keepdims=False)
    other = lax.dynamic_index_in_dim(parted, 1 - core, 1, keepdims=False)
    chip = add_low(mine, swap_core(other))
    chunks = [
        lax.dynamic_index_in_dim(chip, (z + d) % places, 0, keepdims=False) for d in range(places)
    ]
    came = [shift_z(chunks[d], d) for d in range(1, places)]
    return [chunks[0], *came], [()] * 4


def total_of(groups, after=()):
    rows = groups[0][0].shape[0]
    cols = sum(group[0].shape[1] for group in groups)
    return call(
        partial(total_kernel, [len(group) for group in groups]),
        "total",
        [block for group in groups for block in group],
        [shaped((rows, cols), bf16)],
        after,
    )[0]


def on_device(tokens, key_tokens, cotangent, lengths, query_mats, query_small, key_mats, key_small):
    section, batch = lax.axis_index("section"), lax.axis_index("batch")
    part = D // SECTIONS
    rows = query_mats.shape[1]
    place = jnp.stack([section, batch]).astype(jnp.int32)
    shared_q, shared_k = (place, lengths, query_small), (place, lengths, key_small)
    own_turned = shaped((part, TOK), bf16)
    pooled_out = shaped((MICRO, CROPS, part), f32)

    units = [
        [("query", 0, "attention")],
        [("query", 0, "feed")],
        [("query", 1, "attention")],
        [("query", 1, "feed")],
        [("key", 0, "attention"), ("key", 0, "feed")],
        [("key", 1, "attention"), ("key", 1, "feed")],
    ]
    blocks = take(place, query_mats, key_mats, units[:1])
    blocks += take(place, query_mats, key_mats, units[1:], (blocks[0],))
    both = (query_mats, key_mats, query_small, key_small)
    mats_step, early_step = momentum(0, *both, (), (blocks[1],))

    def unit(n, way, *after):
        with jax.named_scope(f"weights_unit_{n}"):
            then = (early_step,) if n == 0 else ()
            return gather_rows(place, put_after(blocks[n], *after), way, then)

    chunks = [unit(0, "once")]
    chunks.append(unit(1, "twice", *landed(chunks[0]), early_step))
    for n in range(2, 4):
        chunks.append(unit(n, "twice", *near(chunks[-1])))
    for n in range(4, 6):
        chunks.append(unit(n, "line", *landed(chunks[-1])[-1:]))
    lines = [steps_of(found) for found in chunks[4:]]
    attn_q, feed_q = [(chunks[0], 0), (chunks[2], 0)], [(chunks[1], 0), (chunks[3], 0)]

    kept, weights = [], []
    inputs, sums = tokens, None
    for layer in range(LAYERS):
        found = attention(layer, inputs, sums, shared_q, attn_q[layer], True, "q")
        parts, found, attn_w = found[:2], found[2:-1], found[-1]
        if layer > 0:
            inputs, hat, rate = found[:3]
            kept[-1] += (hat, rate)
            found = found[3:]
        sums, _ = sum_parts(f"q{2 * layer}", *parts)
        attn_in, attn_kept = inputs, tuple(found)
        p0, p1, inputs, hat, rate, hidden, active, feed_w = feed(
            layer, inputs, sums, shared_q, feed_q[layer], True, "q"
        )
        gates = ((), lines[0][0]) if layer > 0 else ()
        sums, _ = sum_parts(f"q{2 * layer + 1}", p0, p1, *gates)
        if chunks[0][1] == "whole":
            attn_w, feed_w = attn_q[layer][0][0][0], feed_q[layer][0][0][0]
        weights.append((attn_w, feed_w))
        kept.append((attn_in, attn_kept, hat, rate, inputs, hidden, active))

    attn_k, feed_k = [(chunks[4], 0), (chunks[5], 0)], [(chunks[4], D), (chunks[5], D)]

    def key_attention(layer, inputs, sums, after):
        return attention(layer, inputs, sums, shared_k, attn_k[layer], False, "k", after)

    def key_feed(layer, inputs, sums, after):
        return feed(layer, inputs, sums, shared_k, feed_k[layer], False, "k", after)

    def key_steps():
        after = yield
        sums, after = yield from sum_in_steps("k0", *key_attention(0, key_tokens, None, after))
        found.append(key_feed(0, key_tokens, sums, after))
        yield found[0][:1]

    found, steps = [], key_steps()
    next(steps)
    small_parts = [None] * LAYERS
    sums_out, turn, done = shaped((3, D), f32), [()] * 4, ()
    for layer in reversed(range(LAYERS)):
        attn_in, attn_kept, hat1, rate1, feed_in, hidden, active, *rest = kept[layer]
        attn_w, feed_w = weights[layer]
        last = layer == LAYERS - 1
        operands = [feed_in, *sums, cotangent, lengths] if last else [carry, *sums, *rest]
        outs = [*part_out, wide_out, rows_out, rows_out, sums_out, shaped((1, D), f32)]
        if last:
            outs += [own_turned, pooled_out]
        p0, p1, carry, branch, grad_hidden, sums_2, db1, *tail = call(
            partial(feed_back_kernel, layer, last),
            f"feed_back{layer}",
            [place, query_small, feed_w, hidden, *operands],
            outs,
            done,
        )
        if last:
            out_q, pooled_q = tail
        gates = (lines[0][1], lines[0][2]) if last else (lines[1][2], turn[0])
        sums, done = sum_parts(f"back{2 * layer + 1}", p0, p1, *gates, steps.send)
        feed_pairs = [(feed_in, grad_hidden), (branch, active)]
        q, k, v, mixed, prob = attn_kept
        p0, p1, carry, branch, grad_proj, sums_1, dbv = call(
            partial(attention_back_kernel, layer),
            f"attention_back{layer}",
            [query_small, place, attn_w, carry, *sums, hat1, rate1, q, k, v, prob],
            [
                *(part_out if last else [shaped((TOK, D // 2), bf16)] * 2),
                wide_out,
                rows_out,
                shaped((TOK, 3 * part), bf16),
                sums_out,
                shaped((1, part), f32),
            ],
            (*done, *turn[1]),
        )
        small_parts[layer] = [sums_1, dbv, sums_2, db1]
        attn_pairs = [(attn_in, grad_proj), (branch, mixed)]
        if last:
            sums, done = sum_parts(f"back{2 * layer}", p0, p1, *lines[1][:2], steps.send)
            with jax.named_scope("grad_layer1"):
                layer_sums, turn = grad_over_batch(
                    place, rows, attn_pairs + feed_pairs, None, sums[::2]
                )
        else:
            sums = sum_own_cols("back0", place, p0, p1)
    (extra,) = call(
        partial(pack_kernel, rows),
        "pack_small",
        [place, *small_parts[0], *small_parts[1]],
        [shaped((D, 128), bf16)],
        scratch=[pltpu.VMEM((1, SMALL), f32), pltpu.VMEM((72, 128), f32)],
    )
    with jax.named_scope("grad_layer0"):
        sums_0, turn_0 = grad_over_batch(place, rows, feed_pairs + attn_pairs, extra)
    with jax.named_scope("place_layer1"):
        got_1 = gather_section(total_of([layer_sums]))

    k0, k1, inputs_k = found[0]
    mats_step, small_step = momentum(1, *both, (mats_step,), (p0,))
    sums_k, _ = sum_parts("k1", k0, k1, (), (*turn[2], *turn_0[3]))
    k0, k1, inputs_k = key_attention(1, inputs_k, sums_k, (*turn_0[0], got_1[1], sums[0]))
    sums_k, _ = sum_parts("k2", k0, k1, (), (*turn_0[1], got_1[2]))
    (input_grad,) = call(input_kernel, "input_grad", [place, carry, *sums], [own_turned])
    k0, k1, inputs_k = key_feed(1, inputs_k, sums_k, (*turn_0[2], got_1[3], input_grad))
    with jax.named_scope("place_layer0"):
        got_0 = gather_section(total_of([sums_0]))
    sums_k, _ = sum_parts("k3", k0, k1)
    (pooled_k,) = call(
        partial(last_kernel, LAYERS - 1),
        "last_k",
        [place, lengths, key_small, inputs_k, *sums_k],
        [pooled_out],
    )
    share = SMALL // lax.axis_size("batch")
    mats_shape = (LAYERS, rows, 12 * D)
    touched = -(-(share + 127) // 128) * 128

    grad_mats = ()
    for layer, blocks in ((1, got_1), (0, got_0)):
        attn_at, feed_at = (0, D) if layer > 0 else (2 * D, 0)
        grad_mats = call(
            partial(place_kernel, layer, len(grad_mats), attn_at, feed_at),
            f"place_grads{layer}",
            [place, *blocks, *map(Raw, grad_mats)],
            [Raw(shaped(mats_shape, f32))],
            scratch=[pltpu.VMEM((rows, 12 * D), f32), pltpu.SemaphoreType.DMA((3,))],
            aliases={1 + len(blocks): 0} if grad_mats else {},
        )
    (grad_mats,) = grad_mats
    (grad_small,) = call(
        small_kernel,
        "own_small",
        [place, *got_0],
        [shaped((LAYERS, share), f32)],
        scratch=[pltpu.VMEM((1, touched), f32)],
    )
    return (
        out_q.T,
        pooled_q,
        pooled_k,
        input_grad.T,
        grad_mats,
        grad_small,
        mats_step,
        small_step,
    )


def solution(mesh):
    in_specs = (
        P("batch", None),
        P("batch", None),
        P("batch", None),
        P("batch", None),
        P(None, "batch", None),
        P(),
        P(None, "batch", None),
        P(),
    )
    out_specs = (
        P("batch", "section"),
        P("batch", None, "section"),
        P("batch", None, "section"),
        P("batch", "section"),
        P(None, "batch", None),
        P(None, "batch"),
        P(None, "batch", None),
        P(),
    )
    return jax.shard_map(
        on_device, mesh=mesh, in_specs=in_specs, out_specs=out_specs, check_vma=False
    )
```

```python
from functools import partial

import jax
import jax.numpy as jnp
from jax import lax
from jax.experimental import pallas as pl
from jax.experimental.pallas import tpu as pltpu
from jax.sharding import PartitionSpec as P

HEADS = 12
HEAD_DIM = 64
D = 768
LAYERS = 2
MICRO = 2
ROW = 256
CROPS = 4
TOK = MICRO * ROW
SMALL = 11 * D

epsilon = 1e-05
keep_rate = 0.9995
score_scale = HEAD_DIM ** (-0.5)
bf16 = jnp.bfloat16
f32 = jnp.float32

AT_BV, AT_BO, AT_G1, AT_S1, AT_B1, AT_B2, AT_G2, AT_S2 = (
    0,
    D,
    2 * D,
    3 * D,
    4 * D,
    8 * D,
    9 * D,
    10 * D,
)


def swap_x(block):
    return lax.ppermute(block, "section", [(0, 1), (1, 0), (2, 3), (3, 2)])


def swap_y(block):
    return lax.ppermute(block, "section", [(0, 2), (2, 0), (1, 3), (3, 1)])


def swap_core(block):
    count = lax.axis_size("batch")
    return lax.ppermute(block, "batch", [(i, i ^ 1) for i in range(count)])


def shift_z(block, distance):
    count = lax.axis_size("batch")
    return lax.ppermute(block, "batch", [(i, (i + 2 * distance) % count) for i in range(count)])


def put_after(value, *others):
    return lax.optimization_barrier((value, *others))[0] if others else value


def sum_parts(name, part_0, part_1, begun=(), later=(), beside=None):
    with jax.named_scope(f"sum_{name}_first"):
        here_0, here_1 = swap_x(part_0), swap_y(put_after(part_1, *begun))
    with jax.named_scope(f"sum_{name}_second"):
        half_0, half_1 = add_parts(part_0, here_0), add_parts(part_1, here_1, later)
        sums = (half_0, swap_y(half_0), half_1, swap_x(half_1))
    return sums, () if beside is None else beside((half_0, half_1))


def sum_in_steps(name, part_0, part_1):
    with jax.named_scope(f"sum_{name}_first"):
        here_0, here_1 = swap_x(part_0), swap_y(part_1)
    after = yield (part_0,)
    with jax.named_scope(f"sum_{name}_second"):
        half_0 = add_parts(part_0, here_0, after)
        half_1 = add_parts(part_1, here_1, after)
        sums = (half_0, swap_y(half_0), half_1, swap_x(half_1))
    after = yield (half_0, half_1)
    return sums, after


def sum_own_cols(name, place, sent, kept):
    wide = kept.shape[1] // 2
    with jax.named_scope(f"sum_{name}"):
        came = swap_y(sent)
        sent, kept = call(
            half_kernel, "own_half", [place, kept, came], [shaped((TOK, wide), bf16)] * 2
        )
        return kept, swap_x(sent)


def pass_z(block, step, first=0):
    count = lax.axis_size("batch")
    last = count // 2 - 1
    sources = range(first, last) if step > 0 else range(1, last + 1 - first)
    pairs = [(2 * z + c, 2 * (z + step) + c) for z in sources for c in range(2)]
    return lax.ppermute(block, "batch", pairs)


def pass_sums(block, step, turn):
    count = lax.axis_size("batch")
    last = count // 2 - 1
    sources = range(turn) if step > 0 else range(last + 1 - turn, last + 1)
    pairs = [(2 * z + c, 2 * (z + step) + c) for z in sources for c in range(2)]
    return lax.ppermute(block, "batch", pairs)


def pass_ends(block):
    pairs = [(2 * z + c, 2 * t + c) for z, t in ((2, 3), (1, 0)) for c in range(2)]
    return lax.ppermute(block, "batch", pairs)


def gather_rows(place, block, way, then=()):
    places = lax.axis_size("batch") // 2
    apart = block.shape[0] % 16 == 0
    if places == 4 and apart and way == "line":
        left, right = pass_z(block, 1), pass_z(block, -1)
        left_2, right_2 = pass_z(left, 1, 1), pass_z(right, -1, 1)
        second = call(
            second_kernel, "second", [place, left_2, right_2], [shaped(block.shape, bf16)]
        )[0]
        own, kind = [block, left, right, second, pass_ends(second)], "line"
    else:
        found = {0: block, 1: shift_z(block, 1), places - 1: shift_z(block, places - 1)}
        for d in range(2, places - 1):
            before = (found[d - 1],) if way == "twice" else ()
            found[d] = shift_z(put_after(block, *before), d)
        own, kind = [found[d] for d in range(places)], "circle"
    other = [swap_core(put_after(chunk, *then)) for chunk in own]
    if apart:
        return own + other, kind
    me = lax.axis_index("batch")
    z, core = me // 2, me % 2
    pair = jnp.stack([jnp.stack(own), jnp.stack(other)], 1)
    pair = jnp.where(core == 0, pair, pair[:, ::-1])
    whole = jnp.take(pair, (z - jnp.arange(places)) % places, axis=0)
    return [whole.reshape(places * 2 * block.shape[0], block.shape[1])], "whole"


def near(found):
    chunks, kind = found
    return () if kind == "whole" else (chunks[1], chunks[len(chunks) // 2 - 1])


def landed(found):
    chunks, kind = found
    return () if kind == "whole" else tuple(chunks[1 : len(chunks) // 2])


def steps_of(found):
    chunks, kind = found
    return [(chunks[i],) for i in (1, 3, 4)] if kind == "line" else [(), (), ()]


def gather_section(block):
    over_x = swap_x(block)
    over_y = swap_y(put_after(block, over_x))
    return [block, over_x, over_y, swap_y(put_after(over_x, over_y))]


def dot_nn(left, right):
    return jnp.dot(left, right, preferred_element_type=f32)


def dot_nt(left, right):
    return lax.dot_general(left, right, (((1,), (1,)), ((), ())), preferred_element_type=f32)


def dot_tn(left, right):
    return lax.dot_general(left, right, (((0,), (0,)), ((), ())), preferred_element_type=f32)


def add_low(left, right):
    return (left.astype(f32) + right.astype(f32)).astype(bf16)


def ends_of(lens_ref, row):
    ends, total = [], 0
    for c in range(CROPS):
        total = total + lens_ref[row, c]
        ends.append(total)
    return ends


def segments(ends, shape, dim):
    position = lax.broadcasted_iota(jnp.int32, shape, dim)
    segment = jnp.zeros(shape, jnp.int32)
    for end in ends:
        segment = segment + (position >= end).astype(jnp.int32)
    return position, segment


def allowed_of(lens_ref, row):
    ends = ends_of(lens_ref, row)
    pos_q, seg_q = segments(ends, (ROW, 1), 0)
    pos_k, seg_k = segments(ends, (1, ROW), 1)
    seg_k = jnp.where(pos_k < ends[-1], seg_k, -1)
    return (seg_q == seg_k) | (pos_q == pos_k)


def pooled_of(lens_ref, row, values):
    ends = ends_of(lens_ref, row)
    pos, seg = segments(ends, (1, ROW), 1)
    crop = lax.broadcasted_iota(jnp.int32, (8, 1), 0)
    seg = jnp.where(pos < ends[-1], seg, -1)
    member = (seg == crop).astype(f32).astype(bf16)
    counts = jnp.ones((8, 1), f32)
    for c in range(CROPS):
        counts = jnp.where(crop == c, jnp.maximum(lens_ref[row, c], 1).astype(f32), counts)
    return (dot_nn(member, values) / counts)[:CROPS]


def standard(summed):
    centre = summed - jnp.mean(summed, axis=-1, keepdims=True)
    spread = jnp.mean(centre * centre, axis=-1, keepdims=True)
    rate = lax.rsqrt(spread + epsilon)
    return centre * rate, rate


def small_at(small_ref, layer, offset, width=D):
    return small_ref[layer : layer + 1, offset : offset + width]


def own_cols(block, section, part):
    value = block[:, :part]
    for k in range(1, block.shape[1] // part):
        value = jnp.where(section == k, block[:, k * part : (k + 1) * part], value)
    return value


def rows_of(row):
    return slice(row * ROW, (row + 1) * ROW)


def summed_row(sums, row):
    return sums[2 * row][...].astype(f32) + sums[2 * row + 1][...].astype(f32)


def norm_in(layer, gain_at, shift_at, bias_at, base_ref, sums, small_ref, row):
    branch = summed_row(sums, row) + small_at(small_ref, layer, bias_at)
    hat, rate = standard(base_ref[rows_of(row), :].astype(f32) + branch)
    out = hat * small_at(small_ref, layer, gain_at) + small_at(small_ref, layer, shift_at)
    return out.astype(bf16), hat, rate


def add_kernel(left_ref, right_ref, out_ref):
    out_ref[...] = add_low(left_ref[...], right_ref[...])


def take_kernel(units, place_ref, query_ref, key_ref, *refs):
    outs, (held, sems) = refs[: len(units)], refs[len(units) :]
    section = place_ref[0]
    part = D // SECTIONS
    first = (section * part) // 128 * 128
    at, copies = 0, []
    for out_ref, pieces in zip(outs, units):
        to = 0
        for encoder, layer, kind in pieces:
            mats_ref = query_ref if encoder == "query" else key_ref
            for j in range(4 if kind == "attention" else 2):
                if kind == "attention":
                    source, wide, got = j * D + first, 256, part
                else:
                    source, wide, got = (4 + 4 * j + section) * D, D, D
                source = mats_ref.at[layer, :, pl.ds(pl.multiple_of(source, 128), wide)]
                copy = pltpu.make_async_copy(
                    source, held.at[:, at : at + wide], sems.at[len(copies)]
                )
                copy.start()
                copies.append((copy, at, wide, out_ref, to, got))
                at, to = at + wide, to + got
    for copy, at, wide, out_ref, to, got in copies:
        copy.wait()
        block = held[:, at : at + wide]
        if wide == 256:
            block = jnp.where(section % 2 == 1, pltpu.roll(block, 192, 1), block)
        out_ref[:, to : to + got] = block[:, :got].astype(bf16)


class Columns:
    def __init__(self, ref, at):
        self.ref, self.at = ref, at

    def __getitem__(self, index):
        start, stop = index[1].start or 0, index[1].stop
        return self.ref[:, self.at + start : self.at + stop]


def second_kernel(place_ref, left_ref, right_ref, out_ref):
    right_half = place_ref[1] >= 4
    out_ref[...] = jnp.where(right_half, left_ref[...], right_ref[...])


def place_rows(kind, refs, at, place_ref, whole_ref):
    wide = whole_ref.shape[1]
    rows, count = refs[0].shape[0], len(refs) // 2
    z, core = place_ref[1] // 2, place_ref[1] % 2

    def put(i, source):
        for chunk, its in ((refs[i], core), (refs[count + i], 1 - core)):
            start = pl.multiple_of((source * 2 + its) * rows, 16)
            whole_ref[pl.ds(start, rows), :] = chunk[:, at : at + wide]

    if kind == "circle":
        for i in range(count):
            put(i, lax.rem(z + count - i, count))
        return
    put(0, z)
    put(1, jnp.where(z == 0, 3, z - 1))
    put(2, jnp.where(z == 3, 0, z + 1))
    put(3, jnp.where(z >= 2, z - 2, z + 2))

    @pl.when((z == 0) | (z == 3))
    def _():
        put(4, 3 - z)


def weights_in(kind, refs, at, place_ref, whole_ref):
    if len(refs) == 1:
        return Columns(refs[0], at)
    place_rows(kind, refs, at, place_ref, whole_ref)
    return whole_ref


def attention_kernel(layer, first, keep, kind, count, at, *refs):
    refs = list(refs)
    place_ref, lens_ref, small_ref = refs[:3]
    chunk_refs, refs = refs[3 : 3 + count], refs[3 + count :]
    base_ref, refs = refs[0], refs[1:]
    if not first:
        sums, refs = refs[:4], refs[4:]
    part_refs, outs = refs[:2], refs[2:]
    whole_ref, outs = outs[-1], outs[:-1]
    weights_ref = weights_in(kind, chunk_refs, at, place_ref, whole_ref)
    if not first:
        y_ref, outs = outs[0], outs[1:]
        if keep:
            hat_ref, rate_ref = outs[:2]
            outs = outs[2:]
    if keep:
        q_ref, k_ref, v_ref, mixed_ref, prob_ref = outs
    part = D // SECTIONS
    bv = own_cols(small_at(small_ref, layer, AT_BV), place_ref[0], part)
    lane = lax.broadcasted_iota(jnp.int32, (1, part), 1)
    for row in range(MICRO):
        here = rows_of(row)
        if first:
            inputs = base_ref[here, :]
        else:
            inputs, hat, rate = norm_in(
                layer - 1, AT_G2, AT_S2, AT_B2, base_ref, sums, small_ref, row
            )
            y_ref[here, :] = inputs
            if keep:
                hat_ref[here, :] = hat
                rate_ref[here, :] = jnp.broadcast_to(rate, (ROW, 128))
        project = dot_nn(inputs, weights_ref[:, : 3 * part])
        query = project[:, :part]
        key_rows = project[:, part : 2 * part].astype(bf16)
        values = (project[:, 2 * part :] + bv).astype(bf16)
        allowed = allowed_of(lens_ref, row)
        mixed = jnp.zeros((ROW, part), f32)
        for head in range(part // HEAD_DIM):
            inside = (lane >= head * HEAD_DIM) & (lane < (head + 1) * HEAD_DIM)
            head_q = jnp.where(inside, query, 0.0).astype(bf16)
            scores = jnp.where(allowed, dot_nt(head_q, key_rows) * score_scale, -1e30)
            terms = jnp.exp(scores - jnp.max(scores, axis=-1, keepdims=True))
            prob = terms / jnp.sum(terms, axis=-1, keepdims=True)
            if keep:
                prob_ref[row, head] = prob
            mixed = jnp.where(inside, dot_nn(prob.astype(bf16), values), mixed)
        mixed = mixed.astype(bf16)
        part_refs[row][...] = dot_nt(mixed, weights_ref[:, 3 * part : 4 * part]).astype(bf16)
        if keep:
            q_ref[here, :] = query.astype(bf16)
            k_ref[here, :] = key_rows
            v_ref[here, :] = values
            mixed_ref[here, :] = mixed


def feed_kernel(layer, keep, kind, count, at, place_ref, small_ref, base_ref, *refs):
    sums, chunk_refs, refs = refs[:4], refs[4 : 4 + count], refs[4 + count :]
    part_refs, y_ref, whole_ref = refs[:2], refs[2], refs[-1]
    weights_ref = weights_in(kind, chunk_refs, at, place_ref, whole_ref)
    if keep:
        hat_ref, rate_ref, hidden_ref, active_ref = refs[3:7]
    b1 = own_cols(small_at(small_ref, layer, AT_B1, 4 * D), place_ref[0], D)
    for row in range(MICRO):
        here = rows_of(row)
        inputs, hat, rate = norm_in(layer, AT_G1, AT_S1, AT_BO, base_ref, sums, small_ref, row)
        y_ref[here, :] = inputs
        hidden = dot_nn(inputs, weights_ref[:, :D]) + b1
        active = (0.5 * hidden * (1.0 + lax.erf(hidden * (0.5**0.5)))).astype(bf16)
        part_refs[row][...] = dot_nt(active, weights_ref[:, D : 2 * D]).astype(bf16)
        if keep:
            hat_ref[here, :] = hat
            rate_ref[here, :] = jnp.broadcast_to(rate, (ROW, 128))
            hidden_ref[here, :] = hidden
            active_ref[here, :] = active


def last_kernel(layer, place_ref, lens_ref, small_ref, base_ref, *refs):
    sums, pooled_ref = refs[:4], refs[4]
    for row in range(MICRO):
        out, hat, rate = norm_in(layer, AT_G2, AT_S2, AT_B2, base_ref, sums, small_ref, row)
        part = pooled_ref.shape[-1]
        pooled_ref[row] = own_cols(pooled_of(lens_ref, row, out), place_ref[0], part)


def norm_back(grad_out, hat, rate, gain):
    inner = grad_out * gain
    return rate * (
        inner
        - jnp.mean(inner, axis=-1, keepdims=True)
        - hat * jnp.mean(inner * hat, axis=-1, keepdims=True)
    )


def row_sum(block):
    return jnp.sum(block, axis=0, keepdims=True)


def arrived_grad(base_ref, sums, row):
    return (base_ref[rows_of(row), :] + summed_row(sums, row)).astype(bf16)


def feed_back_kernel(layer, last, place_ref, small_ref, weights_ref, hidden_ref, base_ref, *refs):
    sums, refs = refs[:4], refs[4:]
    if last:
        cot_ref, lens_ref = refs[:2]
    else:
        hat_ref, rate_ref = refs[:2]
    part_refs = refs[2:4]
    carry_ref, branch_ref, grad_hidden_ref, sums_ref, bias_ref = refs[4:9]
    if last:
        y_ref, pooled_ref = refs[9:]
    gain = small_at(small_ref, layer, AT_G2)
    totals = [jnp.zeros((1, D), f32) for _ in range(4)]
    for row in range(MICRO):
        here = rows_of(row)
        if last:
            out, hat, rate = norm_in(layer, AT_G2, AT_S2, AT_B2, base_ref, sums, small_ref, row)
            part = y_ref.shape[0]
            y_ref[:, here] = own_cols(out.astype(f32), place_ref[0], part).T.astype(bf16)
            pooled_ref[row] = own_cols(pooled_of(lens_ref, row, out), place_ref[0], part)
            grad_out = cot_ref[here, :].astype(f32)
        else:
            hat, rate = hat_ref[here, :], rate_ref[here, :1]
            grad_out = arrived_grad(base_ref, sums, row).astype(f32)
        grad = norm_back(grad_out, hat, rate, gain)
        carry_ref[here, :] = grad
        branch = grad.astype(bf16)
        branch_ref[here, :] = branch
        grad_active = dot_nn(branch, weights_ref[:, D : 2 * D])
        hidden = hidden_ref[here, :]
        slope = 0.5 * (1.0 + lax.erf(hidden * (0.5**0.5))) + hidden * (
            jnp.exp(-0.5 * hidden * hidden) * 0.3989422804014327
        )
        grad_hidden = (grad_active * slope).astype(bf16)
        grad_hidden_ref[here, :] = grad_hidden
        part_refs[row][...] = dot_nt(grad_hidden, weights_ref[:, :D]).astype(bf16)
        totals[0] += row_sum(branch.astype(f32))
        totals[1] += row_sum(grad_out * hat)
        totals[2] += row_sum(grad_out)
        totals[3] += row_sum(grad_hidden.astype(f32))
    for i in range(3):
        sums_ref[i : i + 1, :] = totals[i]
    bias_ref[...] = totals[3]


def attention_back_kernel(layer, small_ref, place_ref, weights_ref, base_ref, *refs):
    sums, hat_ref, rate_ref = refs[:4], refs[4], refs[5]
    q_ref, k_ref, v_ref, prob_ref = refs[6:10]
    refs = refs[10:]
    part_refs = refs[:2]
    carry_ref, branch_ref, grad_proj_ref, sums_ref, bias_ref = refs[2:]
    part = q_ref.shape[1]
    lane = lax.broadcasted_iota(jnp.int32, (1, part), 1)
    gain = small_at(small_ref, layer, AT_G1)
    totals = [jnp.zeros((1, D), f32) for _ in range(3)] + [jnp.zeros((1, part), f32)]
    for row in range(MICRO):
        here = rows_of(row)
        hat, rate = hat_ref[here, :], rate_ref[here, :1]
        grad_out = arrived_grad(base_ref, sums, row).astype(f32)
        grad = norm_back(grad_out, hat, rate, gain)
        carry_ref[here, :] = grad
        branch = grad.astype(bf16)
        branch_ref[here, :] = branch
        grad_mixed = dot_nn(branch, weights_ref[:, 3 * part : 4 * part])
        low_mixed = grad_mixed.astype(bf16)
        query, key_rows, values = q_ref[here, :], k_ref[here, :], v_ref[here, :]
        grads = [jnp.zeros((ROW, part), f32) for _ in range(3)]
        for head in range(part // HEAD_DIM):
            inside = (lane >= head * HEAD_DIM) & (lane < (head + 1) * HEAD_DIM)
            prob = prob_ref[row, head]
            head_mixed = jnp.where(inside, grad_mixed, 0.0).astype(bf16)
            grad_prob = dot_nt(head_mixed, values)
            grad_scores = prob * (
                grad_prob - jnp.sum(grad_prob * prob, axis=-1, keepdims=True)
            )
            grad_scores = grad_scores.astype(bf16)
            grad_q = dot_nn(grad_scores, key_rows) * score_scale
            grad_k = dot_tn(grad_scores, query) * score_scale
            grad_v = dot_tn(prob.astype(bf16), low_mixed)
            grads = [
                jnp.where(inside, new, old) for new, old in zip((grad_q, grad_k, grad_v), grads)
            ]
        grad_proj = jnp.concatenate(grads, axis=1).astype(bf16)
        grad_proj_ref[here, :] = grad_proj
        parted = dot_nt(grad_proj, weights_ref[:, : 3 * part]).astype(bf16)
        if layer > 0:
            part_refs[row][...] = parted
        else:
            half, upper = D // 2, place_ref[0] >= 2
            part_refs[0][here, :] = jnp.where(upper, parted[:, :half], parted[:, half:])
            part_refs[1][here, :] = jnp.where(upper, parted[:, half:], parted[:, :half])
        totals[0] += row_sum(branch.astype(f32))
        totals[1] += row_sum(grad_out * hat)
        totals[2] += row_sum(grad_out)
        totals[3] += row_sum(grads[2].astype(bf16).astype(f32))
    for i in range(3):
        sums_ref[i : i + 1, :] = totals[i]
    bias_ref[...] = totals[3]


def half_kernel(place_ref, kept_ref, came_ref, sent_out, kept_out):
    total = add_low(kept_ref[...], came_ref[...])
    wide = kept_out.shape[1]
    odd = place_ref[0] % 2 == 1
    kept_out[...] = jnp.where(odd, total[:, wide:], total[:, :wide])
    sent_out[...] = jnp.where(odd, total[:, :wide], total[:, wide:])


def input_kernel(place_ref, base_ref, kept_ref, came_ref, out_ref):
    base = own_cols(base_ref[...], place_ref[0], out_ref.shape[0])
    total = kept_ref[...].astype(f32) + came_ref[...].astype(f32)
    out_ref[...] = (base + total).T.astype(bf16)


def pack_kernel(rows, place_ref, *refs):
    ins, (out_ref, vector_ref, piece_ref) = refs[: 4 * LAYERS], refs[4 * LAYERS :]
    section = place_ref[0]
    own = section == 0
    slot = rows // LAYERS
    share = SMALL // (D // rows)
    out_ref[...] = jnp.zeros(out_ref.shape, bf16)
    piece_ref[...] = jnp.zeros(piece_ref.shape, f32)
    for layer in range(LAYERS):
        norm_1, value_bias, norm_2, hidden_bias = ins[4 * layer : 4 * layer + 4]
        part = value_bias.shape[1]
        for k in range(SECTIONS):
            mine = section == k
            vector_ref[:, k * part : (k + 1) * part] = jnp.where(mine, value_bias[...], 0.0)
            at = AT_B1 + k * D
            vector_ref[:, at : at + D] = jnp.where(mine, hidden_bias[...], 0.0)
        for i in range(3):
            vector_ref[:, AT_BO + i * D : AT_BO + (i + 1) * D] = jnp.where(
                own, norm_1[i : i + 1, :], 0.0
            )
            vector_ref[:, AT_B2 + i * D : AT_B2 + (i + 1) * D] = jnp.where(
                own, norm_2[i : i + 1, :], 0.0
            )
        for i in range(SMALL // 128):
            piece_ref[i : i + 1, :] = vector_ref[:, i * 128 : (i + 1) * 128]
        for b in range(D // rows):
            first = b * share // 128
            last = (b * share + share - 1) // 128 + 1
            start = b * rows + layer * slot
            out_ref[start : start + last - first, :] = piece_ref[first:last, :].astype(bf16)


def grad_kernel(rows, count, place_ref, *refs):
    mine_ref, other_ref, whole_ref = refs[-3:]
    at = 0
    for left_ref, right_ref in zip(refs[: 2 * count : 2], refs[1 : 2 * count : 2]):
        wide = right_ref.shape[1]
        whole_ref[:, at : at + wide] = dot_tn(left_ref[...], right_ref[...]).astype(bf16)
        at += wide
    if at < whole_ref.shape[1]:
        whole_ref[:, at:] = refs[2 * count][...]
    core = place_ref[1] % 2
    for out, owner in ((other_ref, 1 - core), (mine_ref, core)):
        for z in range(mine_ref.shape[0]):
            start = pl.multiple_of((2 * z + owner) * rows, 16)
            out[z] = whole_ref[pl.ds(start, rows), :]


def line_kernel(turn, place_ref, mine_ref, came_ref, *refs):
    places = mine_ref.shape[0]
    z = place_ref[1] // 2

    def rows_for(chip):
        return mine_ref[chip].astype(f32) + came_ref[chip].astype(f32)

    outs = refs if turn == 1 else refs[2:]
    right = rows_for(jnp.minimum(z + places - turn, places - 1))
    left = rows_for(jnp.maximum(z - places + turn, 0))
    if turn > 1:
        right, left = right + refs[0][...].astype(f32), left + refs[1][...].astype(f32)
    outs[0][...], outs[1][...] = right.astype(bf16), left.astype(bf16)
    if turn == places - 1:
        outs[2][...] = rows_for(z).astype(bf16)


def total_kernel(counts, *refs):
    out_ref, at = refs[-1], 0
    for count in counts:
        total = refs[0][...].astype(f32)
        for ref in refs[1:count]:
            total = total + ref[...].astype(f32)
        refs = refs[count:]
        out_ref[:, at : at + total.shape[1]] = total.astype(bf16)
        at += total.shape[1]


def place_kernel(layer, count, attn_at, feed_at, place_ref, *refs):
    blocks, refs = refs[:SECTIONS], refs[SECTIONS:]
    out_ref, buffer, sems = refs[count:]
    section = place_ref[0]
    part = D // SECTIONS

    def owned(group, start, stop):
        found = []
        for slot in range(SECTIONS):
            value = group[0][:, start:stop]
            for k in range(1, SECTIONS):
                value = jnp.where(section ^ slot == k, group[k][:, start:stop], value)
            found.append(value.astype(f32))
        return found

    copies = []

    def push(start, stop):
        there = out_ref.at[layer, :, start:stop]
        copies.append(pltpu.make_async_copy(buffer.at[:, start:stop], there, sems.at[len(copies)]))
        copies[-1].start()

    ffn = owned(blocks, feed_at, feed_at + 2 * D)
    for j in range(2):
        for slot, block in enumerate(ffn):
            start = (4 + 4 * j + slot) * D
            buffer[:, start : start + D] = block[:, j * D : (j + 1) * D]
        push((4 + 4 * j) * D, (8 + 4 * j) * D)
    attn = owned(blocks, attn_at, attn_at + D)
    for j in range(4):
        columns = [a[:, j * part : (j + 1) * part] for a in attn]
        buffer[:, j * D : (j + 1) * D] = jnp.concatenate(columns, axis=1)
    push(0, 4 * D)
    for copy in copies:
        copy.wait()


def small_kernel(place_ref, *refs):
    blocks, (small_ref, vector_ref) = refs[:SECTIONS], refs[SECTIONS:]
    rows, share = blocks[0].shape[0], small_ref.shape[1]
    for layer in range(LAYERS):
        slot = rows // LAYERS
        at, count = layer * slot, min(16, slot)
        total = jnp.zeros((count, 128), f32)
        for block in blocks:
            total = total + block[at : at + count, 3 * D :].astype(f32)
        wide = vector_ref.shape[1]
        for i in range(wide // 128):
            vector_ref[:, i * 128 : (i + 1) * 128] = total[i : i + 1, :]
        inside = lax.rem(place_ref[1] * share, 128)
        moved = pltpu.roll(jnp.broadcast_to(vector_ref[...], (8, wide)), wide - inside, 1)
        small_ref[layer : layer + 1, :] = moved[:1, :share]


def momentum_kernel(layer, query_ref, key_ref, query_small, key_small, *refs):
    out_ref, small_out, q_buf, k_buf, out_buf, in_sems, out_sems = refs[-7:]
    rows = query_ref.shape[1]
    depth, step = q_buf.shape[0], q_buf.shape[1]
    blocks = [(layer, pl.ds(j, step)) for j in range(0, rows, step)]

    def fetch(n):
        i, j = blocks[n]
        pair = [
            pltpu.make_async_copy(ref.at[i, j], buf.at[n % depth], in_sems.at[m, n % depth])
            for m, (ref, buf) in enumerate(((query_ref, q_buf), (key_ref, k_buf)))
        ]
        for copy in pair:
            copy.start()
        return pair

    small_out[...] = (query_small[...] - key_small[...]) * (1.0 - keep_rate)
    coming = [fetch(n) for n in range(min(depth, len(blocks)))]
    leaving = []
    for n, (i, j) in enumerate(blocks):
        for copy in coming[n]:
            copy.wait()
        if n >= depth:
            leaving[n - depth].wait()
        at = n % depth
        out_buf[at] = (q_buf[at] - k_buf[at]) * (1.0 - keep_rate)
        leaving.append(pltpu.make_async_copy(out_buf.at[at], out_ref.at[i, j], out_sems.at[at]))
        leaving[-1].start()
        if n + depth < len(blocks):
            coming.append(fetch(n + depth))
    for copy in leaving[-depth:]:
        copy.wait()


VMEM = pl.BlockSpec(memory_space=pltpu.VMEM)
SMEM = pl.BlockSpec(memory_space=pltpu.SMEM)
ANY = pl.BlockSpec(memory_space=pl.ANY)
SECTIONS = 4


def shaped(shape, kind):
    return jax.ShapeDtypeStruct(shape, kind)


class Raw:
    def __init__(self, value):
        self.value = value


def call(body, name, operands, outs, after=(), scratch=(), limit=12, aliases=None):
    arrays = [a.value if isinstance(a, Raw) else a for a in operands]
    results = [a.value if isinstance(a, Raw) else a for a in outs]
    specs = []
    for given, array in zip(operands, arrays):
        specs.append(ANY if isinstance(given, Raw) else SMEM if array.dtype == jnp.int32 else VMEM)
    count, skipped = len(operands), len(after)

    def kernel(*refs):
        body(*refs[:count], *refs[count + skipped :])

    return pl.pallas_call(
        kernel,
        name=name,
        in_specs=specs + [ANY] * len(after),
        out_specs=[ANY if isinstance(a, Raw) else VMEM for a in outs],
        out_shape=results,
        scratch_shapes=list(scratch),
        input_output_aliases=aliases or {},
        cost_estimate=pl.CostEstimate(flops=1, bytes_accessed=1, transcendentals=0),
        compiler_params=pltpu.CompilerParams(vmem_limit_bytes=limit * 2**20),
    )(*arrays, *after)


part_out = [shaped((ROW, D), bf16)] * 2
rows_out = shaped((TOK, D), bf16)
wide_out = shaped((TOK, D), f32)
rate_out = shaped((TOK, 128), f32)


def add_parts(left, right, after=()):
    return call(add_kernel, "add_parts", [left, right], [shaped(left.shape, bf16)], after)[0]


def momentum(layer, query, key, query_small, key_small, into, after):
    depth, step = 3, 24
    block = (depth, step, query.shape[2])
    return call(
        partial(momentum_kernel, layer),
        f"momentum{layer}",
        [Raw(query), Raw(key), query_small, key_small] + [Raw(a) for a in into],
        [Raw(shaped(query.shape, f32)), shaped(query_small.shape, f32)],
        after,
        [pltpu.VMEM(block, f32)] * 3
        + [pltpu.SemaphoreType.DMA((2, depth)), pltpu.SemaphoreType.DMA((depth,))],
        58,
        {4: 0} if into else {},
    )


def take(place, query_mats, key_mats, units, after=()):
    rows = query_mats.shape[1]
    kinds = [[kind for _, _, kind in pieces] for pieces in units]
    cols = [sum(D if kind == "attention" else 2 * D for kind in found) for found in kinds]
    held = sum(4 * 256 if kind == "attention" else 2 * D for found in kinds for kind in found)
    count = sum(4 if kind == "attention" else 2 for found in kinds for kind in found)
    return call(
        partial(take_kernel, units),
        "take",
        [place, Raw(query_mats), Raw(key_mats)],
        [shaped((rows, c), bf16) for c in cols],
        after,
        [pltpu.VMEM((rows, held), f32), pltpu.SemaphoreType.DMA((count,))],
        limit=58,
    )


def attention(layer, inputs, sums, shared, weights, keep, tag, after=()):
    (chunks, kind), at = weights
    part = D // SECTIONS
    operands = [*shared, *chunks, inputs] + ([] if sums is None else list(sums))
    outs = list(part_out)
    if sums is not None:
        outs += [rows_out] + ([wide_out, rate_out] if keep else [])
    if keep:
        outs += [shaped((TOK, part), bf16)] * 4
        outs += [shaped((MICRO, part // HEAD_DIM, ROW, ROW), f32)]
    shape = (D, 4 * part)
    return call(
        partial(attention_kernel, layer, sums is None, keep, kind, len(chunks), at),
        f"attention_{tag}{layer}",
        operands,
        outs + ([shaped(shape, bf16)] if keep else []),
        after,
        [] if keep else [pltpu.VMEM(shape, bf16)],
    )


def feed(layer, inputs, sums, shared, weights, keep, tag, after=()):
    (chunks, kind), at = weights
    place, lengths, small = shared
    shape = (D, 2 * D)
    outs = [*part_out, rows_out]
    outs += [wide_out, rate_out, wide_out, rows_out, shaped(shape, bf16)] if keep else []
    return call(
        partial(feed_kernel, layer, keep, kind, len(chunks), at),
        f"feed_{tag}{layer}",
        [place, small, inputs, *sums, *chunks],
        outs,
        after,
        [] if keep else [pltpu.VMEM(shape, bf16)],
    )


def grad_over_batch(place, rows, pairs, extra=None, begin=()):
    places = lax.axis_size("batch") // 2
    wide = sum(right.shape[1] for _, right in pairs)
    cols = wide + (0 if extra is None else extra.shape[1])
    chunk = shaped((rows, cols), bf16)
    if places == 4 and rows % 16 == 0:
        mine, other = call(
            partial(grad_kernel, rows, len(pairs)),
            "grad",
            [place, *(x for pair in pairs for x in pair)] + ([] if extra is None else [extra]),
            [shaped((places, rows, cols), bf16)] * 2,
            begin,
            [pltpu.VMEM((D, cols), bf16)],
        )
        came, arrived, shown = swap_core(other), (), []
        for turn in range(1, places):
            sent = call(
                partial(line_kernel, turn),
                "line_sums",
                [place, mine, came, *arrived],
                [chunk] * (3 if turn == places - 1 else 2),
            )
            arrived = (pass_sums(sent[0], 1, turn), pass_sums(sent[1], -1, turn))
            shown.append(arrived)
        return [sent[2], *arrived], (*shown, (sent[0],))
    me = lax.axis_index("batch")
    z, core = me // 2, me % 2
    block = jnp.concatenate([dot_tn(l, r).astype(bf16) for l, r in pairs], axis=1)
    if extra is not None:
        block = jnp.concatenate([block, extra], axis=1)
    parted = block.reshape(places, 2, rows, cols)
    mine = lax.dynamic_index_in_dim(parted, core, 1, keepdims=False)
    other = lax.dynamic_index_in_dim(parted, 1 - core, 1, keepdims=False)
    chip = add_low(mine, swap_core(other))
    chunks = [
        lax.dynamic_index_in_dim(chip, (z + d) % places, 0, keepdims=False) for d in range(places)
    ]
    came = [shift_z(chunks[d], d) for d in range(1, places)]
    return [chunks[0], *came], [()] * 4


def total_of(groups, after=()):
    rows = groups[0][0].shape[0]
    cols = sum(group[0].shape[1] for group in groups)
    return call(
        partial(total_kernel, [len(group) for group in groups]),
        "total",
        [block for group in groups for block in group],
        [shaped((rows, cols), bf16)],
        after,
    )[0]


def on_device(tokens, key_tokens, cotangent, lengths, query_mats, query_small, key_mats, key_small):
    section, batch = lax.axis_index("section"), lax.axis_index("batch")
    part = D // SECTIONS
    rows = query_mats.shape[1]
    place = jnp.stack([section, batch]).astype(jnp.int32)
    shared_q, shared_k = (place, lengths, query_small), (place, lengths, key_small)
    own_turned = shaped((part, TOK), bf16)
    pooled_out = shaped((MICRO, CROPS, part), f32)

    units = [
        [("query", 0, "attention")],
        [("query", 0, "feed")],
        [("query", 1, "attention")],
        [("query", 1, "feed")],
        [("key", 0, "attention"), ("key", 0, "feed")],
        [("key", 1, "attention"), ("key", 1, "feed")],
    ]
    blocks = take(place, query_mats, key_mats, units[:1])
    blocks += take(place, query_mats, key_mats, units[1:], (blocks[0],))
    both = (query_mats, key_mats, query_small, key_small)
    mats_step, early_step = momentum(0, *both, (), (blocks[1],))

    def unit(n, way, *after):
        with jax.named_scope(f"weights_unit_{n}"):
            then = (early_step,) if n == 0 else ()
            return gather_rows(place, put_after(blocks[n], *after), way, then)

    chunks = [unit(0, "once")]
    chunks.append(unit(1, "twice", *landed(chunks[0]), early_step))
    for n in range(2, 4):
        chunks.append(unit(n, "once" if n == 2 else "twice", *near(chunks[-1])))
    for n in range(4, 6):
        chunks.append(unit(n, "line", *landed(chunks[-1])[-1:]))
    lines = [steps_of(found) for found in chunks[4:]]
    attn_q, feed_q = [(chunks[0], 0), (chunks[2], 0)], [(chunks[1], 0), (chunks[3], 0)]

    kept, weights = [], []
    inputs, sums = tokens, None
    for layer in range(LAYERS):
        found = attention(layer, inputs, sums, shared_q, attn_q[layer], True, "q")
        parts, found, attn_w = found[:2], found[2:-1], found[-1]
        if layer > 0:
            inputs, hat, rate = found[:3]
            kept[-1] += (hat, rate)
            found = found[3:]
        sums, _ = sum_parts(f"q{2 * layer}", *parts)
        attn_in, attn_kept = inputs, tuple(found)
        p0, p1, inputs, hat, rate, hidden, active, feed_w = feed(
            layer, inputs, sums, shared_q, feed_q[layer], True, "q"
        )
        gates = ((), lines[0][0]) if layer > 0 else ()
        sums, _ = sum_parts(f"q{2 * layer + 1}", p0, p1, *gates)
        if chunks[0][1] == "whole":
            attn_w, feed_w = attn_q[layer][0][0][0], feed_q[layer][0][0][0]
        weights.append((attn_w, feed_w))
        kept.append((attn_in, attn_kept, hat, rate, inputs, hidden, active))

    attn_k, feed_k = [(chunks[4], 0), (chunks[5], 0)], [(chunks[4], D), (chunks[5], D)]

    def key_attention(layer, inputs, sums, after):
        return attention(layer, inputs, sums, shared_k, attn_k[layer], False, "k", after)

    def key_feed(layer, inputs, sums, after):
        return feed(layer, inputs, sums, shared_k, feed_k[layer], False, "k", after)

    def key_steps():
        after = yield
        sums, after = yield from sum_in_steps("k0", *key_attention(0, key_tokens, None, after))
        found.append(sums)
        yield ()

    found, steps = [], key_steps()
    next(steps)
    small_parts = [None] * LAYERS
    sums_out, turn, done = shaped((3, D), f32), [()] * 4, ()
    for layer in reversed(range(LAYERS)):
        attn_in, attn_kept, hat1, rate1, feed_in, hidden, active, *rest = kept[layer]
        attn_w, feed_w = weights[layer]
        last = layer == LAYERS - 1
        operands = [feed_in, *sums, cotangent, lengths] if last else [carry, *sums, *rest]
        outs = [*part_out, wide_out, rows_out, rows_out, sums_out, shaped((1, D), f32)]
        if last:
            outs += [own_turned, pooled_out]
        p0, p1, carry, branch, grad_hidden, sums_2, db1, *tail = call(
            partial(feed_back_kernel, layer, last),
            f"feed_back{layer}",
            [place, query_small, feed_w, hidden, *operands],
            outs,
            done,
        )
        if last:
            out_q, pooled_q = tail
        gates = (lines[0][1], lines[0][2]) if last else (lines[1][2], turn[0])
        sums, done = sum_parts(f"back{2 * layer + 1}", p0, p1, *gates, steps.send)
        feed_pairs = [(feed_in, grad_hidden), (branch, active)]
        q, k, v, mixed, prob = attn_kept
        p0, p1, carry, branch, grad_proj, sums_1, dbv = call(
            partial(attention_back_kernel, layer),
            f"attention_back{layer}",
            [query_small, place, attn_w, carry, *sums, hat1, rate1, q, k, v, prob],
            [
                *(part_out if last else [shaped((TOK, D // 2), bf16)] * 2),
                wide_out,
                rows_out,
                shaped((TOK, 3 * part), bf16),
                sums_out,
                shaped((1, part), f32),
            ],
            (*done, *turn[1]),
        )
        small_parts[layer] = [sums_1, dbv, sums_2, db1]
        attn_pairs = [(attn_in, grad_proj), (branch, mixed)]
        if last:
            sums, done = sum_parts(f"back{2 * layer}", p0, p1, *lines[1][:2], steps.send)
            with jax.named_scope("grad_layer1"):
                layer_sums, turn = grad_over_batch(
                    place, rows, attn_pairs + feed_pairs, None, sums[::2]
                )
        else:
            sums = sum_own_cols("back0", place, p0, p1)
    (extra,) = call(
        partial(pack_kernel, rows),
        "pack_small",
        [place, *small_parts[0], *small_parts[1]],
        [shaped((D, 128), bf16)],
        scratch=[pltpu.VMEM((1, SMALL), f32), pltpu.VMEM((72, 128), f32)],
    )
    with jax.named_scope("grad_layer0"):
        sums_0, turn_0 = grad_over_batch(place, rows, feed_pairs + attn_pairs, extra)
    with jax.named_scope("place_layer1"):
        got_1 = gather_section(total_of([layer_sums]))

    k0, k1, inputs_k = key_feed(0, key_tokens, found[0], (p0,))
    mats_step, small_step = momentum(1, *both, (mats_step,), (p0,))
    sums_k, _ = sum_parts("k1", k0, k1, (), (*turn[2], *turn_0[3]))
    k0, k1, inputs_k = key_attention(1, inputs_k, sums_k, (*turn_0[0], got_1[1], sums[0]))
    sums_k, _ = sum_parts("k2", k0, k1, (), (*turn_0[1], got_1[2]))
    (input_grad,) = call(input_kernel, "input_grad", [place, carry, *sums], [own_turned])
    k0, k1, inputs_k = key_feed(1, inputs_k, sums_k, (*turn_0[2], got_1[3], input_grad))
    with jax.named_scope("place_layer0"):
        got_0 = gather_section(total_of([sums_0]))
    sums_k, _ = sum_parts("k3", k0, k1, (), (small_step,))
    (pooled_k,) = call(
        partial(last_kernel, LAYERS - 1),
        "last_k",
        [place, lengths, key_small, inputs_k, *sums_k],
        [pooled_out],
    )
    share = SMALL // lax.axis_size("batch")
    mats_shape = (LAYERS, rows, 12 * D)
    touched = -(-(share + 127) // 128) * 128

    grad_mats = ()
    for layer, blocks in ((1, got_1), (0, got_0)):
        attn_at, feed_at = (0, D) if layer > 0 else (2 * D, 0)
        grad_mats = call(
            partial(place_kernel, layer, len(grad_mats), attn_at, feed_at),
            f"place_grads{layer}",
            [place, *blocks, *map(Raw, grad_mats)],
            [Raw(shaped(mats_shape, f32))],
            scratch=[pltpu.VMEM((rows, 12 * D), f32), pltpu.SemaphoreType.DMA((3,))],
            aliases={1 + len(blocks): 0} if grad_mats else {},
        )
    (grad_mats,) = grad_mats
    (grad_small,) = call(
        small_kernel,
        "own_small",
        [place, *got_0],
        [shaped((LAYERS, share), f32)],
        scratch=[pltpu.VMEM((1, touched), f32)],
    )
    return (
        out_q.T,
        pooled_q,
        pooled_k,
        input_grad.T,
        grad_mats,
        grad_small,
        mats_step,
        small_step,
    )


def solution(mesh):
    in_specs = (
        P("batch", None),
        P("batch", None),
        P("batch", None),
        P("batch", None),
        P(None, "batch", None),
        P(),
        P(None, "batch", None),
        P(),
    )
    out_specs = (
        P("batch", "section"),
        P("batch", None, "section"),
        P("batch", None, "section"),
        P("batch", "section"),
        P(None, "batch", None),
        P(None, "batch"),
        P(None, "batch", None),
        P(),
    )
    return jax.shard_map(
        on_device, mesh=mesh, in_specs=in_specs, out_specs=out_specs, check_vma=False
    )
```

```python
from functools import partial

import jax
import jax.numpy as jnp
from jax import lax
from jax.experimental import pallas as pl
from jax.experimental.pallas import tpu as pltpu
from jax.sharding import PartitionSpec as P

HEADS = 12
HEAD_DIM = 64
D = 768
LAYERS = 2
MICRO = 2
ROW = 256
CROPS = 4
TOK = MICRO * ROW
SMALL = 11 * D

epsilon = 1e-05
keep_rate = 0.9995
score_scale = HEAD_DIM ** (-0.5)
bf16 = jnp.bfloat16
f32 = jnp.float32

AT_BV, AT_BO, AT_G1, AT_S1, AT_B1, AT_B2, AT_G2, AT_S2 = (
    0,
    D,
    2 * D,
    3 * D,
    4 * D,
    8 * D,
    9 * D,
    10 * D,
)


def swap_x(block):
    return lax.ppermute(block, "section", [(0, 1), (1, 0), (2, 3), (3, 2)])


def swap_y(block):
    return lax.ppermute(block, "section", [(0, 2), (2, 0), (1, 3), (3, 1)])


def swap_core(block):
    count = lax.axis_size("batch")
    return lax.ppermute(block, "batch", [(i, i ^ 1) for i in range(count)])


def shift_z(block, distance):
    count = lax.axis_size("batch")
    return lax.ppermute(block, "batch", [(i, (i + 2 * distance) % count) for i in range(count)])


def put_after(value, *others):
    return lax.optimization_barrier((value, *others))[0] if others else value


def sum_parts(name, part_0, part_1, begun=(), later=(), beside=None):
    with jax.named_scope(f"sum_{name}_first"):
        here_0, here_1 = swap_x(part_0), swap_y(put_after(part_1, *begun))
    with jax.named_scope(f"sum_{name}_second"):
        half_0, half_1 = add_parts(part_0, here_0), add_parts(part_1, here_1, later)
        sums = (half_0, swap_y(half_0), half_1, swap_x(half_1))
    return sums, () if beside is None else beside((half_0, half_1))


def sum_in_steps(name, part_0, part_1):
    with jax.named_scope(f"sum_{name}_first"):
        here_0, here_1 = swap_x(part_0), swap_y(part_1)
    after = yield (part_0,)
    with jax.named_scope(f"sum_{name}_second"):
        half_0 = add_parts(part_0, here_0, after)
        half_1 = add_parts(part_1, here_1, after)
        sums = (half_0, swap_y(half_0), half_1, swap_x(half_1))
    after = yield (half_0, half_1)
    return sums, after


def sum_own_cols(name, place, sent, kept):
    wide = kept.shape[1] // 2
    with jax.named_scope(f"sum_{name}"):
        came = swap_y(sent)
        sent, kept = call(
            half_kernel, "own_half", [place, kept, came], [shaped((TOK, wide), bf16)] * 2
        )
        return kept, swap_x(sent)


def pass_z(block, step, first=0):
    count = lax.axis_size("batch")
    last = count // 2 - 1
    sources = range(first, last) if step > 0 else range(1, last + 1 - first)
    pairs = [(2 * z + c, 2 * (z + step) + c) for z in sources for c in range(2)]
    return lax.ppermute(block, "batch", pairs)


def pass_sums(block, step, turn):
    count = lax.axis_size("batch")
    last = count // 2 - 1
    sources = range(turn) if step > 0 else range(last + 1 - turn, last + 1)
    pairs = [(2 * z + c, 2 * (z + step) + c) for z in sources for c in range(2)]
    return lax.ppermute(block, "batch", pairs)


def pass_ends(block):
    pairs = [(2 * z + c, 2 * t + c) for z, t in ((2, 3), (1, 0)) for c in range(2)]
    return lax.ppermute(block, "batch", pairs)


def gather_rows(place, block, way, then=()):
    places = lax.axis_size("batch") // 2
    apart = block.shape[0] % 16 == 0
    if places == 4 and apart and way == "line":
        left, right = pass_z(block, 1), pass_z(block, -1)
        left_2, right_2 = pass_z(left, 1, 1), pass_z(right, -1, 1)
        second = call(
            second_kernel, "second", [place, left_2, right_2], [shaped(block.shape, bf16)]
        )[0]
        own, kind = [block, left, right, second, pass_ends(second)], "line"
    else:
        found = {0: block, 1: shift_z(block, 1), places - 1: shift_z(block, places - 1)}
        for d in range(2, places - 1):
            before = (found[d - 1],) if way == "twice" else ()
            found[d] = shift_z(put_after(block, *before), d)
        own, kind = [found[d] for d in range(places)], "circle"
    other = [swap_core(put_after(chunk, *then)) for chunk in own]
    if apart:
        return own + other, kind
    me = lax.axis_index("batch")
    z, core = me // 2, me % 2
    pair = jnp.stack([jnp.stack(own), jnp.stack(other)], 1)
    pair = jnp.where(core == 0, pair, pair[:, ::-1])
    whole = jnp.take(pair, (z - jnp.arange(places)) % places, axis=0)
    return [whole.reshape(places * 2 * block.shape[0], block.shape[1])], "whole"


def near(found):
    chunks, kind = found
    return () if kind == "whole" else (chunks[1], chunks[len(chunks) // 2 - 1])


def landed(found):
    chunks, kind = found
    return () if kind == "whole" else tuple(chunks[1 : len(chunks) // 2])


def steps_of(found):
    chunks, kind = found
    return [(chunks[i],) for i in (1, 3, 4)] if kind == "line" else [(), (), ()]


def gather_section(block):
    over_x = swap_x(block)
    over_y = swap_y(put_after(block, over_x))
    return [block, over_x, over_y, swap_y(put_after(over_x, over_y))]


def dot_nn(left, right):
    return jnp.dot(left, right, preferred_element_type=f32)


def dot_nt(left, right):
    return lax.dot_general(left, right, (((1,), (1,)), ((), ())), preferred_element_type=f32)


def dot_tn(left, right):
    return lax.dot_general(left, right, (((0,), (0,)), ((), ())), preferred_element_type=f32)


def add_low(left, right):
    return (left.astype(f32) + right.astype(f32)).astype(bf16)


def ends_of(lens_ref, row):
    ends, total = [], 0
    for c in range(CROPS):
        total = total + lens_ref[row, c]
        ends.append(total)
    return ends


def segments(ends, shape, dim):
    position = lax.broadcasted_iota(jnp.int32, shape, dim)
    segment = jnp.zeros(shape, jnp.int32)
    for end in ends:
        segment = segment + (position >= end).astype(jnp.int32)
    return position, segment


def allowed_of(lens_ref, row):
    ends = ends_of(lens_ref, row)
    pos_q, seg_q = segments(ends, (ROW, 1), 0)
    pos_k, seg_k = segments(ends, (1, ROW), 1)
    seg_k = jnp.where(pos_k < ends[-1], seg_k, -1)
    return (seg_q == seg_k) | (pos_q == pos_k)


def pooled_of(lens_ref, row, values):
    ends = ends_of(lens_ref, row)
    pos, seg = segments(ends, (1, ROW), 1)
    crop = lax.broadcasted_iota(jnp.int32, (8, 1), 0)
    seg = jnp.where(pos < ends[-1], seg, -1)
    member = (seg == crop).astype(f32).astype(bf16)
    counts = jnp.ones((8, 1), f32)
    for c in range(CROPS):
        counts = jnp.where(crop == c, jnp.maximum(lens_ref[row, c], 1).astype(f32), counts)
    return (dot_nn(member, values) / counts)[:CROPS]


def standard(summed):
    centre = summed - jnp.mean(summed, axis=-1, keepdims=True)
    spread = jnp.mean(centre * centre, axis=-1, keepdims=True)
    rate = lax.rsqrt(spread + epsilon)
    return centre * rate, rate


def small_at(small_ref, layer, offset, width=D):
    return small_ref[layer : layer + 1, offset : offset + width]


def own_cols(block, section, part):
    value = block[:, :part]
    for k in range(1, block.shape[1] // part):
        value = jnp.where(section == k, block[:, k * part : (k + 1) * part], value)
    return value


def rows_of(row):
    return slice(row * ROW, (row + 1) * ROW)


def summed_row(sums, row):
    return sums[2 * row][...].astype(f32) + sums[2 * row + 1][...].astype(f32)


def norm_in(layer, gain_at, shift_at, bias_at, base_ref, sums, small_ref, row):
    branch = summed_row(sums, row) + small_at(small_ref, layer, bias_at)
    hat, rate = standard(base_ref[rows_of(row), :].astype(f32) + branch)
    out = hat * small_at(small_ref, layer, gain_at) + small_at(small_ref, layer, shift_at)
    return out.astype(bf16), hat, rate


def add_kernel(left_ref, right_ref, out_ref):
    out_ref[...] = add_low(left_ref[...], right_ref[...])


def take_kernel(units, place_ref, query_ref, key_ref, *refs):
    outs, (held, sems) = refs[: len(units)], refs[len(units) :]
    section = place_ref[0]
    part = D // SECTIONS
    first = (section * part) // 128 * 128
    at, copies = 0, []
    for out_ref, pieces in zip(outs, units):
        to = 0
        for encoder, layer, kind in pieces:
            mats_ref = query_ref if encoder == "query" else key_ref
            for j in range(4 if kind == "attention" else 2):
                if kind == "attention":
                    source, wide, got = j * D + first, 256, part
                else:
                    source, wide, got = (4 + 4 * j + section) * D, D, D
                source = mats_ref.at[layer, :, pl.ds(pl.multiple_of(source, 128), wide)]
                copy = pltpu.make_async_copy(
                    source, held.at[:, at : at + wide], sems.at[len(copies)]
                )
                copy.start()
                copies.append((copy, at, wide, out_ref, to, got))
                at, to = at + wide, to + got
    for copy, at, wide, out_ref, to, got in copies:
        copy.wait()
        block = held[:, at : at + wide]
        if wide == 256:
            block = jnp.where(section % 2 == 1, pltpu.roll(block, 192, 1), block)
        out_ref[:, to : to + got] = block[:, :got].astype(bf16)


class Columns:
    def __init__(self, ref, at):
        self.ref, self.at = ref, at

    def __getitem__(self, index):
        start, stop = index[1].start or 0, index[1].stop
        return self.ref[:, self.at + start : self.at + stop]


def second_kernel(place_ref, left_ref, right_ref, out_ref):
    right_half = place_ref[1] >= 4
    out_ref[...] = jnp.where(right_half, left_ref[...], right_ref[...])


def place_rows(kind, refs, at, place_ref, whole_ref):
    wide = whole_ref.shape[1]
    rows, count = refs[0].shape[0], len(refs) // 2
    z, core = place_ref[1] // 2, place_ref[1] % 2

    def put(i, source):
        for chunk, its in ((refs[i], core), (refs[count + i], 1 - core)):
            start = pl.multiple_of((source * 2 + its) * rows, 16)
            whole_ref[pl.ds(start, rows), :] = chunk[:, at : at + wide]

    if kind == "circle":
        for i in range(count):
            put(i, lax.rem(z + count - i, count))
        return
    put(0, z)
    put(1, jnp.where(z == 0, 3, z - 1))
    put(2, jnp.where(z == 3, 0, z + 1))
    put(3, jnp.where(z >= 2, z - 2, z + 2))

    @pl.when((z == 0) | (z == 3))
    def _():
        put(4, 3 - z)


def weights_in(kind, refs, at, place_ref, whole_ref):
    if len(refs) == 1:
        return Columns(refs[0], at)
    place_rows(kind, refs, at, place_ref, whole_ref)
    return whole_ref


def attention_kernel(layer, first, keep, kind, count, at, *refs):
    refs = list(refs)
    place_ref, lens_ref, small_ref = refs[:3]
    chunk_refs, refs = refs[3 : 3 + count], refs[3 + count :]
    base_ref, refs = refs[0], refs[1:]
    if not first:
        sums, refs = refs[:4], refs[4:]
    part_refs, outs = refs[:2], refs[2:]
    whole_ref, outs = outs[-1], outs[:-1]
    weights_ref = weights_in(kind, chunk_refs, at, place_ref, whole_ref)
    if not first:
        y_ref, outs = outs[0], outs[1:]
        if keep:
            hat_ref, rate_ref = outs[:2]
            outs = outs[2:]
    if keep:
        q_ref, k_ref, v_ref, mixed_ref, prob_ref = outs
    part = D // SECTIONS
    bv = own_cols(small_at(small_ref, layer, AT_BV), place_ref[0], part)
    lane = lax.broadcasted_iota(jnp.int32, (1, part), 1)
    for row in range(MICRO):
        here = rows_of(row)
        if first:
            inputs = base_ref[here, :]
        else:
            inputs, hat, rate = norm_in(
                layer - 1, AT_G2, AT_S2, AT_B2, base_ref, sums, small_ref, row
            )
            y_ref[here, :] = inputs
            if keep:
                hat_ref[here, :] = hat
                rate_ref[here, :] = jnp.broadcast_to(rate, (ROW, 128))
        project = dot_nn(inputs, weights_ref[:, : 3 * part])
        query = project[:, :part]
        key_rows = project[:, part : 2 * part].astype(bf16)
        values = (project[:, 2 * part :] + bv).astype(bf16)
        allowed = allowed_of(lens_ref, row)
        mixed = jnp.zeros((ROW, part), f32)
        for head in range(part // HEAD_DIM):
            inside = (lane >= head * HEAD_DIM) & (lane < (head + 1) * HEAD_DIM)
            head_q = jnp.where(inside, query, 0.0).astype(bf16)
            scores = jnp.where(allowed, dot_nt(head_q, key_rows) * score_scale, -1e30)
            terms = jnp.exp(scores - jnp.max(scores, axis=-1, keepdims=True))
            prob = terms / jnp.sum(terms, axis=-1, keepdims=True)
            if keep:
                prob_ref[row, head] = prob
            mixed = jnp.where(inside, dot_nn(prob.astype(bf16), values), mixed)
        mixed = mixed.astype(bf16)
        part_refs[row][...] = dot_nt(mixed, weights_ref[:, 3 * part : 4 * part]).astype(bf16)
        if keep:
            q_ref[here, :] = query.astype(bf16)
            k_ref[here, :] = key_rows
            v_ref[here, :] = values
            mixed_ref[here, :] = mixed


def feed_kernel(layer, keep, kind, count, at, place_ref, small_ref, base_ref, *refs):
    sums, chunk_refs, refs = refs[:4], refs[4 : 4 + count], refs[4 + count :]
    part_refs, y_ref, whole_ref = refs[:2], refs[2], refs[-1]
    weights_ref = weights_in(kind, chunk_refs, at, place_ref, whole_ref)
    if keep:
        hat_ref, rate_ref, hidden_ref, active_ref = refs[3:7]
    b1 = own_cols(small_at(small_ref, layer, AT_B1, 4 * D), place_ref[0], D)
    for row in range(MICRO):
        here = rows_of(row)
        inputs, hat, rate = norm_in(layer, AT_G1, AT_S1, AT_BO, base_ref, sums, small_ref, row)
        y_ref[here, :] = inputs
        hidden = dot_nn(inputs, weights_ref[:, :D]) + b1
        active = (0.5 * hidden * (1.0 + lax.erf(hidden * (0.5**0.5)))).astype(bf16)
        part_refs[row][...] = dot_nt(active, weights_ref[:, D : 2 * D]).astype(bf16)
        if keep:
            hat_ref[here, :] = hat
            rate_ref[here, :] = jnp.broadcast_to(rate, (ROW, 128))
            hidden_ref[here, :] = hidden
            active_ref[here, :] = active


def last_kernel(layer, place_ref, lens_ref, small_ref, base_ref, *refs):
    sums, pooled_ref = refs[:4], refs[4]
    for row in range(MICRO):
        out, hat, rate = norm_in(layer, AT_G2, AT_S2, AT_B2, base_ref, sums, small_ref, row)
        part = pooled_ref.shape[-1]
        pooled_ref[row] = own_cols(pooled_of(lens_ref, row, out), place_ref[0], part)


def norm_back(grad_out, hat, rate, gain):
    inner = grad_out * gain
    return rate * (
        inner
        - jnp.mean(inner, axis=-1, keepdims=True)
        - hat * jnp.mean(inner * hat, axis=-1, keepdims=True)
    )


def row_sum(block):
    return jnp.sum(block, axis=0, keepdims=True)


def arrived_grad(base_ref, sums, row):
    return (base_ref[rows_of(row), :] + summed_row(sums, row)).astype(bf16)


def feed_back_kernel(layer, last, place_ref, small_ref, weights_ref, hidden_ref, base_ref, *refs):
    sums, refs = refs[:4], refs[4:]
    if last:
        cot_ref, lens_ref = refs[:2]
    else:
        hat_ref, rate_ref = refs[:2]
    part_refs = refs[2:4]
    carry_ref, branch_ref, grad_hidden_ref, sums_ref, bias_ref = refs[4:9]
    if last:
        y_ref, pooled_ref = refs[9:]
    gain = small_at(small_ref, layer, AT_G2)
    totals = [jnp.zeros((1, D), f32) for _ in range(4)]
    for row in range(MICRO):
        here = rows_of(row)
        if last:
            out, hat, rate = norm_in(layer, AT_G2, AT_S2, AT_B2, base_ref, sums, small_ref, row)
            part = y_ref.shape[0]
            y_ref[:, here] = own_cols(out.astype(f32), place_ref[0], part).T.astype(bf16)
            pooled_ref[row] = own_cols(pooled_of(lens_ref, row, out), place_ref[0], part)
            grad_out = cot_ref[here, :].astype(f32)
        else:
            hat, rate = hat_ref[here, :], rate_ref[here, :1]
            grad_out = arrived_grad(base_ref, sums, row).astype(f32)
        grad = norm_back(grad_out, hat, rate, gain)
        carry_ref[here, :] = grad
        branch = grad.astype(bf16)
        branch_ref[here, :] = branch
        grad_active = dot_nn(branch, weights_ref[:, D : 2 * D])
        hidden = hidden_ref[here, :]
        slope = 0.5 * (1.0 + lax.erf(hidden * (0.5**0.5))) + hidden * (
            jnp.exp(-0.5 * hidden * hidden) * 0.3989422804014327
        )
        grad_hidden = (grad_active * slope).astype(bf16)
        grad_hidden_ref[here, :] = grad_hidden
        part_refs[row][...] = dot_nt(grad_hidden, weights_ref[:, :D]).astype(bf16)
        totals[0] += row_sum(branch.astype(f32))
        totals[1] += row_sum(grad_out * hat)
        totals[2] += row_sum(grad_out)
        totals[3] += row_sum(grad_hidden.astype(f32))
    for i in range(3):
        sums_ref[i : i + 1, :] = totals[i]
    bias_ref[...] = totals[3]


def attention_back_kernel(layer, small_ref, place_ref, weights_ref, base_ref, *refs):
    sums, hat_ref, rate_ref = refs[:4], refs[4], refs[5]
    q_ref, k_ref, v_ref, prob_ref = refs[6:10]
    refs = refs[10:]
    part_refs = refs[:2]
    carry_ref, branch_ref, grad_proj_ref, sums_ref, bias_ref = refs[2:]
    part = q_ref.shape[1]
    lane = lax.broadcasted_iota(jnp.int32, (1, part), 1)
    gain = small_at(small_ref, layer, AT_G1)
    totals = [jnp.zeros((1, D), f32) for _ in range(3)] + [jnp.zeros((1, part), f32)]
    for row in range(MICRO):
        here = rows_of(row)
        hat, rate = hat_ref[here, :], rate_ref[here, :1]
        grad_out = arrived_grad(base_ref, sums, row).astype(f32)
        grad = norm_back(grad_out, hat, rate, gain)
        carry_ref[here, :] = grad
        branch = grad.astype(bf16)
        branch_ref[here, :] = branch
        grad_mixed = dot_nn(branch, weights_ref[:, 3 * part : 4 * part])
        low_mixed = grad_mixed.astype(bf16)
        query, key_rows, values = q_ref[here, :], k_ref[here, :], v_ref[here, :]
        grads = [jnp.zeros((ROW, part), f32) for _ in range(3)]
        for head in range(part // HEAD_DIM):
            inside = (lane >= head * HEAD_DIM) & (lane < (head + 1) * HEAD_DIM)
            prob = prob_ref[row, head]
            head_mixed = jnp.where(inside, grad_mixed, 0.0).astype(bf16)
            grad_prob = dot_nt(head_mixed, values)
            grad_scores = prob * (
                grad_prob - jnp.sum(grad_prob * prob, axis=-1, keepdims=True)
            )
            grad_scores = grad_scores.astype(bf16)
            grad_q = dot_nn(grad_scores, key_rows) * score_scale
            grad_k = dot_tn(grad_scores, query) * score_scale
            grad_v = dot_tn(prob.astype(bf16), low_mixed)
            grads = [
                jnp.where(inside, new, old) for new, old in zip((grad_q, grad_k, grad_v), grads)
            ]
        grad_proj = jnp.concatenate(grads, axis=1).astype(bf16)
        grad_proj_ref[here, :] = grad_proj
        parted = dot_nt(grad_proj, weights_ref[:, : 3 * part]).astype(bf16)
        if layer > 0:
            part_refs[row][...] = parted
        else:
            half, upper = D // 2, place_ref[0] >= 2
            part_refs[0][here, :] = jnp.where(upper, parted[:, :half], parted[:, half:])
            part_refs[1][here, :] = jnp.where(upper, parted[:, half:], parted[:, :half])
        totals[0] += row_sum(branch.astype(f32))
        totals[1] += row_sum(grad_out * hat)
        totals[2] += row_sum(grad_out)
        totals[3] += row_sum(grads[2].astype(bf16).astype(f32))
    for i in range(3):
        sums_ref[i : i + 1, :] = totals[i]
    bias_ref[...] = totals[3]


def half_kernel(place_ref, kept_ref, came_ref, sent_out, kept_out):
    total = add_low(kept_ref[...], came_ref[...])
    wide = kept_out.shape[1]
    odd = place_ref[0] % 2 == 1
    kept_out[...] = jnp.where(odd, total[:, wide:], total[:, :wide])
    sent_out[...] = jnp.where(odd, total[:, :wide], total[:, wide:])


def input_kernel(place_ref, base_ref, kept_ref, came_ref, out_ref):
    base = own_cols(base_ref[...], place_ref[0], out_ref.shape[0])
    total = kept_ref[...].astype(f32) + came_ref[...].astype(f32)
    out_ref[...] = (base + total).T.astype(bf16)


def pack_kernel(rows, place_ref, *refs):
    ins, (out_ref, vector_ref, piece_ref) = refs[: 4 * LAYERS], refs[4 * LAYERS :]
    section = place_ref[0]
    own = section == 0
    slot = rows // LAYERS
    share = SMALL // (D // rows)
    out_ref[...] = jnp.zeros(out_ref.shape, bf16)
    piece_ref[...] = jnp.zeros(piece_ref.shape, f32)
    for layer in range(LAYERS):
        norm_1, value_bias, norm_2, hidden_bias = ins[4 * layer : 4 * layer + 4]
        part = value_bias.shape[1]
        for k in range(SECTIONS):
            mine = section == k
            vector_ref[:, k * part : (k + 1) * part] = jnp.where(mine, value_bias[...], 0.0)
            at = AT_B1 + k * D
            vector_ref[:, at : at + D] = jnp.where(mine, hidden_bias[...], 0.0)
        for i in range(3):
            vector_ref[:, AT_BO + i * D : AT_BO + (i + 1) * D] = jnp.where(
                own, norm_1[i : i + 1, :], 0.0
            )
            vector_ref[:, AT_B2 + i * D : AT_B2 + (i + 1) * D] = jnp.where(
                own, norm_2[i : i + 1, :], 0.0
            )
        for i in range(SMALL // 128):
            piece_ref[i : i + 1, :] = vector_ref[:, i * 128 : (i + 1) * 128]
        for b in range(D // rows):
            first = b * share // 128
            last = (b * share + share - 1) // 128 + 1
            start = b * rows + layer * slot
            out_ref[start : start + last - first, :] = piece_ref[first:last, :].astype(bf16)


def grad_kernel(rows, count, place_ref, *refs):
    mine_ref, other_ref, whole_ref = refs[-3:]
    at = 0
    for left_ref, right_ref in zip(refs[: 2 * count : 2], refs[1 : 2 * count : 2]):
        wide = right_ref.shape[1]
        whole_ref[:, at : at + wide] = dot_tn(left_ref[...], right_ref[...]).astype(bf16)
        at += wide
    if at < whole_ref.shape[1]:
        whole_ref[:, at:] = refs[2 * count][...]
    core = place_ref[1] % 2
    for out, owner in ((other_ref, 1 - core), (mine_ref, core)):
        for z in range(mine_ref.shape[0]):
            start = pl.multiple_of((2 * z + owner) * rows, 16)
            out[z] = whole_ref[pl.ds(start, rows), :]


def line_kernel(turn, place_ref, mine_ref, came_ref, *refs):
    places = mine_ref.shape[0]
    z = place_ref[1] // 2

    def rows_for(chip):
        return mine_ref[chip].astype(f32) + came_ref[chip].astype(f32)

    outs = refs if turn == 1 else refs[2:]
    right = rows_for(jnp.minimum(z + places - turn, places - 1))
    left = rows_for(jnp.maximum(z - places + turn, 0))
    if turn > 1:
        right, left = right + refs[0][...].astype(f32), left + refs[1][...].astype(f32)
    outs[0][...], outs[1][...] = right.astype(bf16), left.astype(bf16)
    if turn == places - 1:
        outs[2][...] = rows_for(z).astype(bf16)


def total_kernel(counts, *refs):
    out_ref, at = refs[-1], 0
    for count in counts:
        total = refs[0][...].astype(f32)
        for ref in refs[1:count]:
            total = total + ref[...].astype(f32)
        refs = refs[count:]
        out_ref[:, at : at + total.shape[1]] = total.astype(bf16)
        at += total.shape[1]


def place_kernel(layer, count, attn_at, feed_at, place_ref, *refs):
    blocks, refs = refs[:SECTIONS], refs[SECTIONS:]
    out_ref, buffer, sems = refs[count:]
    section = place_ref[0]
    part = D // SECTIONS

    def owned(group, start, stop):
        found = []
        for slot in range(SECTIONS):
            value = group[0][:, start:stop]
            for k in range(1, SECTIONS):
                value = jnp.where(section ^ slot == k, group[k][:, start:stop], value)
            found.append(value.astype(f32))
        return found

    copies = []

    def push(start, stop):
        there = out_ref.at[layer, :, start:stop]
        copies.append(pltpu.make_async_copy(buffer.at[:, start:stop], there, sems.at[len(copies)]))
        copies[-1].start()

    ffn = owned(blocks, feed_at, feed_at + 2 * D)
    for j in range(2):
        for slot, block in enumerate(ffn):
            start = (4 + 4 * j + slot) * D
            buffer[:, start : start + D] = block[:, j * D : (j + 1) * D]
        push((4 + 4 * j) * D, (8 + 4 * j) * D)
    attn = owned(blocks, attn_at, attn_at + D)
    for j in range(4):
        columns = [a[:, j * part : (j + 1) * part] for a in attn]
        buffer[:, j * D : (j + 1) * D] = jnp.concatenate(columns, axis=1)
    push(0, 4 * D)
    for copy in copies:
        copy.wait()


def small_kernel(place_ref, *refs):
    blocks, (small_ref, vector_ref) = refs[:SECTIONS], refs[SECTIONS:]
    rows, share = blocks[0].shape[0], small_ref.shape[1]
    for layer in range(LAYERS):
        slot = rows // LAYERS
        at, count = layer * slot, min(16, slot)
        total = jnp.zeros((count, 128), f32)
        for block in blocks:
            total = total + block[at : at + count, 3 * D :].astype(f32)
        wide = vector_ref.shape[1]
        for i in range(wide // 128):
            vector_ref[:, i * 128 : (i + 1) * 128] = total[i : i + 1, :]
        inside = lax.rem(place_ref[1] * share, 128)
        moved = pltpu.roll(jnp.broadcast_to(vector_ref[...], (8, wide)), wide - inside, 1)
        small_ref[layer : layer + 1, :] = moved[:1, :share]


def momentum_kernel(layer, query_ref, key_ref, query_small, key_small, *refs):
    out_ref, small_out, q_buf, k_buf, out_buf, in_sems, out_sems = refs[-7:]
    rows = query_ref.shape[1]
    depth, step = q_buf.shape[0], q_buf.shape[1]
    blocks = [(layer, pl.ds(j, step)) for j in range(0, rows, step)]

    def fetch(n):
        i, j = blocks[n]
        pair = [
            pltpu.make_async_copy(ref.at[i, j], buf.at[n % depth], in_sems.at[m, n % depth])
            for m, (ref, buf) in enumerate(((query_ref, q_buf), (key_ref, k_buf)))
        ]
        for copy in pair:
            copy.start()
        return pair

    small_out[...] = (query_small[...] - key_small[...]) * (1.0 - keep_rate)
    coming = [fetch(n) for n in range(min(depth, len(blocks)))]
    leaving = []
    for n, (i, j) in enumerate(blocks):
        for copy in coming[n]:
            copy.wait()
        if n >= depth:
            leaving[n - depth].wait()
        at = n % depth
        out_buf[at] = (q_buf[at] - k_buf[at]) * (1.0 - keep_rate)
        leaving.append(pltpu.make_async_copy(out_buf.at[at], out_ref.at[i, j], out_sems.at[at]))
        leaving[-1].start()
        if n + depth < len(blocks):
            coming.append(fetch(n + depth))
    for copy in leaving[-depth:]:
        copy.wait()


VMEM = pl.BlockSpec(memory_space=pltpu.VMEM)
SMEM = pl.BlockSpec(memory_space=pltpu.SMEM)
ANY = pl.BlockSpec(memory_space=pl.ANY)
SECTIONS = 4


def shaped(shape, kind):
    return jax.ShapeDtypeStruct(shape, kind)


class Raw:
    def __init__(self, value):
        self.value = value


def call(body, name, operands, outs, after=(), scratch=(), limit=12, aliases=None):
    arrays = [a.value if isinstance(a, Raw) else a for a in operands]
    results = [a.value if isinstance(a, Raw) else a for a in outs]
    specs = []
    for given, array in zip(operands, arrays):
        specs.append(ANY if isinstance(given, Raw) else SMEM if array.dtype == jnp.int32 else VMEM)
    count, skipped = len(operands), len(after)

    def kernel(*refs):
        body(*refs[:count], *refs[count + skipped :])

    return pl.pallas_call(
        kernel,
        name=name,
        in_specs=specs + [ANY] * len(after),
        out_specs=[ANY if isinstance(a, Raw) else VMEM for a in outs],
        out_shape=results,
        scratch_shapes=list(scratch),
        input_output_aliases=aliases or {},
        cost_estimate=pl.CostEstimate(flops=1, bytes_accessed=1, transcendentals=0),
        compiler_params=pltpu.CompilerParams(vmem_limit_bytes=limit * 2**20),
    )(*arrays, *after)


part_out = [shaped((ROW, D), bf16)] * 2
rows_out = shaped((TOK, D), bf16)
wide_out = shaped((TOK, D), f32)
rate_out = shaped((TOK, 128), f32)


def add_parts(left, right, after=()):
    return call(add_kernel, "add_parts", [left, right], [shaped(left.shape, bf16)], after)[0]


def momentum(layer, query, key, query_small, key_small, into, after):
    depth, step = 3, 24
    block = (depth, step, query.shape[2])
    return call(
        partial(momentum_kernel, layer),
        f"momentum{layer}",
        [Raw(query), Raw(key), query_small, key_small] + [Raw(a) for a in into],
        [Raw(shaped(query.shape, f32)), shaped(query_small.shape, f32)],
        after,
        [pltpu.VMEM(block, f32)] * 3
        + [pltpu.SemaphoreType.DMA((2, depth)), pltpu.SemaphoreType.DMA((depth,))],
        58,
        {4: 0} if into else {},
    )


def take(place, query_mats, key_mats, units, after=()):
    rows = query_mats.shape[1]
    kinds = [[kind for _, _, kind in pieces] for pieces in units]
    cols = [sum(D if kind == "attention" else 2 * D for kind in found) for found in kinds]
    held = sum(4 * 256 if kind == "attention" else 2 * D for found in kinds for kind in found)
    count = sum(4 if kind == "attention" else 2 for found in kinds for kind in found)
    return call(
        partial(take_kernel, units),
        "take",
        [place, Raw(query_mats), Raw(key_mats)],
        [shaped((rows, c), bf16) for c in cols],
        after,
        [pltpu.VMEM((rows, held), f32), pltpu.SemaphoreType.DMA((count,))],
        limit=58,
    )


def attention(layer, inputs, sums, shared, weights, keep, tag, after=()):
    (chunks, kind), at = weights
    part = D // SECTIONS
    operands = [*shared, *chunks, inputs] + ([] if sums is None else list(sums))
    outs = list(part_out)
    if sums is not None:
        outs += [rows_out] + ([wide_out, rate_out] if keep else [])
    if keep:
        outs += [shaped((TOK, part), bf16)] * 4
        outs += [shaped((MICRO, part // HEAD_DIM, ROW, ROW), f32)]
    shape = (D, 4 * part)
    return call(
        partial(attention_kernel, layer, sums is None, keep, kind, len(chunks), at),
        f"attention_{tag}{layer}",
        operands,
        outs + ([shaped(shape, bf16)] if keep else []),
        after,
        [] if keep else [pltpu.VMEM(shape, bf16)],
    )


def feed(layer, inputs, sums, shared, weights, keep, tag, after=()):
    (chunks, kind), at = weights
    place, lengths, small = shared
    shape = (D, 2 * D)
    outs = [*part_out, rows_out]
    outs += [wide_out, rate_out, wide_out, rows_out, shaped(shape, bf16)] if keep else []
    return call(
        partial(feed_kernel, layer, keep, kind, len(chunks), at),
        f"feed_{tag}{layer}",
        [place, small, inputs, *sums, *chunks],
        outs,
        after,
        [] if keep else [pltpu.VMEM(shape, bf16)],
    )


def grad_over_batch(place, rows, pairs, extra=None, begin=()):
    places = lax.axis_size("batch") // 2
    wide = sum(right.shape[1] for _, right in pairs)
    cols = wide + (0 if extra is None else extra.shape[1])
    chunk = shaped((rows, cols), bf16)
    if places == 4 and rows % 16 == 0:
        mine, other = call(
            partial(grad_kernel, rows, len(pairs)),
            "grad",
            [place, *(x for pair in pairs for x in pair)] + ([] if extra is None else [extra]),
            [shaped((places, rows, cols), bf16)] * 2,
            begin,
            [pltpu.VMEM((D, cols), bf16)],
        )
        came, arrived, shown = swap_core(other), (), []
        for turn in range(1, places):
            sent = call(
                partial(line_kernel, turn),
                "line_sums",
                [place, mine, came, *arrived],
                [chunk] * (3 if turn == places - 1 else 2),
            )
            arrived = (pass_sums(sent[0], 1, turn), pass_sums(sent[1], -1, turn))
            shown.append(arrived)
        return [sent[2], *arrived], (*shown, (sent[0],))
    me = lax.axis_index("batch")
    z, core = me // 2, me % 2
    block = jnp.concatenate([dot_tn(l, r).astype(bf16) for l, r in pairs], axis=1)
    if extra is not None:
        block = jnp.concatenate([block, extra], axis=1)
    parted = block.reshape(places, 2, rows, cols)
    mine = lax.dynamic_index_in_dim(parted, core, 1, keepdims=False)
    other = lax.dynamic_index_in_dim(parted, 1 - core, 1, keepdims=False)
    chip = add_low(mine, swap_core(other))
    chunks = [
        lax.dynamic_index_in_dim(chip, (z + d) % places, 0, keepdims=False) for d in range(places)
    ]
    came = [shift_z(chunks[d], d) for d in range(1, places)]
    return [chunks[0], *came], [()] * 4


def total_of(groups, after=()):
    rows = groups[0][0].shape[0]
    cols = sum(group[0].shape[1] for group in groups)
    return call(
        partial(total_kernel, [len(group) for group in groups]),
        "total",
        [block for group in groups for block in group],
        [shaped((rows, cols), bf16)],
        after,
    )[0]


def on_device(tokens, key_tokens, cotangent, lengths, query_mats, query_small, key_mats, key_small):
    section, batch = lax.axis_index("section"), lax.axis_index("batch")
    part = D // SECTIONS
    rows = query_mats.shape[1]
    place = jnp.stack([section, batch]).astype(jnp.int32)
    shared_q, shared_k = (place, lengths, query_small), (place, lengths, key_small)
    own_turned = shaped((part, TOK), bf16)
    pooled_out = shaped((MICRO, CROPS, part), f32)

    units = [
        [("query", 0, "attention")],
        [("query", 0, "feed")],
        [("query", 1, "attention")],
        [("query", 1, "feed")],
        [("key", 0, "attention"), ("key", 0, "feed")],
        [("key", 1, "attention"), ("key", 1, "feed")],
    ]
    blocks = take(place, query_mats, key_mats, units[:1])
    blocks += take(place, query_mats, key_mats, units[1:], (blocks[0],))
    both = (query_mats, key_mats, query_small, key_small)
    mats_step, early_step = momentum(0, *both, (), (blocks[1],))

    def unit(n, way, *after):
        with jax.named_scope(f"weights_unit_{n}"):
            then = (early_step,) if n == 0 else ()
            return gather_rows(place, put_after(blocks[n], *after), way, then)

    chunks = [unit(0, "once")]
    chunks.append(unit(1, "twice", *landed(chunks[0]), early_step))
    for n in range(2, 4):
        chunks.append(unit(n, "once" if n == 2 else "twice", *near(chunks[-1])))
    for n in range(4, 6):
        chunks.append(unit(n, "line", *landed(chunks[-1])[-1:]))
    lines = [steps_of(found) for found in chunks[4:]]
    attn_q, feed_q = [(chunks[0], 0), (chunks[2], 0)], [(chunks[1], 0), (chunks[3], 0)]

    kept, weights = [], []
    inputs, sums = tokens, None
    for layer in range(LAYERS):
        found = attention(layer, inputs, sums, shared_q, attn_q[layer], True, "q")
        parts, found, attn_w = found[:2], found[2:-1], found[-1]
        if layer > 0:
            inputs, hat, rate = found[:3]
            kept[-1] += (hat, rate)
            found = found[3:]
        sums, _ = sum_parts(f"q{2 * layer}", *parts)
        attn_in, attn_kept = inputs, tuple(found)
        p0, p1, inputs, hat, rate, hidden, active, feed_w = feed(
            layer, inputs, sums, shared_q, feed_q[layer], True, "q"
        )
        gates = ((), lines[0][0]) if layer > 0 else ()
        sums, _ = sum_parts(f"q{2 * layer + 1}", p0, p1, *gates)
        if chunks[0][1] == "whole":
            attn_w, feed_w = attn_q[layer][0][0][0], feed_q[layer][0][0][0]
        weights.append((attn_w, feed_w))
        kept.append((attn_in, attn_kept, hat, rate, inputs, hidden, active))

    attn_k, feed_k = [(chunks[4], 0), (chunks[5], 0)], [(chunks[4], D), (chunks[5], D)]

    def key_attention(layer, inputs, sums, after):
        return attention(layer, inputs, sums, shared_k, attn_k[layer], False, "k", after)

    def key_feed(layer, inputs, sums, after):
        return feed(layer, inputs, sums, shared_k, feed_k[layer], False, "k", after)

    def key_steps():
        after = yield
        sums, after = yield from sum_in_steps("k0", *key_attention(0, key_tokens, None, after))
        found.append(sums)
        yield ()

    found, steps = [], key_steps()
    next(steps)
    small_parts = [None] * LAYERS
    sums_out, turn, done = shaped((3, D), f32), [()] * 4, ()
    for layer in reversed(range(LAYERS)):
        attn_in, attn_kept, hat1, rate1, feed_in, hidden, active, *rest = kept[layer]
        attn_w, feed_w = weights[layer]
        last = layer == LAYERS - 1
        operands = [feed_in, *sums, cotangent, lengths] if last else [carry, *sums, *rest]
        outs = [*part_out, wide_out, rows_out, rows_out, sums_out, shaped((1, D), f32)]
        if last:
            outs += [own_turned, pooled_out]
        p0, p1, carry, branch, grad_hidden, sums_2, db1, *tail = call(
            partial(feed_back_kernel, layer, last),
            f"feed_back{layer}",
            [place, query_small, feed_w, hidden, *operands],
            outs,
            done,
        )
        if last:
            out_q, pooled_q = tail
        gates = (lines[0][1], lines[0][2]) if last else ((), turn[0])
        sums, done = sum_parts(f"back{2 * layer + 1}", p0, p1, *gates, steps.send)
        feed_pairs = [(feed_in, grad_hidden), (branch, active)]
        q, k, v, mixed, prob = attn_kept
        p0, p1, carry, branch, grad_proj, sums_1, dbv = call(
            partial(attention_back_kernel, layer),
            f"attention_back{layer}",
            [query_small, place, attn_w, carry, *sums, hat1, rate1, q, k, v, prob],
            [
                *(part_out if last else [shaped((TOK, D // 2), bf16)] * 2),
                wide_out,
                rows_out,
                shaped((TOK, 3 * part), bf16),
                sums_out,
                shaped((1, part), f32),
            ],
            (*done, *turn[1]),
        )
        small_parts[layer] = [sums_1, dbv, sums_2, db1]
        attn_pairs = [(attn_in, grad_proj), (branch, mixed)]
        if last:
            sums, done = sum_parts(f"back{2 * layer}", p0, p1, *lines[1][:2], steps.send)
            with jax.named_scope("grad_layer1"):
                layer_sums, turn = grad_over_batch(
                    place, rows, attn_pairs + feed_pairs, None, sums[::2]
                )
        else:
            sums = sum_own_cols("back0", place, p0, p1)
    (extra,) = call(
        partial(pack_kernel, rows),
        "pack_small",
        [place, *small_parts[0], *small_parts[1]],
        [shaped((D, 128), bf16)],
        scratch=[pltpu.VMEM((1, SMALL), f32), pltpu.VMEM((72, 128), f32)],
    )
    with jax.named_scope("grad_layer0"):
        sums_0, turn_0 = grad_over_batch(place, rows, feed_pairs + attn_pairs, extra)
    with jax.named_scope("place_layer1"):
        got_1 = gather_section(total_of([layer_sums]))

    k0, k1, inputs_k = key_feed(0, key_tokens, found[0], (p0,))
    mats_step, small_step = momentum(1, *both, (mats_step,), (p0,))
    sums_k, _ = sum_parts("k1", k0, k1, (), (*turn[2], *turn_0[3]))
    k0, k1, inputs_k = key_attention(1, inputs_k, sums_k, (*turn_0[0], got_1[1], sums[0]))
    sums_k, _ = sum_parts("k2", k0, k1, (), (*turn_0[1], got_1[2]))
    (input_grad,) = call(input_kernel, "input_grad", [place, carry, *sums], [own_turned])
    k0, k1, inputs_k = key_feed(1, inputs_k, sums_k, (*turn_0[2], got_1[3], input_grad))
    with jax.named_scope("place_layer0"):
        got_0 = gather_section(total_of([sums_0]))
    sums_k, _ = sum_parts("k3", k0, k1, (), (small_step,))
    (pooled_k,) = call(
        partial(last_kernel, LAYERS - 1),
        "last_k",
        [place, lengths, key_small, inputs_k, *sums_k],
        [pooled_out],
    )
    share = SMALL // lax.axis_size("batch")
    mats_shape = (LAYERS, rows, 12 * D)
    touched = -(-(share + 127) // 128) * 128

    grad_mats = ()
    for layer, blocks in ((1, got_1), (0, got_0)):
        attn_at, feed_at = (0, D) if layer > 0 else (2 * D, 0)
        grad_mats = call(
            partial(place_kernel, layer, len(grad_mats), attn_at, feed_at),
            f"place_grads{layer}",
            [place, *blocks, *map(Raw, grad_mats)],
            [Raw(shaped(mats_shape, f32))],
            scratch=[pltpu.VMEM((rows, 12 * D), f32), pltpu.SemaphoreType.DMA((3,))],
            aliases={1 + len(blocks): 0} if grad_mats else {},
        )
    (grad_mats,) = grad_mats
    (grad_small,) = call(
        small_kernel,
        "own_small",
        [place, *got_0],
        [shaped((LAYERS, share), f32)],
        scratch=[pltpu.VMEM((1, touched), f32)],
    )
    return (
        out_q.T,
        pooled_q,
        pooled_k,
        input_grad.T,
        grad_mats,
        grad_small,
        mats_step,
        small_step,
    )


def solution(mesh):
    in_specs = (
        P("batch", None),
        P("batch", None),
        P("batch", None),
        P("batch", None),
        P(None, "batch", None),
        P(),
        P(None, "batch", None),
        P(),
    )
    out_specs = (
        P("batch", "section"),
        P("batch", None, "section"),
        P("batch", None, "section"),
        P("batch", "section"),
        P(None, "batch", None),
        P(None, "batch"),
        P(None, "batch", None),
        P(),
    )
    return jax.shard_map(
        on_device, mesh=mesh, in_specs=in_specs, out_specs=out_specs, check_vma=False
    )
```
